32 devices in a mesh: row: 4 (over y, x), col: 8 (over z, core).
Axes of the slice: x: 2, y: 2, z: 4, core: 2. Of those that a mesh axis runs over, the one named last changes fastest.
Arguments:
- positions: float32 [3, 2048], P(None, ('row', 'col')), may hold values from -1 to 70, as said below
- noise: float32 [8, 3, 2048], P(None, None, ('row', 'col')), may hold values from -6 to 6
Outputs:
- basis: float32 [8, 3, 2048], P(None, None, ('row', 'col'))
- residual: float32 [8, 3, 2048], P(None, None, ('row', 'col'))
- coefficients: float32 [3, 8, 8], replicated
The draws below stay inside these ranges and needn't reach their ends.
Inputs may be any that keep to these rules, and one draw needn't show every extreme that they name: `positions`: bead k lies within 0.77 of each coordinate of its own point of a cubic lattice of spacing 2.2 with 32 by 32 points a layer, distinct beads on distinct points.
All inputs are finite; a program needn't handle non-finite values.
Results may differ from the reference program's by a relative error of at most 0.0003.
Values sent between devices are 32-bit elements; how exact they have to be, the bound alone decides.
No kernel may reach another device: no remote copies, remote signals or barrier semaphores. Data moves between devices by JAX's collectives and lax.ppermute only.
A program may use at most 64 MiB of HBM per device.

```python
import jax
import jax.numpy as jnp
from jax import lax

VECS = 8
BEADS = 2048


def draw_positions(key, part):
    order_key = jax.random.fold_in(key, 11)
    jitter_key = jax.random.fold_in(key, 12)
    sites = jax.random.permutation(order_key, BEADS)
    lattice = jnp.stack([sites % 32, sites // 32 % 32, sites // 1024]).astype(jnp.float32)
    jitter_reach = 0.22
    jitter = jax.random.uniform(jitter_key, (3, BEADS), jnp.float32, -jitter_reach, jitter_reach)
    return 2.2 * (lattice + jitter)


def block_levels(stream_key, dims, cuts, low, top_value):
    factor_of, own = 1.0, jax.random.fold_in(stream_key, 6)
    for axis_at, parts in cuts:
        steps = jnp.exp(jax.random.uniform(jax.random.fold_in(own, axis_at), (parts,), jnp.float32, low / len(cuts), top_value / len(cuts)))
        factor_of = factor_of * jnp.repeat(steps, dims[axis_at] // parts).reshape([-1 if axis == axis_at else 1 for axis in range(len(dims))])
    return factor_of


def gaussian(rng, extent, width, most, pieces=(), kind=jnp.bfloat16):
    values = jax.random.normal(rng, extent, jnp.float32) * width
    if len(pieces) > 0:
        values = block_levels(rng, extent, pieces, -0.22, 0.18) * values
    return jnp.clip(values, min=-most, max=most).astype(kind)


def setup_inputs(seed: int = 0) -> dict:
    seeds = jax.random.split(jax.random.key(seed), 3)
    return {
        "positions": draw_positions(jax.random.fold_in(seeds[2], 71), 0),
        "noise": gaussian(seeds[1], (VECS, 3, BEADS), 1.0, 6.0, ((2, 32),), jnp.float32),
    }


def pair_tensor(target_pos, source_pos):
    displace = target_pos[:, :, None] - source_pos[:, None, :]
    distance_sq = lax.optimization_barrier(jnp.sum(displace * displace, axis=0))
    distance = jnp.sqrt(distance_sq)
    safe_distance = jnp.where(distance > 0, distance, 1.0)
    safe_sq = safe_distance * safe_distance
    far_iso = 0.75 / safe_distance * (1.0 + 2.0 / (3.0 * safe_sq))
    far_dir = 0.75 / safe_distance * (1.0 - 2.0 / safe_sq) / safe_sq
    near_iso = 1.0 - 9.0 * distance / 32.0
    near_dir = 3.0 / (32.0 * safe_distance)
    intersecting = distance < 2.0
    iso_part = jnp.where(intersecting, near_iso, far_iso)
    dir_part = jnp.where(intersecting, near_dir, far_dir)
    identity = jnp.eye(3, dtype=displace.dtype)
    return identity[:, :, None, None] * iso_part + dir_part * displace[:, None] * displace[None, :]

def apply_mobility(positions, vectors):
    total = positions.shape[1]
    blocks = positions.reshape(3, total // 32, 32).transpose(1, 0, 2)

    def one_block(target_pos):
        tensor = pair_tensor(target_pos, positions)
        return jnp.einsum('abts,kbs->kat', tensor, vectors, precision=lax.Precision.HIGHEST)
    images = lax.map(one_block, blocks)
    return images.transpose(1, 2, 0, 3).reshape(vectors.shape[0], 3, total)

def gram(left, right):
    return jnp.einsum('kan,jan->kj', left, right, precision=lax.Precision.HIGHEST) / (3.0 * left.shape[2])

def combine(vectors, matrix):
    return jnp.einsum('kan,kj->jan', vectors, matrix, precision=lax.Precision.HIGHEST)

def orthonormal(block):
    factor = jnp.linalg.cholesky(gram(block, block))
    inverse = jax.scipy.linalg.solve_triangular(factor, jnp.eye(factor.shape[0], dtype=factor.dtype), lower=True)
    return (combine(block, inverse.T), factor)

def reference(positions, noise):
    first, unused_factor = orthonormal(noise)
    image = apply_mobility(positions, first)
    alpha_one = gram(first, image)
    remainder = image - combine(first, alpha_one)
    basis, factor_one = orthonormal(remainder)
    image = apply_mobility(positions, basis) - combine(first, factor_one)
    alpha_two = gram(basis, image)
    residual = image - combine(basis, alpha_two)
    return (basis, residual, jnp.stack([alpha_one, factor_one, alpha_two]))
```

```python
import functools

import jax
import jax.numpy as jnp
from jax import lax
from jax.experimental import pallas as pl
from jax.experimental.pallas import tpu as pltpu
from jax.sharding import PartitionSpec as P

CORES = 2
CHUNK = 2048
F32 = jnp.float32
BF16 = jnp.bfloat16


def pack_kernel(positions, noise, block):
    beads = positions.shape[1]
    vecs = noise.shape[0]
    block[...] = jnp.zeros(block.shape, F32)
    block[:vecs, :beads] = noise[:, 0, :]
    block[:vecs, beads:] = noise[:, 1, :]
    block[vecs:, :beads] = noise[:, 2, :]
    block[vecs : vecs + 3, beads:] = positions[...]


def split_two(value):
    high = value.astype(BF16)
    return high, (value - high.astype(F32)).astype(BF16)


def matmul_nt(left, right, precision=lax.Precision.HIGHEST):
    return lax.dot_general(
        left, right, (((1,), (1,)), ((), ())), precision=precision, preferred_element_type=F32
    )


def matmul(left, right):
    return lax.dot_general(
        left, right, (((1,), (0,)), ((), ())), precision=lax.Precision.HIGHEST, preferred_element_type=F32
    )


def matmul_tn(left, right):
    return lax.dot_general(
        left, right, (((0,), (0,)), ((), ())), precision=lax.Precision.HIGHEST, preferred_element_type=F32
    )


def unpack(sources, rows, beads, wide):
    at = 0
    for ref in sources:
        for index in range(0, ref.shape[0], 2):
            one, two = ref[index], ref[index + 1]
            lanes = pl.ds(at, 2 * beads)
            half = one.shape[0] // 2
            for part in range(2):
                one_part = one[part * half : (part + 1) * half]
                two_part = two[part * half : (part + 1) * half]
                if 2 * part < rows:
                    wide[2 * part * half : (2 * part + 1) * half, lanes] = jnp.concatenate(
                        [one_part[:, :beads], two_part[:, :beads]], axis=1
                    )
                if 2 * part + 1 < rows:
                    wide[(2 * part + 1) * half : (2 * part + 2) * half, lanes] = jnp.concatenate(
                        [one_part[:, beads:], two_part[:, beads:]], axis=1
                    )
            at += 2 * beads


def fill_tensor(targets, wide, pos_row, start, high, low):
    beads = targets.shape[0]
    step = 128
    columns = [jnp.broadcast_to(targets[:, axis : axis + 1], (beads, step)) for axis in range(3)]

    def body(index, carry):
        at = pl.multiple_of(start + index * step, step)
        to = pl.ds(pl.multiple_of(index * step, step), step)
        moved = [columns[axis] - wide[pos_row + axis : pos_row + axis + 1, pl.ds(at, step)] for axis in range(3)]
        square = moved[0] * moved[0] + moved[1] * moved[1] + moved[2] * moved[2]
        inverse = lax.rsqrt(jnp.maximum(square, 1e-12))
        inverse_sq = inverse * inverse
        far_iso = inverse * (0.75 + 0.5 * inverse_sq)
        far_dir = inverse * inverse_sq * (0.75 - 1.5 * inverse_sq)
        near_iso = 1.0 - (9.0 / 32.0) * (square * inverse)
        near_dir = (3.0 / 32.0) * inverse
        near = square < 4.0
        iso = jnp.where(near, near_iso, far_iso)
        along = jnp.where(near, near_dir, far_dir)
        scaled = [along * item for item in moved]
        parts = [
            iso + scaled[0] * moved[0],
            scaled[0] * moved[1],
            scaled[0] * moved[2],
            iso + scaled[1] * moved[1],
            scaled[1] * moved[2],
            iso + scaled[2] * moved[2],
        ]
        for part, value in enumerate(parts):
            upper, lower = split_two(value)
            high[part * beads : (part + 1) * beads, to] = upper
            low[part * beads : (part + 1) * beads, to] = lower
        return carry

    lax.fori_loop(0, high.shape[1] // step, body, 0)


def apply_tensor(wide, start, high, low):
    chunk = high.shape[1]
    vectors = wide[:24, pl.ds(start, chunk)]
    upper, lower = split_two(vectors)
    both = jnp.concatenate([upper, lower], axis=0)
    first = matmul_nt(both, high[...], None)
    second = matmul_nt(upper, low[...], None)
    return first[:24] + first[24:] + second


def assemble(products, beads):
    def part(row, component):
        return products[8 * row : 8 * row + 8, component * beads : (component + 1) * beads]

    x = part(0, 0) + part(1, 1) + part(2, 2)
    y = part(0, 1) + part(1, 3) + part(2, 4)
    z = part(0, 2) + part(1, 4) + part(2, 5)
    return x, y, z


def first_kernel(count, beads, targets, *refs):
    sources, (image, wide, high, low) = refs[:count], refs[count:]
    unpack(sources, 4, beads, wide)
    total = wide.shape[1]
    chunk = high.shape[1]
    products = jnp.zeros((24, 6 * beads), F32)
    for start in range(0, total, chunk):
        fill_tensor(targets, wide, 24, start, high, low)
        products = products + apply_tensor(wide, start, high, low)
    x, y, z = assemble(products, beads)
    image[...] = jnp.zeros(image.shape, F32)
    image[:8, :beads] = x
    image[:8, beads:] = y
    image[8:, :beads] = z


def cholesky(matrix):
    size = matrix.shape[0]
    rows = lax.broadcasted_iota(jnp.int32, (size, size), 0)
    cols = lax.broadcasted_iota(jnp.int32, (size, size), 1)
    upper = matrix
    inverse = (rows == cols).astype(F32)
    scale = jnp.zeros((size, size), F32)
    for step in range(size):
        pivot_row = upper[step : step + 1, :]
        pivot = pivot_row[:, step : step + 1]
        below = rows > step
        column = jnp.broadcast_to(upper[:, step : step + 1] / pivot, (size, size))
        factor = jnp.where(below, column, 0.0)
        upper = upper - factor * pivot_row
        inverse = inverse - factor * inverse[step : step + 1, :]
        scale = jnp.where(rows == step, lax.rsqrt(pivot), scale)
    return jnp.where(rows <= cols, upper * scale, 0.0), inverse * scale


def gram_rows(left, right):
    result = matmul_nt(left[0:8, :], right[0:8, :])
    for part in range(1, 3):
        result = result + matmul_nt(left[8 * part : 8 * part + 8, :], right[8 * part : 8 * part + 8, :])
    return result


def second_kernel(count, beads, targets, own, own_image, *refs):
    sources, images = refs[:count], refs[count : 2 * count]
    basis, image, alpha_one, factor_one, partial, wide, wide_image, high, low = refs[2 * count :]
    unpack(sources, 4, beads, wide)
    unpack(images, 3, beads, wide_image)
    total = wide.shape[1]
    chunk = high.shape[1]
    products = jnp.zeros((24, 6 * beads), F32)
    for start in range(0, total, chunk):
        fill_tensor(targets, wide, 24, start, high, low)
        products = products + apply_tensor(wide_image, start, high, low)
    twice = assemble(products, beads)
    size = 3.0 * total
    start_matrix = gram_rows(wide, wide) / size
    cross = gram_rows(wide, wide_image) / size
    squared = gram_rows(wide_image, wide_image) / size
    _, inverse_zero = cholesky(start_matrix)
    alpha = matmul_nt(matmul(inverse_zero, cross), inverse_zero)
    remainder = matmul_nt(matmul(inverse_zero, squared), inverse_zero) - matmul_tn(alpha, alpha)
    factor_t, inverse_one = cholesky(remainder)
    alpha_one[...] = alpha
    factor_one[...] = factor_t.T
    gram = jnp.zeros((8, 8), F32)
    for part in range(3):
        half, side = part // 2 * 8, part % 2 * beads
        noise = own[half : half + 8, side : side + beads]
        once = own_image[half : half + 8, side : side + beads]
        first = matmul(inverse_zero, noise)
        moved = matmul(inverse_zero, once)
        moved_twice = matmul(inverse_zero, twice[part])
        vector = matmul(inverse_one, moved - matmul_tn(alpha, first))
        shifted = matmul(inverse_one, moved_twice - matmul_tn(alpha, moved)) - matmul(factor_t, first)
        basis[part] = vector
        image[part] = shifted
        gram = gram + matmul_nt(vector, shifted)
    partial[...] = gram


def last_kernel(size, count, basis, image, *refs):
    partials, (vectors, residual, alpha_two) = refs[:count], refs[count:]
    total = jnp.zeros((8, 8), F32)
    for ref in partials:
        for index in range(ref.shape[0]):
            total = total + ref[index]
    alpha = total / size
    alpha_two[...] = alpha
    for part in range(3):
        vectors[:, part, :] = basis[part]
        residual[:, part, :] = image[part] - matmul_tn(alpha, basis[part])


def call(kernel, shapes, scratch=()):
    return pl.pallas_call(
        kernel,
        out_shape=[jax.ShapeDtypeStruct(shape, F32) for shape in shapes],
        scratch_shapes=list(scratch),
        compiler_params=pltpu.CompilerParams(vmem_limit_bytes=48 * 1024 * 1024),
    )


def moved_by(value, axis, shift):
    size = lax.axis_size(axis)
    return lax.ppermute(value, axis, [(index, (index + shift) % size) for index in range(size)])


def gather(block):
    cols, rows = lax.axis_size("col"), lax.axis_size("row")
    layers = [block[None]]
    for shift in range(CORES, cols, CORES):
        layers.append(moved_by(block[None], "col", shift))
    held = jnp.concatenate(layers, axis=0)
    plane = [held]
    for shift in range(1, rows):
        plane.append(moved_by(held, "row", shift))
    held = jnp.concatenate(plane, axis=0)
    core = [(index, index ^ 1) for index in range(cols)]
    return [held, lax.ppermute(held, "col", core)]


def local(positions, noise):
    vecs, _, beads = noise.shape
    devices = lax.axis_size("row") * lax.axis_size("col")
    total = beads * devices
    chunk = min(total, CHUNK)
    targets = positions.T
    (block,) = call(pack_kernel, [(2 * vecs, 2 * beads)])(positions, noise)
    sources = gather(block)
    tensors = [pltpu.VMEM((6 * beads, chunk), BF16), pltpu.VMEM((6 * beads, chunk), BF16)]
    wide = pltpu.VMEM((4 * vecs, total), F32)
    (image,) = call(
        functools.partial(first_kernel, len(sources), beads), [(2 * vecs, 2 * beads)], [wide] + tensors
    )(targets, *sources)
    images = gather(image)
    basis, moved, alpha_one, factor_one, partial = call(
        functools.partial(second_kernel, len(sources), beads),
        [(3, vecs, beads), (3, vecs, beads), (vecs, vecs), (vecs, vecs), (vecs, vecs)],
        [wide, wide] + tensors,
    )(targets, block, image, *sources, *images)
    partials = gather(partial)
    vectors, residual, alpha_two = call(
        functools.partial(last_kernel, 3.0 * total, len(partials)),
        [(vecs, 3, beads), (vecs, 3, beads), (vecs, vecs)],
    )(basis, moved, *partials)
    return (vectors, residual, jnp.stack([alpha_one, factor_one, alpha_two]))


def solution(mesh):
    return jax.shard_map(
        local,
        mesh=mesh,
        in_specs=(P(None, ("row", "col")), P(None, None, ("row", "col"))),
        out_specs=(P(None, None, ("row", "col")), P(None, None, ("row", "col")), P()),
        check_vma=False,
    )
```

```python
import functools

import jax
import jax.numpy as jnp
from jax import lax
from jax.experimental import pallas as pl
from jax.experimental.pallas import tpu as pltpu
from jax.sharding import PartitionSpec as P

CHUNK = 2048
F32 = jnp.float32
BF16 = jnp.bfloat16


def pack_kernel(positions, noise, block):
    beads = positions.shape[1]
    vecs = noise.shape[1]
    block[...] = jnp.zeros(block.shape, F32)
    block[:vecs, :beads] = noise[0]
    block[:vecs, beads:] = noise[1]
    block[vecs:, :beads] = noise[2]
    block[vecs : vecs + 3, beads:] = positions[...]


def split_two(value):
    high = value.astype(BF16)
    return high, (value - high.astype(F32)).astype(BF16)


def matmul_nt(left, right, precision=lax.Precision.HIGHEST):
    return lax.dot_general(
        left, right, (((1,), (1,)), ((), ())), precision=precision, preferred_element_type=F32
    )


def matmul(left, right):
    return lax.dot_general(
        left, right, (((1,), (0,)), ((), ())), precision=lax.Precision.HIGHEST, preferred_element_type=F32
    )


def matmul_tn(left, right):
    return lax.dot_general(
        left, right, (((0,), (0,)), ((), ())), precision=lax.Precision.HIGHEST, preferred_element_type=F32
    )


def unpack(sources, rows, beads, wide):
    at = 0
    for ref in sources:
        for index in range(0, ref.shape[0], 2):
            one, two = ref[index], ref[index + 1]
            lanes = pl.ds(at, 2 * beads)
            half = one.shape[0] // 2
            for part in range(2):
                one_part = one[part * half : (part + 1) * half]
                two_part = two[part * half : (part + 1) * half]
                if 2 * part < rows:
                    wide[2 * part * half : (2 * part + 1) * half, lanes] = jnp.concatenate(
                        [one_part[:, :beads], two_part[:, :beads]], axis=1
                    )
                if 2 * part + 1 < rows:
                    wide[(2 * part + 1) * half : (2 * part + 2) * half, lanes] = jnp.concatenate(
                        [one_part[:, beads:], two_part[:, beads:]], axis=1
                    )
            at += 2 * beads


def fill_tensor(targets, wide, pos_row, start, high, low):
    beads = targets.shape[0]
    step = 128
    columns = [jnp.broadcast_to(targets[:, axis : axis + 1], (beads, step)) for axis in range(3)]

    def body(index, carry):
        at = pl.multiple_of(start + index * step, step)
        to = pl.ds(pl.multiple_of(index * step, step), step)
        moved = [columns[axis] - wide[pos_row + axis : pos_row + axis + 1, pl.ds(at, step)] for axis in range(3)]
        square = moved[0] * moved[0] + moved[1] * moved[1] + moved[2] * moved[2]
        inverse = lax.rsqrt(jnp.maximum(square, 1e-12))
        inverse_sq = inverse * inverse
        far_iso = inverse * (0.75 + 0.5 * inverse_sq)
        far_dir = inverse * inverse_sq * (0.75 - 1.5 * inverse_sq)
        near_iso = 1.0 - (9.0 / 32.0) * (square * inverse)
        near_dir = (3.0 / 32.0) * inverse
        near = square < 4.0
        iso = jnp.where(near, near_iso, far_iso)
        along = jnp.where(near, near_dir, far_dir)
        scaled = [along * item for item in moved]
        parts = [
            iso + scaled[0] * moved[0],
            scaled[0] * moved[1],
            scaled[0] * moved[2],
            iso + scaled[1] * moved[1],
            scaled[1] * moved[2],
            iso + scaled[2] * moved[2],
        ]
        for part, value in enumerate(parts):
            upper, lower = split_two(value)
            high[part * beads : (part + 1) * beads, to] = upper
            low[part * beads : (part + 1) * beads, to] = lower
        return carry

    lax.fori_loop(0, high.shape[1] // step, body, 0)


def apply_tensor(wide, start, high, low):
    chunk = high.shape[1]
    vectors = wide[:24, pl.ds(start, chunk)]
    upper, lower = split_two(vectors)
    both = jnp.concatenate([upper, lower], axis=0)
    first = matmul_nt(both, high[...], None)
    second = matmul_nt(upper, low[...], None)
    return first[:24] + first[24:] + second


def assemble(products, beads):
    def part(row, component):
        return products[8 * row : 8 * row + 8, component * beads : (component + 1) * beads]

    x = part(0, 0) + part(1, 1) + part(2, 2)
    y = part(0, 1) + part(1, 3) + part(2, 4)
    z = part(0, 2) + part(1, 4) + part(2, 5)
    return x, y, z


def first_kernel(count, beads, targets, *refs):
    sources, (image, wide, high, low) = refs[:count], refs[count:]
    unpack(sources, 4, beads, wide)
    total = wide.shape[1]
    chunk = high.shape[1]
    products = jnp.zeros((24, 6 * beads), F32)
    for start in range(0, total, chunk):
        fill_tensor(targets, wide, 24, start, high, low)
        products = products + apply_tensor(wide, start, high, low)
    x, y, z = assemble(products, beads)
    image[...] = jnp.zeros(image.shape, F32)
    image[:8, :beads] = x
    image[:8, beads:] = y
    image[8:, :beads] = z


def cholesky(matrix):
    size = matrix.shape[0]
    rows = lax.broadcasted_iota(jnp.int32, (size, size), 0)
    cols = lax.broadcasted_iota(jnp.int32, (size, size), 1)
    upper = matrix
    inverse = (rows == cols).astype(F32)
    scale = jnp.zeros((size, size), F32)
    for step in range(size):
        pivot_row = upper[step : step + 1, :]
        pivot = pivot_row[:, step : step + 1]
        below = rows > step
        column = jnp.broadcast_to(upper[:, step : step + 1] / pivot, (size, size))
        factor = jnp.where(below, column, 0.0)
        upper = upper - factor * pivot_row
        inverse = inverse - factor * inverse[step : step + 1, :]
        scale = jnp.where(rows == step, lax.rsqrt(pivot), scale)
    return jnp.where(rows <= cols, upper * scale, 0.0), inverse * scale


def gram_rows(left, right):
    result = matmul_nt(left[0:8, :], right[0:8, :])
    for part in range(1, 3):
        result = result + matmul_nt(left[8 * part : 8 * part + 8, :], right[8 * part : 8 * part + 8, :])
    return result


def second_kernel(count, beads, targets, own, own_image, *refs):
    sources, images = refs[:count], refs[count : 2 * count]
    basis, image, coefficients, partial, wide, wide_image, high, low = refs[2 * count :]
    unpack(sources, 4, beads, wide)
    unpack(images, 3, beads, wide_image)
    total = wide.shape[1]
    chunk = high.shape[1]
    products = jnp.zeros((24, 6 * beads), F32)
    for start in range(0, total, chunk):
        fill_tensor(targets, wide, 24, start, high, low)
        products = products + apply_tensor(wide_image, start, high, low)
    twice = assemble(products, beads)
    size = 3.0 * total
    start_matrix = gram_rows(wide, wide) / size
    cross = gram_rows(wide, wide_image) / size
    squared = gram_rows(wide_image, wide_image) / size
    _, inverse_zero = cholesky(start_matrix)
    alpha = matmul_nt(matmul(inverse_zero, cross), inverse_zero)
    remainder = matmul_nt(matmul(inverse_zero, squared), inverse_zero) - matmul_tn(alpha, alpha)
    factor_t, inverse_one = cholesky(remainder)
    coefficients[0] = alpha
    coefficients[1] = factor_t.T
    gram = jnp.zeros((8, 8), F32)
    for part in range(3):
        half, side = part // 2 * 8, part % 2 * beads
        noise = own[half : half + 8, side : side + beads]
        once = own_image[half : half + 8, side : side + beads]
        first = matmul(inverse_zero, noise)
        moved = matmul(inverse_zero, once)
        moved_twice = matmul(inverse_zero, twice[part])
        vector = matmul(inverse_one, moved - matmul_tn(alpha, first))
        shifted = matmul(inverse_one, moved_twice - matmul_tn(alpha, moved)) - matmul(factor_t, first)
        basis[part] = vector
        image[part] = shifted
        gram = gram + matmul_nt(vector, shifted)
    partial[...] = gram


def last_kernel(size, count, basis, image, both, *refs):
    partials, (residual, coefficients) = refs[:count], refs[count:]
    total = jnp.zeros((8, 8), F32)
    for ref in partials:
        for index in range(ref.shape[0]):
            total = total + ref[index]
    alpha = total / size
    coefficients[0:2] = both[...]
    coefficients[2] = alpha
    for part in range(3):
        residual[part] = image[part] - matmul_tn(alpha, basis[part])


def call(kernel, shapes, scratch=()):
    return pl.pallas_call(
        kernel,
        out_shape=[jax.ShapeDtypeStruct(shape, F32) for shape in shapes],
        scratch_shapes=list(scratch),
        compiler_params=pltpu.CompilerParams(vmem_limit_bytes=48 * 1024 * 1024),
    )


def gather(block):
    devices = lax.axis_size("row") * lax.axis_size("col")
    copies = jnp.broadcast_to(block[None], (devices,) + block.shape)
    return [lax.all_to_all(copies, ("row", "col"), 0, 0, tiled=True)]


def local(positions, noise):
    vecs, _, beads = noise.shape
    devices = lax.axis_size("row") * lax.axis_size("col")
    total = beads * devices
    chunk = min(total, CHUNK)
    targets = positions.T
    (block,) = call(pack_kernel, [(2 * vecs, 2 * beads)])(positions, noise.transpose(1, 0, 2))
    sources = gather(block)
    tensors = [pltpu.VMEM((6 * beads, chunk), BF16), pltpu.VMEM((6 * beads, chunk), BF16)]
    wide = pltpu.VMEM((4 * vecs, total), F32)
    (image,) = call(
        functools.partial(first_kernel, len(sources), beads), [(2 * vecs, 2 * beads)], [wide] + tensors
    )(targets, *sources)
    images = gather(image)
    basis, moved, both, partial = call(
        functools.partial(second_kernel, len(sources), beads),
        [(3, vecs, beads), (3, vecs, beads), (2, vecs, vecs), (vecs, vecs)],
        [wide, wide] + tensors,
    )(targets, block, image, *sources, *images)
    partials = gather(partial)
    residual, coefficients = call(
        functools.partial(last_kernel, 3.0 * total, len(partials)),
        [(3, vecs, beads), (3, vecs, vecs)],
    )(basis, moved, both, *partials)
    return (basis.transpose(1, 0, 2), residual.transpose(1, 0, 2), coefficients)


def solution(mesh):
    return jax.shard_map(
        local,
        mesh=mesh,
        in_specs=(P(None, ("row", "col")), P(None, None, ("row", "col"))),
        out_specs=(P(None, None, ("row", "col")), P(None, None, ("row", "col")), P()),
        check_vma=False,
    )
```

```python
import functools

import jax
import jax.numpy as jnp
from jax import lax
from jax.experimental import pallas as pl
from jax.experimental.pallas import tpu as pltpu
from jax.sharding import PartitionSpec as P

CHUNK = 2048
KEPT = 8 * 1024 * 1024
F32 = jnp.float32
BF16 = jnp.bfloat16


def pack_kernel(positions, noise, blocks, held_positions, held_noise, block, sems):
    one = pltpu.make_async_copy(positions, held_positions, sems.at[0])
    two = pltpu.make_async_copy(noise, held_noise, sems.at[1])
    one.start()
    two.start()
    beads = positions.shape[1]
    vecs = noise.shape[1]
    block[...] = jnp.zeros(block.shape, F32)
    one.wait()
    two.wait()
    block[:vecs, :beads] = held_noise[0]
    block[:vecs, beads:] = held_noise[1]
    block[vecs:, :beads] = held_noise[2]
    block[vecs : vecs + 3, beads:] = held_positions[...]
    blocks[...] = jnp.broadcast_to(block[...][None], blocks.shape)


def split_two(value):
    high = value.astype(BF16)
    return high, (value - high.astype(F32)).astype(BF16)


def matmul_nt(left, right, precision=None):
    return lax.dot_general(
        left, right, (((1,), (1,)), ((), ())), precision=precision, preferred_element_type=F32
    )


def small_matmul(left, right):
    total = left[:, 0:1] * right[0:1, :]
    for k in range(1, left.shape[1]):
        total = total + left[:, k : k + 1] * right[k : k + 1, :]
    return total


def unpack(blocks, wide, beads):
    for index in range(0, blocks.shape[0], 2):
        one, two = blocks[index], blocks[index + 1]
        half = one.shape[0] // 2
        lanes = pl.ds(index * beads, 2 * beads)
        for part in range(4):
            rows = slice(part // 2 * half, (part // 2 + 1) * half)
            side = slice(part % 2 * beads, (part % 2 + 1) * beads)
            wide[part * half : (part + 1) * half, lanes] = jnp.concatenate(
                [one[rows, side], two[rows, side]], axis=1
            )


def fill_tensor(own, wide, start, high, low):
    beads = own.shape[1] // 2
    step = 128
    targets = own[8:16, beads:].T
    columns = [jnp.broadcast_to(targets[:, axis : axis + 1], (beads, step)) for axis in range(3)]

    def body(index, carry):
        at = pl.multiple_of(start + index * step, step)
        to = pl.ds(pl.multiple_of(index * step, step), step)
        moved = [columns[axis] - wide[24 + axis : 25 + axis, pl.ds(at, step)] for axis in range(3)]
        square = moved[0] * moved[0] + moved[1] * moved[1] + moved[2] * moved[2]
        inverse = lax.rsqrt(jnp.maximum(square, 1e-12))
        inverse_sq = inverse * inverse
        far_iso = inverse * (0.75 + 0.5 * inverse_sq)
        far_dir = inverse * inverse_sq * (0.75 - 1.5 * inverse_sq)
        near_iso = 1.0 - (9.0 / 32.0) * (square * inverse)
        near_dir = (3.0 / 32.0) * inverse
        near = square < 4.0
        iso = jnp.where(near, near_iso, far_iso)
        along = jnp.where(near, near_dir, far_dir)
        scaled = [along * item for item in moved]
        parts = [
            iso + scaled[0] * moved[0],
            scaled[0] * moved[1],
            scaled[0] * moved[2],
            iso + scaled[1] * moved[1],
            scaled[1] * moved[2],
            iso + scaled[2] * moved[2],
        ]
        for part, value in enumerate(parts):
            upper, lower = split_two(value)
            high[part * beads : (part + 1) * beads, to] = upper
            low[part * beads : (part + 1) * beads, to] = lower
        return carry

    lax.fori_loop(0, high.shape[1] // step, body, 0)


def apply_tensor(wide, start, high, low):
    upper, lower = split_two(wide[:, pl.ds(start, high.shape[1])])
    both = jnp.concatenate([upper, lower], axis=0)
    first = matmul_nt(both, high[...])
    second = matmul_nt(upper, low[...])
    return first[:24] + first[32:56] + second[:24]


def assemble(products, image):
    beads = image.shape[1] // 2

    def part(row, component):
        return products[8 * row : 8 * row + 8, component * beads : (component + 1) * beads]

    image[...] = jnp.zeros(image.shape, F32)
    image[:8, :beads] = part(0, 0) + part(1, 1) + part(2, 2)
    image[:8, beads:] = part(0, 1) + part(1, 3) + part(2, 4)
    image[8:, :beads] = part(0, 2) + part(1, 4) + part(2, 5)


def flat(block):
    return jnp.concatenate([block[:8], block[8:]], axis=1)


def product(own, wide_from, wide, high, low, fill):
    chunk = high.shape[1]
    total = jnp.zeros((24, high.shape[0]), F32)
    for start in range(0, wide.shape[1], chunk):
        if fill:
            fill_tensor(own, wide_from, start, high, low)
        total = total + apply_tensor(wide, start, high, low)
    return total


def first_half_kernel(own_blocks, blocks, products, high, low, wide):
    own = own_blocks[0]
    unpack(blocks, wide, own.shape[1] // 2)
    products[...] = product(own, wide, wide, high, low, True)


def second_half_kernel(own_blocks, blocks, products, images, high, low, wide, image):
    own = own_blocks[0]
    unpack(blocks, wide, own.shape[1] // 2)
    assemble(products[...] + product(own, wide, wide, high, low, True), image)
    images[...] = jnp.broadcast_to(image[...][None], images.shape)


def cholesky(matrix):
    size = matrix.shape[0]
    shape = (size, size)
    rows = lax.broadcasted_iota(jnp.int32, shape, 0)
    cols = lax.broadcasted_iota(jnp.int32, shape, 1)
    entry = {}
    for j in range(size):
        column = jnp.broadcast_to(matrix[:, j : j + 1], shape)
        for i in range(j, size):
            entry[i, j] = jnp.broadcast_to(column[i : i + 1, :], shape)
    factor_t = jnp.zeros(shape, F32)
    inverse = jnp.zeros(shape, F32)
    inverse_rows = []
    for j in range(size):
        scale = lax.rsqrt(entry[j, j])
        lower_row = entry[j, j] * scale
        entry[j, j] = scale
        for i in range(j + 1, size):
            entry[i, j] = entry[i, j] * scale
        for i in range(j + 1, size):
            for k in range(j + 1, i + 1):
                entry[i, k] = entry[i, k] - entry[i, j] * entry[k, j]
        lower_row = jnp.where(cols == j, lower_row, 0.0)
        for i in range(j + 1, size):
            lower_row = jnp.where(cols == i, entry[i, j], lower_row)
        factor_t = jnp.where(rows == j, lower_row, factor_t)
        row = jnp.where(cols == j, 1.0, 0.0)
        for k in range(j):
            row = row - entry[j, k] * inverse_rows[k]
        row = row * scale
        inverse_rows.append(row)
        inverse = jnp.where(rows == j, row, inverse)
    return factor_t, inverse


def start_kernel(size, images, own_blocks, one_blocks, two_blocks, small, own_first, own_moved, one_first, two_first, wide):
    beads = own_blocks.shape[2] // 2
    gram = jnp.zeros((8, 8), F32)
    for blocks, first in ((one_blocks, one_first), (two_blocks, two_first)):
        unpack(blocks, wide, beads)
        first[...] = wide[:24]
        for part in range(3):
            rows = wide[8 * part : 8 * part + 8]
            gram = gram + matmul_nt(rows, rows, lax.Precision.HIGHEST)
    _, inverse = cholesky(gram / size)
    for first in (one_first, two_first):
        for part in range(3):
            rows = slice(8 * part, 8 * part + 8)
            first[rows] = small_matmul(inverse, first[rows])
    own_first[...] = small_matmul(inverse, flat(own_blocks[0]))
    own_moved[...] = small_matmul(inverse, flat(images[0]))
    small[0] = inverse
    small[1] = inverse.T


def inner(first, wide):
    total = jnp.zeros((16, 16), F32)
    for part in range(3):
        rows = slice(8 * part, 8 * part + 8)
        high, low = split_two(jnp.concatenate([first[rows], wide[rows]], axis=0))
        total = total + (matmul_nt(high, high) + (matmul_nt(high, low) + matmul_nt(low, high)))
    return total


def third_half_kernel(fill, own_blocks, blocks, images, first, high, low, products, gram, wide, *more):
    own = own_blocks[0]
    beads = own.shape[1] // 2
    unpack(images, wide, beads)
    if fill:
        unpack(blocks, more[0], beads)
    products[...] = product(own, more[0] if fill else None, wide, high, low, fill)
    gram[...] = inner(first, wide)


def fourth_half_kernel(
    size, fill, own_blocks, blocks, images, first, high, low, products, gram, own_images, own_first, own_moved, small,
    basis, shifted, coefficients, partials, wide, image, *more
):
    own = own_blocks[0]
    beads = own.shape[1] // 2
    unpack(images, wide, beads)
    if fill:
        unpack(blocks, more[0], beads)
    assemble(products[...] + product(own, more[0] if fill else None, wide, high, low, fill), image)
    twice = flat(image[...])
    both = (gram[...] + inner(first, wide)) / size
    cross_t, cross, squared = both[:8, 8:], both[8:, :8], both[8:, 8:]
    factor_t, inverse = cholesky(squared - small_matmul(cross, cross_t))
    start_inverse_t = small[1]
    alpha = small_matmul(cross_t, start_inverse_t)
    factor_one_t = small_matmul(factor_t, start_inverse_t)
    vectors = small_matmul(inverse, flat(own_images[0]) - small_matmul(cross, own_first[...]))
    moved = small_matmul(inverse, twice - small_matmul(cross, own_moved[...]))
    moved = moved - small_matmul(factor_one_t, own_first[...])
    valid = lax.broadcasted_iota(jnp.int32, vectors.shape, 1) < 3 * beads
    vectors = jnp.where(valid, vectors, 0.0)
    moved = jnp.where(valid, moved, 0.0)
    partial = matmul_nt(vectors, moved, lax.Precision.HIGHEST)
    for row in range(8):
        partials[:, :, 8 * row : 8 * row + 8] = jnp.broadcast_to(
            partial[row : row + 1][None], (partials.shape[0], 1, 8)
        )
    for part in range(3):
        basis[part] = vectors[:, part * beads : (part + 1) * beads]
    shifted[...] = moved
    coefficients[0] = alpha
    coefficients[1] = factor_one_t.T


def last_kernel(size, basis, shifted, both, one_partials, two_partials, residual, coefficients, alpha):
    beads = basis.shape[2]
    total = (jnp.sum(one_partials[...], axis=0) + jnp.sum(two_partials[...], axis=0)) / size
    for row in range(8):
        alpha[row : row + 1, :] = total[:, 8 * row : 8 * row + 8]
    alpha_t = alpha[...].T
    coefficients[0:2] = both[...]
    coefficients[2] = alpha[...]
    for part in range(3):
        residual[part] = shifted[:, part * beads : (part + 1) * beads] - small_matmul(alpha_t, basis[part])


def array(*shape, dtype=F32):
    return jax.ShapeDtypeStruct(shape, dtype)


def call(kernel, outs, scratch=(), **options):
    return pl.pallas_call(
        kernel,
        out_shape=outs,
        scratch_shapes=list(scratch),
        compiler_params=pltpu.CompilerParams(vmem_limit_bytes=48 * 1024 * 1024),
        **options,
    )


def gather(copies):
    rows, cols = lax.axis_size("row"), lax.axis_size("col")
    groups = [
        [row * cols + col for row in range(rows) for col in range(core, cols, 2)] for core in range(2)
    ]
    mine = lax.all_to_all(copies, ("row", "col"), 0, 0, axis_index_groups=groups, tiled=True)
    other = lax.ppermute(mine, "col", [(col, col ^ 1) for col in range(cols)])
    return mine, other


def local(positions, noise):
    vecs, _, beads = noise.shape
    chips = lax.axis_size("row") * lax.axis_size("col") // 2
    half = beads * chips
    size = 3.0 * 2.0 * half
    keep = 2 * 2 * 2 * 6 * beads * half <= KEPT
    width = half if keep else min(half, CHUNK)
    blocks = array(chips, 2 * vecs, 2 * beads)
    wide = pltpu.VMEM((4 * vecs, half), F32)
    block = pltpu.VMEM((2 * vecs, 2 * beads), F32)
    products = array(3 * vecs, 6 * beads)
    tensors = [array(6 * beads, width, dtype=BF16)] * 2 if keep else []
    held = [] if keep else [pltpu.VMEM((6 * beads, width), BF16)] * 2
    flat_block = array(vecs, 4 * beads)

    own = call(
        pack_kernel,
        blocks,
        [pltpu.VMEM(positions.shape, F32), pltpu.VMEM((3, vecs, beads), F32), block, pltpu.SemaphoreType.DMA((2,))],
        in_specs=[pl.BlockSpec(memory_space=pltpu.HBM)] * 2,
    )(positions, noise.transpose(1, 0, 2))
    one, two = gather(own)
    one_products, *one_tensor = call(first_half_kernel, [products] + tensors, held + [wide])(own, one)
    own_images, *two_tensor = call(second_half_kernel, [blocks] + tensors, held + [wide, block])(
        own, two, one_products
    )
    one_images, two_images = gather(own_images)
    small, own_first, own_moved, one_first, two_first = call(
        functools.partial(start_kernel, size),
        [array(2, vecs, vecs), flat_block, flat_block, array(3 * vecs, half), array(3 * vecs, half)],
        [wide],
    )(own_images, own, one, two)
    fill = not keep

    one_products, gram = call(
        first_of_two(fill), [products, array(2 * vecs, 2 * vecs)], held + [wide] + [wide] * fill
    )(own, one, one_images, one_first, *one_tensor)
    basis, shifted, both, partials = call(
        second_of_two(size, fill),
        [array(3, vecs, beads), flat_block, array(2, vecs, vecs), array(chips, 1, vecs * vecs)],
        held + [wide, block] + [wide] * fill,
    )(own, two, two_images, two_first, *two_tensor, one_products, gram, own_images, own_first, own_moved, small)
    one_partials, two_partials = gather(partials)
    residual, coefficients = call(
        functools.partial(last_kernel, size),
        [array(3, vecs, beads), array(3, vecs, vecs)],
        [pltpu.VMEM((vecs, vecs), F32)],
    )(basis, shifted, both, one_partials, two_partials)
    return (basis.transpose(1, 0, 2), residual.transpose(1, 0, 2), coefficients)


def first_of_two(fill):
    if not fill:
        return functools.partial(third_half_kernel, False)

    def kernel(own, blocks, images, first, products, gram, high, low, wide, more):
        third_half_kernel(True, own, blocks, images, first, high, low, products, gram, wide, more)

    return kernel


def second_of_two(size, fill):
    if not fill:
        return functools.partial(fourth_half_kernel, size, False)

    def kernel(own, blocks, images, first, products, gram, own_images, own_first, own_moved, small, *rest):
        outs, (high, low, wide, image, more) = rest[:4], rest[4:]
        fourth_half_kernel(
            size, True, own, blocks, images, first, high, low, products, gram, own_images, own_first, own_moved,
            small, *outs, wide, image, more
        )

    return kernel


def solution(mesh):
    return jax.shard_map(
        local,
        mesh=mesh,
        in_specs=(P(None, ("row", "col")), P(None, None, ("row", "col"))),
        out_specs=(P(None, None, ("row", "col")), P(None, None, ("row", "col")), P()),
        check_vma=False,
    )
```

```python
import functools

import jax
import jax.numpy as jnp
from jax import lax
from jax.experimental import pallas as pl
from jax.experimental.pallas import tpu as pltpu
from jax.sharding import PartitionSpec as P

CHUNK = 2048
KEPT = 8 * 1024 * 1024
F32 = jnp.float32
BF16 = jnp.bfloat16


def pack_kernel(positions, noise, blocks, held_positions, held_noise, block, sems):
    one = pltpu.make_async_copy(positions, held_positions, sems.at[0])
    two = pltpu.make_async_copy(noise, held_noise, sems.at[1])
    one.start()
    two.start()
    beads = positions.shape[1]
    vecs = noise.shape[1]
    block[...] = jnp.zeros(block.shape, F32)
    one.wait()
    two.wait()
    block[:vecs, :beads] = held_noise[0]
    block[:vecs, beads:] = held_noise[1]
    block[vecs:, :beads] = held_noise[2]
    block[vecs : vecs + 3, beads:] = held_positions[...]
    blocks[...] = jnp.broadcast_to(block[...][None], blocks.shape)


def split_two(value):
    high = value.astype(BF16)
    return high, (value - high.astype(F32)).astype(BF16)


def matmul_nt(left, right, precision=None):
    return lax.dot_general(
        left, right, (((1,), (1,)), ((), ())), precision=precision, preferred_element_type=F32
    )


def small_matmul(left, right):
    total = left[:, 0:1] * right[0:1, :]
    for k in range(1, left.shape[1]):
        total = total + left[:, k : k + 1] * right[k : k + 1, :]
    return total


def unpack(blocks, wide, beads):
    for index in range(0, blocks.shape[0], 2):
        one, two = blocks[index], blocks[index + 1]
        half = one.shape[0] // 2
        lanes = pl.ds(index * beads, 2 * beads)
        for part in range(4):
            rows = slice(part // 2 * half, (part // 2 + 1) * half)
            side = slice(part % 2 * beads, (part % 2 + 1) * beads)
            wide[part * half : (part + 1) * half, lanes] = jnp.concatenate(
                [one[rows, side], two[rows, side]], axis=1
            )


def fill_tensor(own, wide, start, high, low):
    beads = own.shape[1] // 2
    step = 128
    targets = own[8:16, beads:].T
    columns = [jnp.broadcast_to(targets[:, axis : axis + 1], (beads, step)) for axis in range(3)]

    def body(index, carry):
        at = pl.multiple_of(start + index * step, step)
        to = pl.ds(pl.multiple_of(index * step, step), step)
        moved = [columns[axis] - wide[24 + axis : 25 + axis, pl.ds(at, step)] for axis in range(3)]
        square = moved[0] * moved[0] + moved[1] * moved[1] + moved[2] * moved[2]
        inverse = lax.rsqrt(jnp.maximum(square, 1e-12))
        inverse_sq = inverse * inverse
        far_iso = inverse * (0.75 + 0.5 * inverse_sq)
        far_dir = inverse * inverse_sq * (0.75 - 1.5 * inverse_sq)
        near_iso = 1.0 - (9.0 / 32.0) * (square * inverse)
        near_dir = (3.0 / 32.0) * inverse
        near = square < 4.0
        iso = jnp.where(near, near_iso, far_iso)
        along = jnp.where(near, near_dir, far_dir)
        scaled = [along * item for item in moved]
        parts = [
            iso + scaled[0] * moved[0],
            scaled[0] * moved[1],
            scaled[0] * moved[2],
            iso + scaled[1] * moved[1],
            scaled[1] * moved[2],
            iso + scaled[2] * moved[2],
        ]
        for part, value in enumerate(parts):
            upper, lower = split_two(value)
            high[part * beads : (part + 1) * beads, to] = upper
            low[part * beads : (part + 1) * beads, to] = lower
        return carry

    lax.fori_loop(0, high.shape[1] // step, body, 0)


def apply_tensor(wide, start, high, low):
    upper, lower = split_two(wide[:, pl.ds(start, high.shape[1])])
    both = jnp.concatenate([upper, lower], axis=0)
    first = matmul_nt(both, high[...])
    second = matmul_nt(upper, low[...])
    return first[:24] + first[32:56] + second[:24]


def assemble(products, image):
    beads = image.shape[1] // 2

    def part(row, component):
        return products[8 * row : 8 * row + 8, component * beads : (component + 1) * beads]

    image[...] = jnp.zeros(image.shape, F32)
    image[:8, :beads] = part(0, 0) + part(1, 1) + part(2, 2)
    image[:8, beads:] = part(0, 1) + part(1, 3) + part(2, 4)
    image[8:, :beads] = part(0, 2) + part(1, 4) + part(2, 5)


def flat(block):
    return jnp.concatenate([block[:8], block[8:]], axis=1)


def product(own, wide_from, wide, high, low, fill):
    chunk = high.shape[1]
    total = jnp.zeros((24, high.shape[0]), F32)
    for start in range(0, wide.shape[1], chunk):
        if fill:
            fill_tensor(own, wide_from, start, high, low)
        total = total + apply_tensor(wide, start, high, low)
    return total


def first_half_kernel(own_blocks, blocks, products, high, low, wide):
    own = own_blocks[0]
    unpack(blocks, wide, own.shape[1] // 2)
    products[...] = product(own, wide, wide, high, low, True)


def second_half_kernel(own_blocks, blocks, products, images, high, low, wide, image):
    own = own_blocks[0]
    unpack(blocks, wide, own.shape[1] // 2)
    assemble(products[...] + product(own, wide, wide, high, low, True), image)
    images[...] = jnp.broadcast_to(image[...][None], images.shape)


def cholesky(matrix):
    size = matrix.shape[0]
    shape = (size, size)
    rows = lax.broadcasted_iota(jnp.int32, shape, 0)
    cols = lax.broadcasted_iota(jnp.int32, shape, 1)
    entry = {}
    for j in range(size):
        column = jnp.broadcast_to(matrix[:, j : j + 1], shape)
        for i in range(j, size):
            entry[i, j] = jnp.broadcast_to(column[i : i + 1, :], shape)
    factor_t = jnp.zeros(shape, F32)
    inverse = jnp.zeros(shape, F32)
    inverse_rows = []
    for j in range(size):
        scale = lax.rsqrt(entry[j, j])
        lower_row = entry[j, j] * scale
        entry[j, j] = scale
        for i in range(j + 1, size):
            entry[i, j] = entry[i, j] * scale
        for i in range(j + 1, size):
            for k in range(j + 1, i + 1):
                entry[i, k] = entry[i, k] - entry[i, j] * entry[k, j]
        lower_row = jnp.where(cols == j, lower_row, 0.0)
        for i in range(j + 1, size):
            lower_row = jnp.where(cols == i, entry[i, j], lower_row)
        factor_t = jnp.where(rows == j, lower_row, factor_t)
        row = jnp.where(cols == j, 1.0, 0.0)
        for k in range(j):
            row = row - entry[j, k] * inverse_rows[k]
        row = row * scale
        inverse_rows.append(row)
        inverse = jnp.where(rows == j, row, inverse)
    return factor_t, inverse


def start_kernel(size, images, own_blocks, one_blocks, two_blocks, small, own_first, own_moved, one_first, two_first, wide):
    beads = own_blocks.shape[2] // 2
    gram = jnp.zeros((8, 8), F32)
    for blocks, first in ((one_blocks, one_first), (two_blocks, two_first)):
        unpack(blocks, wide, beads)
        first[...] = wide[:24]
        for part in range(3):
            rows = wide[8 * part : 8 * part + 8]
            gram = gram + matmul_nt(rows, rows, lax.Precision.HIGHEST)
    _, inverse = cholesky(gram / size)
    for first in (one_first, two_first):
        for part in range(3):
            rows = slice(8 * part, 8 * part + 8)
            first[rows] = small_matmul(inverse, first[rows])
    own_first[...] = small_matmul(inverse, flat(own_blocks[0]))
    own_moved[...] = small_matmul(inverse, flat(images[0]))
    small[0] = inverse
    small[1] = inverse.T


def inner(first, wide):
    total = jnp.zeros((16, 16), F32)
    for part in range(3):
        rows = slice(8 * part, 8 * part + 8)
        high, low = split_two(jnp.concatenate([first[rows], wide[rows]], axis=0))
        total = total + (matmul_nt(high, high) + (matmul_nt(high, low) + matmul_nt(low, high)))
    return total


def third_half_kernel(fill, own_blocks, blocks, images, first, high, low, products, gram, wide, *more):
    own = own_blocks[0]
    beads = own.shape[1] // 2
    unpack(images, wide, beads)
    if fill:
        unpack(blocks, more[0], beads)
    products[...] = product(own, more[0] if fill else None, wide, high, low, fill)
    gram[...] = inner(first, wide)


def fourth_half_kernel(
    size, fill, own_blocks, blocks, images, first, high, low, products, gram, own_images, own_first, own_moved, small,
    basis, shifted, coefficients, partials, wide, image, *more
):
    own = own_blocks[0]
    beads = own.shape[1] // 2
    unpack(images, wide, beads)
    if fill:
        unpack(blocks, more[0], beads)
    assemble(products[...] + product(own, more[0] if fill else None, wide, high, low, fill), image)
    twice = flat(image[...])
    both = (gram[...] + inner(first, wide)) / size
    cross_t, cross, squared = both[:8, 8:], both[8:, :8], both[8:, 8:]
    factor_t, inverse = cholesky(squared - small_matmul(cross, cross_t))
    start_inverse_t = small[1]
    alpha = small_matmul(cross_t, start_inverse_t)
    factor_one_t = small_matmul(factor_t, start_inverse_t)
    vectors = small_matmul(inverse, flat(own_images[0]) - small_matmul(cross, own_first[...]))
    moved = small_matmul(inverse, twice - small_matmul(cross, own_moved[...]))
    moved = moved - small_matmul(factor_one_t, own_first[...])
    valid = lax.broadcasted_iota(jnp.int32, vectors.shape, 1) < 3 * beads
    vectors = jnp.where(valid, vectors, 0.0)
    moved = jnp.where(valid, moved, 0.0)
    partial = matmul_nt(vectors, moved, lax.Precision.HIGHEST)
    for row in range(8):
        partials[:, :, 8 * row : 8 * row + 8] = jnp.broadcast_to(
            partial[row : row + 1][None], (partials.shape[0], 1, 8)
        )
    for part in range(3):
        basis[part] = vectors[:, part * beads : (part + 1) * beads]
    shifted[...] = moved
    coefficients[0] = alpha
    coefficients[1] = factor_one_t.T


def last_kernel(size, basis, shifted, both, one_partials, two_partials, residual, coefficients, alpha):
    beads = basis.shape[2]
    total = (jnp.sum(one_partials[...], axis=0) + jnp.sum(two_partials[...], axis=0)) / size
    for row in range(8):
        alpha[row : row + 1, :] = total[:, 8 * row : 8 * row + 8]
    alpha_t = alpha[...].T
    coefficients[0:2] = both[...]
    coefficients[2] = alpha[...]
    for part in range(3):
        residual[part] = shifted[:, part * beads : (part + 1) * beads] - small_matmul(alpha_t, basis[part])


def array(*shape, dtype=F32):
    return jax.ShapeDtypeStruct(shape, dtype)


def call(kernel, outs, scratch=(), **options):
    return pl.pallas_call(
        kernel,
        out_shape=outs,
        scratch_shapes=list(scratch),
        compiler_params=pltpu.CompilerParams(vmem_limit_bytes=48 * 1024 * 1024),
        **options,
    )


def gather(copies):
    rows, cols = lax.axis_size("row"), lax.axis_size("col")
    groups = [list(range(core, cols, 2)) for core in range(2)]
    line = lax.all_to_all(copies, "col", 0, 0, axis_index_groups=groups, tiled=True)
    mine = lax.all_to_all(jnp.broadcast_to(line[None], (rows,) + line.shape), "row", 0, 0, tiled=True)
    mine = mine.reshape((-1,) + copies.shape[1:])
    other = lax.ppermute(mine, "col", [(col, col ^ 1) for col in range(cols)])
    return mine, other


def local(positions, noise):
    vecs, _, beads = noise.shape
    chips = lax.axis_size("row") * lax.axis_size("col") // 2
    half = beads * chips
    size = 3.0 * 2.0 * half
    keep = 2 * 2 * 2 * 6 * beads * half <= KEPT
    width = half if keep else min(half, CHUNK)
    layers = lax.axis_size("col") // 2
    blocks = array(layers, 2 * vecs, 2 * beads)
    wide = pltpu.VMEM((4 * vecs, half), F32)
    block = pltpu.VMEM((2 * vecs, 2 * beads), F32)
    products = array(3 * vecs, 6 * beads)
    tensors = [array(6 * beads, width, dtype=BF16)] * 2 if keep else []
    held = [] if keep else [pltpu.VMEM((6 * beads, width), BF16)] * 2
    flat_block = array(vecs, 4 * beads)

    own = call(
        pack_kernel,
        blocks,
        [pltpu.VMEM(positions.shape, F32), pltpu.VMEM((3, vecs, beads), F32), block, pltpu.SemaphoreType.DMA((2,))],
        in_specs=[pl.BlockSpec(memory_space=pltpu.HBM)] * 2,
    )(positions, noise.transpose(1, 0, 2))
    one, two = gather(own)
    one_products, *one_tensor = call(first_half_kernel, [products] + tensors, held + [wide])(own, one)
    own_images, *two_tensor = call(second_half_kernel, [blocks] + tensors, held + [wide, block])(
        own, two, one_products
    )
    one_images, two_images = gather(own_images)
    small, own_first, own_moved, one_first, two_first = call(
        functools.partial(start_kernel, size),
        [array(2, vecs, vecs), flat_block, flat_block, array(3 * vecs, half), array(3 * vecs, half)],
        [wide],
    )(own_images, own, one, two)
    fill = not keep

    one_products, gram = call(
        first_of_two(fill), [products, array(2 * vecs, 2 * vecs)], held + [wide] + [wide] * fill
    )(own, one, one_images, one_first, *one_tensor)
    basis, shifted, both, partials = call(
        second_of_two(size, fill),
        [array(3, vecs, beads), flat_block, array(2, vecs, vecs), array(layers, 1, vecs * vecs)],
        held + [wide, block] + [wide] * fill,
    )(own, two, two_images, two_first, *two_tensor, one_products, gram, own_images, own_first, own_moved, small)
    one_partials, two_partials = gather(partials)
    residual, coefficients = call(
        functools.partial(last_kernel, size),
        [array(3, vecs, beads), array(3, vecs, vecs)],
        [pltpu.VMEM((vecs, vecs), F32)],
    )(basis, shifted, both, one_partials, two_partials)
    return (basis.transpose(1, 0, 2), residual.transpose(1, 0, 2), coefficients)


def first_of_two(fill):
    if not fill:
        return functools.partial(third_half_kernel, False)

    def kernel(own, blocks, images, first, products, gram, high, low, wide, more):
        third_half_kernel(True, own, blocks, images, first, high, low, products, gram, wide, more)

    return kernel


def second_of_two(size, fill):
    if not fill:
        return functools.partial(fourth_half_kernel, size, False)

    def kernel(own, blocks, images, first, products, gram, own_images, own_first, own_moved, small, *rest):
        outs, (high, low, wide, image, more) = rest[:4], rest[4:]
        fourth_half_kernel(
            size, True, own, blocks, images, first, high, low, products, gram, own_images, own_first, own_moved,
            small, *outs, wide, image, more
        )

    return kernel


def solution(mesh):
    return jax.shard_map(
        local,
        mesh=mesh,
        in_specs=(P(None, ("row", "col")), P(None, None, ("row", "col"))),
        out_specs=(P(None, None, ("row", "col")), P(None, None, ("row", "col")), P()),
        check_vma=False,
    )
```

```python
import functools

import jax
import jax.numpy as jnp
from jax import lax
from jax.experimental import pallas as pl
from jax.experimental.pallas import tpu as pltpu
from jax.sharding import PartitionSpec as P

CHUNK = 2048
KEPT = 8 * 1024 * 1024
F32 = jnp.float32
BF16 = jnp.bfloat16


def pack_kernel(rows, blocks):
    beads = rows.shape[1]
    vecs = blocks.shape[1] // 2
    upper = jnp.concatenate([rows[:vecs], rows[vecs : 2 * vecs]], axis=1)
    lower = jnp.concatenate([rows[2 * vecs : 3 * vecs], rows[3 * vecs :]], axis=1)
    blocks[:, :vecs] = jnp.broadcast_to(upper[None], (blocks.shape[0], vecs, 2 * beads))
    blocks[:, vecs:] = jnp.broadcast_to(lower[None], (blocks.shape[0], vecs, 2 * beads))


def split_two(value):
    high = value.astype(BF16)
    return high, (value - high.astype(F32)).astype(BF16)


def matmul_nt(left, right, precision=None):
    return lax.dot_general(
        left, right, (((1,), (1,)), ((), ())), precision=precision, preferred_element_type=F32
    )


def small_matmul(left, right):
    total = left[:, 0:1] * right[0:1, :]
    for k in range(1, left.shape[1]):
        total = total + left[:, k : k + 1] * right[k : k + 1, :]
    return total


def unpack(blocks, wide, beads):
    for index in range(0, blocks.shape[0], 2):
        one, two = blocks[index], blocks[index + 1]
        half = one.shape[0] // 2
        lanes = pl.ds(index * beads, 2 * beads)
        for part in range(4):
            rows = slice(part // 2 * half, (part // 2 + 1) * half)
            side = slice(part % 2 * beads, (part % 2 + 1) * beads)
            wide[part * half : (part + 1) * half, lanes] = jnp.concatenate(
                [one[rows, side], two[rows, side]], axis=1
            )


def target_columns(own):
    beads = own.shape[1] // 2
    targets = own[8:16, beads:].T
    return [jnp.broadcast_to(targets[:, axis : axis + 1], (beads, 128)) for axis in range(3)]


def fill_tensor(columns, wide, start, high, low, at):
    beads = columns[0].shape[0]
    sources = pl.ds(start, 128)
    to = pl.ds(at, 128)
    moved = [columns[axis] - wide[24 + axis : 25 + axis, sources] for axis in range(3)]
    square = moved[0] * moved[0] + moved[1] * moved[1] + moved[2] * moved[2]
    square = jnp.maximum(square, 1e-12)
    inverse = lax.rsqrt(square)
    inverse_sq = inverse * inverse
    near = square < 4.0
    iso = inverse * jnp.where(near, square * (inverse - 9.0 / 32.0), 0.75 + 0.5 * inverse_sq)
    along = inverse * jnp.where(near, 3.0 / 32.0, inverse_sq * (0.75 - 1.5 * inverse_sq))
    scaled = [along * item for item in moved]
    parts = [
        iso + scaled[0] * moved[0],
        scaled[0] * moved[1],
        scaled[0] * moved[2],
        iso + scaled[1] * moved[1],
        scaled[1] * moved[2],
        iso + scaled[2] * moved[2],
    ]
    for part, value in enumerate(parts):
        upper, lower = split_two(value)
        high[part * beads : (part + 1) * beads, to] = upper
        low[part * beads : (part + 1) * beads, to] = lower


def apply_tensor(both, high, low, at, step):
    lanes = pl.ds(at, step)
    half = both.shape[0] // 2
    first = matmul_nt(both, high[:, lanes])
    return first[:half] + first[half:] + matmul_nt(both[:half], low[:, lanes])


def split_rows(*values):
    highs, lows = zip(*[split_two(value) for value in values])
    return jnp.concatenate(highs + lows, axis=0)


def inner(both):
    half = both.shape[0] // 2
    first = matmul_nt(both, both[:half])
    return first[:half] + first[half:] + matmul_nt(both[:half], both[half:])


def assemble(products, image):
    beads = image.shape[1] // 2

    def part(row, component):
        return products[8 * row : 8 * row + 8, component * beads : (component + 1) * beads]

    image[...] = jnp.zeros(image.shape, F32)
    image[:8, :beads] = part(0, 0) + part(1, 1) + part(2, 2)
    image[:8, beads:] = part(0, 1) + part(1, 3) + part(2, 4)
    image[8:, :beads] = part(0, 2) + part(1, 4) + part(2, 5)


def flat(block):
    return jnp.concatenate([block[:8], block[8:]], axis=1)


def block_sum(matrix, row, column):
    parts = [
        matrix[row + 8 * part : row + 8 * part + 8, column + 8 * part : column + 8 * part + 8]
        for part in range(3)
    ]
    return parts[0] + parts[1] + parts[2]


def filled_product(columns, source, wide, start, width, high, low, with_gram):
    step = 256 if width % 256 == 0 else 128

    def fill(index):
        for part in range(0, step, 128):
            at = pl.multiple_of(index * step + part, 128)
            fill_tensor(columns, source, pl.multiple_of(start + at, 128), high, low, at)

    def add(index, totals):
        at = pl.multiple_of(index * step, step)
        both = split_rows(wide[:, pl.ds(pl.multiple_of(start + at, 128), step)])
        products = totals[0] + apply_tensor(both, high, low, at, step)
        if with_gram:
            return products, totals[1] + inner(both)
        return (products,)

    def body(index, totals):
        totals = add(index - 1, totals)
        fill(index)
        return totals

    totals = (jnp.zeros((32, high.shape[0]), F32),)
    if with_gram:
        totals = totals + (jnp.zeros((32, 32), F32),)
    fill(0)
    count = width // step
    totals = lax.fori_loop(1, count, body, totals)
    return add(count - 1, totals)


def first_product(own, wide, high, low):
    columns = target_columns(own)
    width = high.shape[1]
    totals = None
    for start in range(0, wide.shape[1], width):
        part = filled_product(columns, wide, wide, start, width, high, low, True)
        totals = part if totals is None else tuple(a + b for a, b in zip(totals, part))
    return totals


def first_half_kernel(own_blocks, blocks, products, gram, wide, high, low):
    own = own_blocks[0]
    unpack(blocks, wide, own.shape[1] // 2)
    products[...], gram[...] = first_product(own, wide, high, low)


def second_half_kernel(own_blocks, blocks, products, images, gram, wide, high, low, image):
    own = own_blocks[0]
    unpack(blocks, wide, own.shape[1] // 2)
    more, gram[...] = first_product(own, wide, high, low)
    assemble(products[...] + more, image)
    images[...] = jnp.broadcast_to(image[...][None], images.shape)


def cholesky(matrix):
    size = matrix.shape[0]
    shape = (size, size)
    rows = lax.broadcasted_iota(jnp.int32, shape, 0)
    cols = lax.broadcasted_iota(jnp.int32, shape, 1)
    entry = {}
    for j in range(size):
        column = jnp.broadcast_to(matrix[:, j : j + 1], shape)
        for i in range(j, size):
            entry[i, j] = jnp.broadcast_to(column[i : i + 1, :], shape)
    factor_t = jnp.zeros(shape, F32)
    inverse = jnp.zeros(shape, F32)
    inverse_rows = []
    for j in range(size):
        scale = lax.rsqrt(entry[j, j])
        lower_row = entry[j, j] * scale
        entry[j, j] = scale
        for i in range(j + 1, size):
            entry[i, j] = entry[i, j] * scale
        for i in range(j + 1, size):
            for k in range(j + 1, i + 1):
                entry[i, k] = entry[i, k] - entry[i, j] * entry[k, j]
        lower_row = jnp.where(cols == j, lower_row, 0.0)
        for i in range(j + 1, size):
            lower_row = jnp.where(cols == i, entry[i, j], lower_row)
        factor_t = jnp.where(rows == j, lower_row, factor_t)
        row = jnp.where(cols == j, 1.0, 0.0)
        for k in range(j):
            row = row - entry[j, k] * inverse_rows[k]
        row = row * scale
        inverse_rows.append(row)
        inverse = jnp.where(rows == j, row, inverse)
    return factor_t, inverse


def start_kernel(size, images, own_blocks, one_gram, two_gram, small, own_first, own_moved):
    _, inverse = cholesky(block_sum(one_gram[...] + two_gram[...], 0, 0) / size)
    own_first[...] = small_matmul(inverse, flat(own_blocks[0]))
    own_moved[...] = small_matmul(inverse, flat(images[0]))
    small[0] = inverse
    small[1] = inverse.T


def second_product(fill, own, wide, wide_image, high, low):
    width = high.shape[1]
    both = split_rows(wide_image[...])
    total = jnp.zeros((32, high.shape[0]), F32)
    for start in range(0, wide.shape[1], width):
        if fill:
            columns = target_columns(own)
            total = total + filled_product(columns, wide, wide_image, start, width, high, low, False)[0]
        else:
            total = total + apply_tensor(both, high, low, 0, width)
    return total, inner(split_rows(wide[...], wide_image[...]))


def third_half_kernel(fill, own_blocks, images, wide, high, low, products, gram, wide_image):
    own = own_blocks[0]
    unpack(images, wide_image, own.shape[1] // 2)
    products[...], gram[...] = second_product(fill, own, wide, wide_image, high, low)


def fourth_half_kernel(
    size, fill, own_blocks, images, wide, high, low, products, gram, own_images, own_first, own_moved, small,
    vectors_out, shifted, coefficients, partials, wide_image, image
):
    own = own_blocks[0]
    beads = own.shape[1] // 2
    unpack(images, wide_image, beads)
    more, more_gram = second_product(fill, own, wide, wide_image, high, low)
    both = (gram[...] + more_gram) / size
    inverse_zero, inverse_zero_t = small[0], small[1]
    cross_t = small_matmul(inverse_zero, block_sum(both, 0, 32))
    cross = small_matmul(block_sum(both, 32, 0), inverse_zero_t)
    factor_t, inverse = cholesky(block_sum(both, 32, 32) - small_matmul(cross, cross_t))
    alpha = small_matmul(cross_t, inverse_zero_t)
    factor_one_t = small_matmul(factor_t, inverse_zero_t)
    assemble(products[...] + more, image)
    first, moved = own_first[...], own_moved[...]
    vectors = small_matmul(inverse, flat(own_images[0]) - small_matmul(cross, first))
    shift = small_matmul(inverse, flat(image[...]) - small_matmul(cross, moved))
    shift = shift - small_matmul(factor_one_t, first)
    valid = lax.broadcasted_iota(jnp.int32, vectors.shape, 1) < 3 * beads
    vectors = jnp.where(valid, vectors, 0.0)
    shift = jnp.where(valid, shift, 0.0)
    partial = matmul_nt(vectors, shift, lax.Precision.HIGHEST)
    for row in range(8):
        partials[:, :, 8 * row : 8 * row + 8] = jnp.broadcast_to(
            partial[row : row + 1][None], (partials.shape[0], 1, 8)
        )
    vectors_out[...] = vectors
    shifted[...] = shift
    coefficients[0] = alpha
    coefficients[1] = factor_one_t.T


def last_kernel(size, vectors, shifted, both, partials, basis, residual, coefficients):
    beads = basis.shape[2]
    width = partials.shape[2]
    total = jnp.sum(partials[...], axis=0) / size
    spread = jnp.broadcast_to(total, (8, width))
    rows = lax.broadcasted_iota(jnp.int32, spread.shape, 0)
    cols = lax.broadcasted_iota(jnp.int32, spread.shape, 1)
    block = vectors[...]
    left = shifted[...]
    transposed = jnp.where(cols % 8 == rows, spread, 0.0)
    for k in range(8):
        column = jnp.sum(jnp.where(cols // 8 == k, transposed, 0.0), axis=1, keepdims=True)
        left = left - column * block[k : k + 1, :]
    coefficients[0:2] = both[...]
    for k in range(8):
        coefficients[2, k : k + 1, :] = total[:, 8 * k : 8 * k + 8]
    for part in range(3):
        basis[part] = block[:, part * beads : (part + 1) * beads]
        residual[part] = left[:, part * beads : (part + 1) * beads]


def array(*shape, dtype=F32):
    return jax.ShapeDtypeStruct(shape, dtype)


def call(kernel, outs, scratch=(), **options):
    return pl.pallas_call(
        kernel,
        out_shape=outs,
        scratch_shapes=list(scratch),
        compiler_params=pltpu.CompilerParams(vmem_limit_bytes=48 * 1024 * 1024),
        **options,
    )


def gather(copies):
    rows, cols = lax.axis_size("row"), lax.axis_size("col")
    groups = [
        [row * cols + col for row in range(rows) for col in range(core, cols, 2)] for core in range(2)
    ]
    mine = lax.all_to_all(copies, ("row", "col"), 0, 0, axis_index_groups=groups, tiled=True)
    other = lax.ppermute(mine, "col", [(col, col ^ 1) for col in range(cols)])
    return mine, other


def local(positions, noise):
    vecs, _, beads = noise.shape
    devices = lax.axis_size("row") * lax.axis_size("col")
    chips = devices // 2
    half = beads * chips
    size = 3.0 * 2.0 * half
    keep = 2 * 2 * 2 * 6 * beads * half <= KEPT
    width = half if keep else min(half, CHUNK)
    blocks = array(chips, 2 * vecs, 2 * beads)
    wide = array(4 * vecs, half)
    held_wide = pltpu.VMEM((4 * vecs, half), F32)
    block = pltpu.VMEM((2 * vecs, 2 * beads), F32)
    products = array(4 * vecs, 6 * beads)
    tensors = [array(6 * beads, width, dtype=BF16)] * 2 if keep else []
    held = [] if keep else [pltpu.VMEM((6 * beads, width), BF16)] * 2
    flat_block = array(vecs, 4 * beads)
    small_gram, large_gram = array(4 * vecs, 4 * vecs), array(8 * vecs, 8 * vecs)

    rows = noise.transpose(1, 0, 2).reshape(3 * vecs, beads)
    rows = jnp.concatenate([rows, jnp.pad(positions, ((0, vecs - 3), (0, 0)))], axis=0)
    own = call(pack_kernel, blocks)(rows)
    one, two = gather(own)
    one_products, one_gram, one_wide, *one_tensor = call(
        first_half_kernel, [products, small_gram, wide] + tensors, held
    )(own, one)
    own_images, two_gram, two_wide, *two_tensor = call(
        second_half_kernel, [blocks, small_gram, wide] + tensors, held + [block]
    )(own, two, one_products)
    one_images, two_images = gather(own_images)
    small, own_first, own_moved = call(
        functools.partial(start_kernel, size), [array(2, vecs, vecs), flat_block, flat_block]
    )(own_images, own, one_gram, two_gram)
    fill = not keep
    one_products, gram = call(ordered(functools.partial(third_half_kernel, fill), fill, 3, 2), [products, large_gram], held + [held_wide])(
        own, one_images, one_wide, *one_tensor
    )
    vectors, shifted, both, partials = call(
        ordered(functools.partial(fourth_half_kernel, size, fill), fill, 9, 4),
        [flat_block, flat_block, array(2, vecs, vecs), array(devices, 1, vecs * vecs)],
        held + [held_wide, block],
    )(own, two_images, two_wide, *two_tensor, one_products, gram, own_images, own_first, own_moved, small)
    partials = lax.all_to_all(partials, ("row", "col"), 0, 0, tiled=True)
    basis, residual, coefficients = call(
        functools.partial(last_kernel, size),
        [array(3, vecs, beads), array(3, vecs, beads), array(3, vecs, vecs)],
    )(vectors, shifted, both, partials)
    return (basis.transpose(1, 0, 2), residual.transpose(1, 0, 2), coefficients)


def ordered(kernel, fill, ins, outs):
    if not fill:
        return kernel

    def moved(*refs):
        scratch = refs[ins + outs :]
        kernel(*refs[:3], *scratch[:2], *refs[3 : ins + outs], *scratch[2:])

    return moved


def solution(mesh):
    return jax.shard_map(
        local,
        mesh=mesh,
        in_specs=(P(None, ("row", "col")), P(None, None, ("row", "col"))),
        out_specs=(P(None, None, ("row", "col")), P(None, None, ("row", "col")), P()),
        check_vma=False,
    )
```

```python
import functools

import jax
import jax.numpy as jnp
from jax import lax
from jax.experimental import pallas as pl
from jax.experimental.pallas import tpu as pltpu
from jax.sharding import PartitionSpec as P

CHUNK = 1024
KEPT = 8 * 1024 * 1024
F32 = jnp.float32
BF16 = jnp.bfloat16


def pack_kernel(rows, blocks):
    beads = rows.shape[1]
    vecs = blocks.shape[1] // 2
    upper = jnp.concatenate([rows[:vecs], rows[vecs : 2 * vecs]], axis=1)
    lower = jnp.concatenate([rows[2 * vecs : 3 * vecs], rows[3 * vecs :]], axis=1)
    blocks[:, :vecs] = jnp.broadcast_to(upper[None], (blocks.shape[0], vecs, 2 * beads))
    blocks[:, vecs:] = jnp.broadcast_to(lower[None], (blocks.shape[0], vecs, 2 * beads))


def split_two(value):
    high = value.astype(BF16)
    return high, (value - high.astype(F32)).astype(BF16)


def matmul_nt(left, right, precision=None):
    return lax.dot_general(
        left, right, (((1,), (1,)), ((), ())), precision=precision, preferred_element_type=F32
    )


def small_matmul(left, right):
    total = left[:, 0:1] * right[0:1, :]
    for k in range(1, left.shape[1]):
        total = total + left[:, k : k + 1] * right[k : k + 1, :]
    return total


def unpack(blocks, wide, beads):
    for index in range(0, blocks.shape[0], 2):
        one, two = blocks[index], blocks[index + 1]
        half = one.shape[0] // 2
        lanes = pl.ds(index * beads, 2 * beads)
        for part in range(4):
            rows = slice(part // 2 * half, (part // 2 + 1) * half)
            side = slice(part % 2 * beads, (part % 2 + 1) * beads)
            wide[part * half : (part + 1) * half, lanes] = jnp.concatenate(
                [one[rows, side], two[rows, side]], axis=1
            )


def target_columns(own):
    beads = own.shape[1] // 2
    targets = own[8:16, beads:].T
    return [jnp.broadcast_to(targets[:, axis : axis + 1], (beads, 128)) for axis in range(3)]


def fill_tensor(columns, wide, start, high, low, at):
    beads = columns[0].shape[0]
    sources = pl.ds(start, 128)
    to = pl.ds(at, 128)
    moved = [columns[axis] - wide[24 + axis : 25 + axis, sources] for axis in range(3)]
    square = moved[0] * moved[0] + moved[1] * moved[1] + moved[2] * moved[2]
    square = jnp.maximum(square, 1e-12)
    inverse = lax.rsqrt(square)
    inverse_sq = inverse * inverse
    near = square < 4.0
    iso = inverse * jnp.where(near, square * (inverse - 9.0 / 32.0), 0.75 + 0.5 * inverse_sq)
    along = inverse * jnp.where(near, 3.0 / 32.0, inverse_sq * (0.75 - 1.5 * inverse_sq))
    scaled = [along * item for item in moved]
    parts = [
        iso + scaled[0] * moved[0],
        scaled[0] * moved[1],
        scaled[0] * moved[2],
        iso + scaled[1] * moved[1],
        scaled[1] * moved[2],
        iso + scaled[2] * moved[2],
    ]
    for part, value in enumerate(parts):
        upper, lower = split_two(value)
        high[part * beads : (part + 1) * beads, to] = upper
        low[part * beads : (part + 1) * beads, to] = lower


def apply_tensor(both, high, low, at, step):
    lanes = pl.ds(at, step)
    half = both.shape[0] // 2
    first = matmul_nt(both, high[:, lanes])
    return first[:half] + first[half:] + matmul_nt(both[:half], low[:, lanes])


def split_rows(*values):
    highs, lows = zip(*[split_two(value) for value in values])
    return jnp.concatenate(highs + lows, axis=0)


def inner(both):
    half = both.shape[0] // 2
    first = matmul_nt(both, both[:half])
    return first[:half] + first[half:] + matmul_nt(both[:half], both[half:])


def assemble(products, image):
    beads = image.shape[1] // 2

    def part(row, component):
        return products[8 * row : 8 * row + 8, component * beads : (component + 1) * beads]

    image[...] = jnp.zeros(image.shape, F32)
    image[:8, :beads] = part(0, 0) + part(1, 1) + part(2, 2)
    image[:8, beads:] = part(0, 1) + part(1, 3) + part(2, 4)
    image[8:, :beads] = part(0, 2) + part(1, 4) + part(2, 5)


def flat(block):
    return jnp.concatenate([block[:8], block[8:]], axis=1)


def block_sum(matrix, row, column):
    parts = [
        matrix[row + 8 * part : row + 8 * part + 8, column + 8 * part : column + 8 * part + 8]
        for part in range(3)
    ]
    return parts[0] + parts[1] + parts[2]


def filled_product(columns, source, wide, start, high, low, with_gram):
    width = high.shape[1]
    step = 256 if width % 256 == 0 else 128
    products = jnp.zeros((32, high.shape[0]), F32)
    for at in range(0, width, step):
        for part in range(at, at + step, 128):
            fill_tensor(columns, source, pl.multiple_of(start + part, 128), high, low, part)
        both = split_rows(wide[:, pl.ds(pl.multiple_of(start + at, 128), step)])
        products = products + apply_tensor(both, high, low, at, step)
    if with_gram:
        both = split_rows(wide[:, pl.ds(pl.multiple_of(start, 128), width)])
        return products, inner(both)
    return (products,)


def all_chunks(total, width, chunk):
    if total == width:
        return chunk(0)
    body = lambda index, sums: tuple(a + b for a, b in zip(sums, chunk(index * width)))
    return lax.fori_loop(1, total // width, body, chunk(0))


def first_product(own, wide, high, low):
    columns = target_columns(own)
    return all_chunks(
        wide.shape[1], high.shape[1], lambda start: filled_product(columns, wide, wide, start, high, low, True)
    )


def first_half_kernel(own_blocks, blocks, products, gram, wide, high, low):
    own = own_blocks[0]
    unpack(blocks, wide, own.shape[1] // 2)
    products[...], gram[...] = first_product(own, wide, high, low)


def second_half_kernel(own_blocks, blocks, products, images, gram, wide, high, low, image):
    own = own_blocks[0]
    unpack(blocks, wide, own.shape[1] // 2)
    more, gram[...] = first_product(own, wide, high, low)
    assemble(products[...] + more, image)
    images[...] = jnp.broadcast_to(image[...][None], images.shape)


def cholesky(matrix):
    size = matrix.shape[0]
    shape = (size, size)
    rows = lax.broadcasted_iota(jnp.int32, shape, 0)
    cols = lax.broadcasted_iota(jnp.int32, shape, 1)
    entry = {}
    for j in range(size):
        column = jnp.broadcast_to(matrix[:, j : j + 1], shape)
        for i in range(j, size):
            entry[i, j] = jnp.broadcast_to(column[i : i + 1, :], shape)
    factor_t = jnp.zeros(shape, F32)
    inverse = jnp.zeros(shape, F32)
    inverse_rows = []
    for j in range(size):
        scale = lax.rsqrt(entry[j, j])
        lower_row = entry[j, j] * scale
        entry[j, j] = scale
        for i in range(j + 1, size):
            entry[i, j] = entry[i, j] * scale
        for i in range(j + 1, size):
            for k in range(j + 1, i + 1):
                entry[i, k] = entry[i, k] - entry[i, j] * entry[k, j]
        lower_row = jnp.where(cols == j, lower_row, 0.0)
        for i in range(j + 1, size):
            lower_row = jnp.where(cols == i, entry[i, j], lower_row)
        factor_t = jnp.where(rows == j, lower_row, factor_t)
        row = jnp.where(cols == j, 1.0, 0.0)
        for k in range(j):
            row = row - entry[j, k] * inverse_rows[k]
        row = row * scale
        inverse_rows.append(row)
        inverse = jnp.where(rows == j, row, inverse)
    return factor_t, inverse


def start_kernel(size, images, own_blocks, one_gram, two_gram, small, own_first, own_moved):
    _, inverse = cholesky(block_sum(one_gram[...] + two_gram[...], 0, 0) / size)
    own_first[...] = small_matmul(inverse, flat(own_blocks[0]))
    own_moved[...] = small_matmul(inverse, flat(images[0]))
    small[0] = inverse
    small[1] = inverse.T


def second_product(fill, own, wide, wide_image, high, low):
    grams = inner(split_rows(wide[...], wide_image[...]))
    if not fill:
        return apply_tensor(split_rows(wide_image[...]), high, low, 0, high.shape[1]), grams
    columns = target_columns(own)
    (products,) = all_chunks(
        wide.shape[1],
        high.shape[1],
        lambda start: filled_product(columns, wide, wide_image, start, high, low, False),
    )
    return products, grams


def third_half_kernel(fill, own_blocks, images, wide, high, low, products, gram, wide_image):
    own = own_blocks[0]
    unpack(images, wide_image, own.shape[1] // 2)
    products[...], gram[...] = second_product(fill, own, wide, wide_image, high, low)


def fourth_half_kernel(
    size, fill, own_blocks, images, wide, high, low, products, gram, own_images, own_first, own_moved, small,
    vectors_out, shifted, coefficients, partials, wide_image, image
):
    own = own_blocks[0]
    beads = own.shape[1] // 2
    unpack(images, wide_image, beads)
    more, more_gram = second_product(fill, own, wide, wide_image, high, low)
    both = (gram[...] + more_gram) / size
    inverse_zero, inverse_zero_t = small[0], small[1]
    cross_t = small_matmul(inverse_zero, block_sum(both, 0, 32))
    cross = small_matmul(block_sum(both, 32, 0), inverse_zero_t)
    factor_t, inverse = cholesky(block_sum(both, 32, 32) - small_matmul(cross, cross_t))
    alpha = small_matmul(cross_t, inverse_zero_t)
    factor_one_t = small_matmul(factor_t, inverse_zero_t)
    assemble(products[...] + more, image)
    first, moved = own_first[...], own_moved[...]
    vectors = small_matmul(inverse, flat(own_images[0]) - small_matmul(cross, first))
    shift = small_matmul(inverse, flat(image[...]) - small_matmul(cross, moved))
    shift = shift - small_matmul(factor_one_t, first)
    valid = lax.broadcasted_iota(jnp.int32, vectors.shape, 1) < 3 * beads
    vectors = jnp.where(valid, vectors, 0.0)
    shift = jnp.where(valid, shift, 0.0)
    partial = matmul_nt(vectors, shift, lax.Precision.HIGHEST)
    for row in range(8):
        partials[:, :, 8 * row : 8 * row + 8] = jnp.broadcast_to(
            partial[row : row + 1][None], (partials.shape[0], 1, 8)
        )
    vectors_out[...] = vectors
    shifted[...] = shift
    coefficients[0] = alpha
    coefficients[1] = factor_one_t.T


def last_kernel(size, vectors, shifted, both, partials, basis, residual, coefficients):
    beads = basis.shape[2]
    width = partials.shape[2]
    total = jnp.sum(partials[...], axis=0) / size
    spread = jnp.broadcast_to(total, (8, width))
    rows = lax.broadcasted_iota(jnp.int32, spread.shape, 0)
    cols = lax.broadcasted_iota(jnp.int32, spread.shape, 1)
    block = vectors[...]
    left = shifted[...]
    transposed = jnp.where(cols % 8 == rows, spread, 0.0)
    for k in range(8):
        column = jnp.sum(jnp.where(cols // 8 == k, transposed, 0.0), axis=1, keepdims=True)
        left = left - column * block[k : k + 1, :]
    coefficients[0:2] = both[...]
    for k in range(8):
        coefficients[2, k : k + 1, :] = total[:, 8 * k : 8 * k + 8]
    for part in range(3):
        basis[part] = block[:, part * beads : (part + 1) * beads]
        residual[part] = left[:, part * beads : (part + 1) * beads]


def array(*shape, dtype=F32):
    return jax.ShapeDtypeStruct(shape, dtype)


def call(kernel, outs, scratch=(), **options):
    return pl.pallas_call(
        kernel,
        out_shape=outs,
        scratch_shapes=list(scratch),
        compiler_params=pltpu.CompilerParams(vmem_limit_bytes=48 * 1024 * 1024),
        **options,
    )


def gather(copies):
    rows, cols = lax.axis_size("row"), lax.axis_size("col")
    groups = [[], []]
    for row in range(rows):
        for col in range(cols):
            groups[(bin(row).count("1") + col // 2 + col) % 2].append(row * cols + col)
    mine = lax.all_to_all(copies, ("row", "col"), 0, 0, axis_index_groups=groups, tiled=True)
    other = lax.ppermute(mine, "col", [(col, col ^ 1) for col in range(cols)])
    return mine, other


def local(positions, noise):
    vecs, _, beads = noise.shape
    devices = lax.axis_size("row") * lax.axis_size("col")
    chips = devices // 2
    half = beads * chips
    size = 3.0 * 2.0 * half
    keep = 2 * 2 * 2 * 6 * beads * half <= KEPT
    width = half if keep else min(half, CHUNK)
    blocks = array(chips, 2 * vecs, 2 * beads)
    wide = array(4 * vecs, half)
    held_wide = pltpu.VMEM((4 * vecs, half), F32)
    block = pltpu.VMEM((2 * vecs, 2 * beads), F32)
    products = array(4 * vecs, 6 * beads)
    tensors = [array(6 * beads, width, dtype=BF16)] * 2 if keep else []
    held = [] if keep else [pltpu.VMEM((6 * beads, width), BF16)] * 2
    flat_block = array(vecs, 4 * beads)
    small_gram, large_gram = array(4 * vecs, 4 * vecs), array(8 * vecs, 8 * vecs)

    rows = noise.transpose(1, 0, 2).reshape(3 * vecs, beads)
    rows = jnp.concatenate([rows, jnp.pad(positions, ((0, vecs - 3), (0, 0)))], axis=0)
    own = call(pack_kernel, blocks)(rows)
    one, two = gather(own)
    one_products, one_gram, one_wide, *one_tensor = call(
        first_half_kernel, [products, small_gram, wide] + tensors, held
    )(own, one)
    own_images, two_gram, two_wide, *two_tensor = call(
        second_half_kernel, [blocks, small_gram, wide] + tensors, held + [block]
    )(own, two, one_products)
    one_images, two_images = gather(own_images)
    small, own_first, own_moved = call(
        functools.partial(start_kernel, size), [array(2, vecs, vecs), flat_block, flat_block]
    )(own_images, own, one_gram, two_gram)
    fill = not keep
    one_products, gram = call(ordered(functools.partial(third_half_kernel, fill), fill, 3, 2), [products, large_gram], held + [held_wide])(
        own, one_images, one_wide, *one_tensor
    )
    vectors, shifted, both, partials = call(
        ordered(functools.partial(fourth_half_kernel, size, fill), fill, 9, 4),
        [flat_block, flat_block, array(2, vecs, vecs), array(devices, 1, vecs * vecs)],
        held + [held_wide, block],
    )(own, two_images, two_wide, *two_tensor, one_products, gram, own_images, own_first, own_moved, small)
    partials = lax.all_to_all(partials, ("row", "col"), 0, 0, tiled=True)
    basis, residual, coefficients = call(
        functools.partial(last_kernel, size),
        [array(3, vecs, beads), array(3, vecs, beads), array(3, vecs, vecs)],
    )(vectors, shifted, both, partials)
    return (basis.transpose(1, 0, 2), residual.transpose(1, 0, 2), coefficients)


def ordered(kernel, fill, ins, outs):
    if not fill:
        return kernel

    def moved(*refs):
        scratch = refs[ins + outs :]
        kernel(*refs[:3], *scratch[:2], *refs[3 : ins + outs], *scratch[2:])

    return moved


def solution(mesh):
    return jax.shard_map(
        local,
        mesh=mesh,
        in_specs=(P(None, ("row", "col")), P(None, None, ("row", "col"))),
        out_specs=(P(None, None, ("row", "col")), P(None, None, ("row", "col")), P()),
        check_vma=False,
    )
```

```python
import functools

import jax
import jax.numpy as jnp
from jax import lax
from jax.experimental import pallas as pl
from jax.experimental.pallas import tpu as pltpu
from jax.sharding import PartitionSpec as P

CHUNK = 1024
KEPT = 8 * 1024 * 1024
F32 = jnp.float32
BF16 = jnp.bfloat16


def pack_kernel(rows, blocks):
    beads = rows.shape[1]
    vecs = blocks.shape[1] // 2
    upper = jnp.concatenate([rows[:vecs], rows[vecs : 2 * vecs]], axis=1)
    lower = jnp.concatenate([rows[2 * vecs : 3 * vecs], rows[3 * vecs :]], axis=1)
    blocks[:, :vecs] = jnp.broadcast_to(upper[None], (blocks.shape[0], vecs, 2 * beads))
    blocks[:, vecs:] = jnp.broadcast_to(lower[None], (blocks.shape[0], vecs, 2 * beads))


def split_two(value):
    high = value.astype(BF16)
    return high, (value - high.astype(F32)).astype(BF16)


def matmul_nt(left, right, precision=None):
    return lax.dot_general(
        left, right, (((1,), (1,)), ((), ())), precision=precision, preferred_element_type=F32
    )


def small_matmul(left, right):
    total = left[:, 0:1] * right[0:1, :]
    for k in range(1, left.shape[1]):
        total = total + left[:, k : k + 1] * right[k : k + 1, :]
    return total


def unpack(arrays, wide, beads):
    blocks = [(array, index) for array in arrays for index in range(array.shape[0])]
    for at in range(0, len(blocks), 2):
        one, two = [array[index] for array, index in blocks[at : at + 2]]
        half = one.shape[0] // 2
        lanes = pl.ds(at * beads, 2 * beads)
        for part in range(4):
            rows = slice(part // 2 * half, (part // 2 + 1) * half)
            side = slice(part % 2 * beads, (part % 2 + 1) * beads)
            wide[part * half : (part + 1) * half, lanes] = jnp.concatenate(
                [one[rows, side], two[rows, side]], axis=1
            )


def target_columns(own):
    beads = own.shape[1] // 2
    targets = own[8:16, beads:].T
    return [jnp.broadcast_to(targets[:, axis : axis + 1], (beads, 128)) for axis in range(3)]


def fill_tensor(columns, wide, start, high, low, at):
    beads = columns[0].shape[0]
    sources = pl.ds(start, 128)
    to = pl.ds(at, 128)
    moved = [columns[axis] - wide[24 + axis : 25 + axis, sources] for axis in range(3)]
    square = moved[0] * moved[0] + moved[1] * moved[1] + moved[2] * moved[2]
    square = jnp.maximum(square, 1e-12)
    inverse = lax.rsqrt(square)
    inverse_sq = inverse * inverse
    near = square < 4.0
    iso = inverse * jnp.where(near, square * (inverse - 9.0 / 32.0), 0.75 + 0.5 * inverse_sq)
    along = inverse * jnp.where(near, 3.0 / 32.0, inverse_sq * (0.75 - 1.5 * inverse_sq))
    scaled = [along * item for item in moved]
    parts = [
        iso + scaled[0] * moved[0],
        scaled[0] * moved[1],
        scaled[0] * moved[2],
        iso + scaled[1] * moved[1],
        scaled[1] * moved[2],
        iso + scaled[2] * moved[2],
    ]
    for part, value in enumerate(parts):
        upper, lower = split_two(value)
        high[part * beads : (part + 1) * beads, to] = upper
        low[part * beads : (part + 1) * beads, to] = lower


def apply_tensor(both, high, low, at, step):
    lanes = pl.ds(at, step)
    half = both.shape[0] // 2
    first = matmul_nt(both, high[:, lanes])
    return first[:half] + first[half:] + matmul_nt(both[:half], low[:, lanes])


def split_rows(*values):
    highs, lows = zip(*[split_two(value) for value in values])
    return jnp.concatenate(highs + lows, axis=0)


def inner(both):
    half = both.shape[0] // 2
    first = matmul_nt(both, both[:half])
    return first[:half] + first[half:] + matmul_nt(both[:half], both[half:])


def assemble(products, image):
    beads = image.shape[1] // 2

    def part(row, component):
        return products[8 * row : 8 * row + 8, component * beads : (component + 1) * beads]

    image[...] = jnp.zeros(image.shape, F32)
    image[:8, :beads] = part(0, 0) + part(1, 1) + part(2, 2)
    image[:8, beads:] = part(0, 1) + part(1, 3) + part(2, 4)
    image[8:, :beads] = part(0, 2) + part(1, 4) + part(2, 5)


def flat(block):
    return jnp.concatenate([block[:8], block[8:]], axis=1)


def block_sum(matrix, row, column):
    parts = [
        matrix[row + 8 * part : row + 8 * part + 8, column + 8 * part : column + 8 * part + 8]
        for part in range(3)
    ]
    return parts[0] + parts[1] + parts[2]


def filled_product(columns, source, wide, start, high, low, with_gram):
    width = high.shape[1]
    products = jnp.zeros((32, high.shape[0]), F32)
    for at in range(0, width, 256):
        step = min(256, width - at)
        for part in range(at, at + step, 128):
            fill_tensor(columns, source, pl.multiple_of(start + part, 128), high, low, part)
        both = split_rows(wide[:, pl.ds(pl.multiple_of(start + at, 128), step)])
        products = products + apply_tensor(both, high, low, at, step)
    if with_gram:
        both = split_rows(wide[:, pl.ds(pl.multiple_of(start, 128), width)])
        return products, inner(both)
    return (products,)


def all_chunks(total, width, chunk):
    if total == width:
        return chunk(0)
    body = lambda index, sums: tuple(a + b for a, b in zip(sums, chunk(index * width)))
    return lax.fori_loop(1, total // width, body, chunk(0))


def first_product(own, wide, high, low):
    columns = target_columns(own)
    return all_chunks(
        wide.shape[1], high.shape[1], lambda start: filled_product(columns, wide, wide, start, high, low, True)
    )


def first_stage(count, earlier, last, *refs):
    refs = list(refs)
    own_ref, blocks, refs = refs[0], refs[1 : count + 1], refs[count + 1 :]
    before, refs = refs[: 2 * earlier], refs[2 * earlier :]
    out, gram, wide, high, low = refs[:5]
    own = own_ref[0]
    unpack(blocks, wide, own.shape[1] // 2)
    products, grams = first_product(own, wide, high, low)
    if earlier:
        products, grams = products + before[0][...], grams + before[1][...]
    gram[...] = grams
    if last:
        assemble(products, refs[5])
        out[0] = refs[5][...]
    else:
        out[...] = products


def cholesky(matrix):
    size = matrix.shape[0]
    shape = (size, size)
    rows = lax.broadcasted_iota(jnp.int32, shape, 0)
    cols = lax.broadcasted_iota(jnp.int32, shape, 1)
    entry = {}
    for j in range(size):
        column = jnp.broadcast_to(matrix[:, j : j + 1], shape)
        for i in range(j, size):
            entry[i, j] = jnp.broadcast_to(column[i : i + 1, :], shape)
    factor_t = jnp.zeros(shape, F32)
    inverse = jnp.zeros(shape, F32)
    inverse_rows = []
    for j in range(size):
        scale = lax.rsqrt(entry[j, j])
        lower_row = entry[j, j] * scale
        entry[j, j] = scale
        for i in range(j + 1, size):
            entry[i, j] = entry[i, j] * scale
        for i in range(j + 1, size):
            for k in range(j + 1, i + 1):
                entry[i, k] = entry[i, k] - entry[i, j] * entry[k, j]
        lower_row = jnp.where(cols == j, lower_row, 0.0)
        for i in range(j + 1, size):
            lower_row = jnp.where(cols == i, entry[i, j], lower_row)
        factor_t = jnp.where(rows == j, lower_row, factor_t)
        row = jnp.where(cols == j, 1.0, 0.0)
        for k in range(j):
            row = row - entry[j, k] * inverse_rows[k]
        row = row * scale
        inverse_rows.append(row)
        inverse = jnp.where(rows == j, row, inverse)
    return factor_t, inverse


def start_kernel(size, image, own_block, gram, small, own_first, own_moved):
    _, inverse = cholesky(block_sum(gram[...], 0, 0) / size)
    own_first[...] = small_matmul(inverse, flat(own_block[0]))
    own_moved[...] = small_matmul(inverse, flat(image[0]))
    small[0] = inverse
    small[1] = inverse.T


def second_product(fill, own, wide, wide_image, high, low):
    grams = inner(split_rows(wide[...], wide_image[...]))
    if not fill:
        return apply_tensor(split_rows(wide_image[...]), high, low, 0, high.shape[1]), grams
    columns = target_columns(own)
    (products,) = all_chunks(
        wide.shape[1],
        high.shape[1],
        lambda start: filled_product(columns, wide, wide_image, start, high, low, False),
    )
    return products, grams


def second_stage(size, count, earlier, last, fill, *refs):
    refs = list(refs)
    own_ref, wide, refs = refs[0], refs[1], refs[2:]
    if not fill:
        (high, low), refs = refs[:2], refs[2:]
    images, refs = refs[:count], refs[count:]
    before, refs = refs[: 2 * earlier], refs[2 * earlier :]
    if last:
        (own_image, own_first, own_moved, small), refs = refs[:4], refs[4:]
    outs, refs = refs[: 4 if last else 2], refs[4 if last else 2 :]
    if fill:
        (high, low), refs = refs[:2], refs[2:]
    wide_image = refs[0]
    own = own_ref[0]
    beads = own.shape[1] // 2
    unpack(images, wide_image, beads)
    products, grams = second_product(fill, own, wide, wide_image, high, low)
    if earlier:
        products, grams = products + before[0][...], grams + before[1][...]
    if not last:
        outs[0][...], outs[1][...] = products, grams
        return
    vectors_out, shifted, coefficients, partials = outs
    grams = grams / size
    inverse_zero, inverse_zero_t = small[0], small[1]
    cross_t = small_matmul(inverse_zero, block_sum(grams, 0, 32))
    cross = small_matmul(block_sum(grams, 32, 0), inverse_zero_t)
    factor_t, inverse = cholesky(block_sum(grams, 32, 32) - small_matmul(cross, cross_t))
    alpha = small_matmul(cross_t, inverse_zero_t)
    factor_one_t = small_matmul(factor_t, inverse_zero_t)
    assemble(products, refs[1])
    first, moved = own_first[...], own_moved[...]
    vectors = small_matmul(inverse, flat(own_image[0]) - small_matmul(cross, first))
    shift = small_matmul(inverse, flat(refs[1][...]) - small_matmul(cross, moved))
    shift = shift - small_matmul(factor_one_t, first)
    valid = lax.broadcasted_iota(jnp.int32, vectors.shape, 1) < 3 * beads
    vectors = jnp.where(valid, vectors, 0.0)
    shift = jnp.where(valid, shift, 0.0)
    partial = matmul_nt(vectors, shift, lax.Precision.HIGHEST)
    for row in range(8):
        partials[:, :, 8 * row : 8 * row + 8] = jnp.broadcast_to(
            partial[row : row + 1][None], (partials.shape[0], 1, 8)
        )
    vectors_out[...] = vectors
    shifted[...] = shift
    coefficients[0] = alpha
    coefficients[1] = factor_one_t.T


def last_kernel(size, vectors, shifted, both, partials, basis, residual, coefficients):
    beads = basis.shape[2]
    width = partials.shape[2]
    total = jnp.sum(partials[...], axis=0) / size
    spread = jnp.broadcast_to(total, (8, width))
    rows = lax.broadcasted_iota(jnp.int32, spread.shape, 0)
    cols = lax.broadcasted_iota(jnp.int32, spread.shape, 1)
    block = vectors[...]
    left = shifted[...]
    transposed = jnp.where(cols % 8 == rows, spread, 0.0)
    for k in range(8):
        column = jnp.sum(jnp.where(cols // 8 == k, transposed, 0.0), axis=1, keepdims=True)
        left = left - column * block[k : k + 1, :]
    coefficients[0:2] = both[...]
    for k in range(8):
        coefficients[2, k : k + 1, :] = total[:, 8 * k : 8 * k + 8]
    for part in range(3):
        basis[part] = block[:, part * beads : (part + 1) * beads]
        residual[part] = left[:, part * beads : (part + 1) * beads]


def array(*shape, dtype=F32):
    return jax.ShapeDtypeStruct(shape, dtype)


def call(kernel, outs, scratch=(), **options):
    return pl.pallas_call(
        kernel,
        out_shape=outs,
        scratch_shapes=list(scratch),
        compiler_params=pltpu.CompilerParams(vmem_limit_bytes=48 * 1024 * 1024),
        **options,
    )


def exchange(block, first, second):
    rows, cols = lax.axis_size("row"), lax.axis_size("col")
    layers = cols // 2
    pairs = []
    for chip in range(rows * layers):
        for core, offset in enumerate((first, second)):
            if offset is not None:
                pairs.append((2 * chip + core, 2 * (chip ^ offset) + core))
    return lax.ppermute(block, ("row", "col"), pairs)


def between_cores(block):
    cols = lax.axis_size("col")
    return lax.ppermute(block, "col", [(col, col ^ 1) for col in range(cols)])


ROWS, LAYERS = 4, 4
ALONE = 1
OFFSETS = ((3, 6), (5, 2), (4, 9), (8, 12))


def spread(block, use):
    rows, cols = lax.axis_size("row"), lax.axis_size("col")
    if (rows, cols) == (ROWS, 2 * LAYERS):
        pair = jnp.concatenate([block, between_cores(block)], axis=0)
        one = exchange(pair, *OFFSETS[0])
        alone = exchange(pair, None, ALONE)
        two = exchange(pair, *OFFSETS[1])
        three = exchange(jnp.concatenate([pair, one], axis=0), *OFFSETS[2])
        four = exchange(jnp.concatenate([pair, one, two], axis=0), *OFFSETS[3])
        siblings = between_cores(jnp.concatenate([alone, one, two, three], axis=0))
        used = use(0, False, [pair, one, two, three])
        four, used = lax.optimization_barrier((four, used))
        last = between_cores(four)
        used = use(1, False, [four, alone, siblings], *used)
        return use(2, True, [last], *used)
    groups = [[row * cols + col for row in range(rows) for col in range(core, cols, 2)] for core in range(2)]
    copies = jnp.broadcast_to(block, (rows * cols // 2,) + block.shape[1:])
    mine = lax.all_to_all(copies, ("row", "col"), 0, 0, axis_index_groups=groups, tiled=True)
    other = between_cores(mine)
    return use(1, True, [other], *use(0, False, [mine]))


def local(positions, noise):
    vecs, _, beads = noise.shape
    devices = lax.axis_size("row") * lax.axis_size("col")
    size = 3.0 * beads * devices
    keep = 2 * 2 * 6 * beads * beads * devices <= KEPT
    block = array(1, 2 * vecs, 2 * beads)
    held_block = pltpu.VMEM((2 * vecs, 2 * beads), F32)
    products = array(4 * vecs, 6 * beads)
    flat_block = array(vecs, 4 * beads)
    small_gram, large_gram = array(4 * vecs, 4 * vecs), array(8 * vecs, 8 * vecs)

    rows = noise.transpose(1, 0, 2).reshape(3 * vecs, beads)
    rows = jnp.concatenate([rows, jnp.pad(positions, ((0, vecs - 3), (0, 0)))], axis=0)
    own = call(pack_kernel, block)(rows)
    kept = {}

    def use_first(index, last, blocks, *before):
        total = beads * sum(item.shape[0] for item in blocks)
        shape = (6 * beads, total if keep else min(total, CHUNK))
        kernel = functools.partial(first_stage, len(blocks), index > 0, last)
        outs = [block if last else products, small_gram, array(4 * vecs, total)]
        scratch = [held_block] if last else []
        if keep:
            outs = outs + [array(*shape, dtype=BF16)] * 2
        else:
            scratch = [pltpu.VMEM(shape, BF16)] * 2 + scratch
        *before, wide, high, low = (list(call(kernel, outs, scratch)(own, *blocks, *before)) + [None, None])[:5]
        kept[index] = (wide, high, low) if keep else (wide,)
        return before

    image, gram = spread(own, use_first)
    small, own_first, own_moved = call(
        functools.partial(start_kernel, size), [array(2, vecs, vecs), flat_block, flat_block]
    )(image, own, gram)

    def use_second(index, last, blocks, *before):
        total = beads * sum(item.shape[0] for item in blocks)
        kernel = functools.partial(second_stage, size, len(blocks), index > 0, last, not keep)
        outs, ins = [products, large_gram], []
        scratch = [pltpu.VMEM((4 * vecs, total), F32)]
        if last:
            outs = [flat_block, flat_block, array(2, vecs, vecs), array(devices, 1, vecs * vecs)]
            ins = [image, own_first, own_moved, small]
            scratch = scratch + [held_block]
        if not keep:
            scratch = [pltpu.VMEM((6 * beads, min(total, CHUNK)), BF16)] * 2 + scratch
        return call(kernel, outs, scratch)(own, *kept[index], *blocks, *before, *ins)

    vectors, shifted, both, partials = spread(image, use_second)
    partials = lax.all_to_all(partials, ("row", "col"), 0, 0, tiled=True)
    basis, residual, coefficients = call(
        functools.partial(last_kernel, size),
        [array(3, vecs, beads), array(3, vecs, beads), array(3, vecs, vecs)],
    )(vectors, shifted, both, partials)
    return (basis.transpose(1, 0, 2), residual.transpose(1, 0, 2), coefficients)


def solution(mesh):
    return jax.shard_map(
        local,
        mesh=mesh,
        in_specs=(P(None, ("row", "col")), P(None, None, ("row", "col"))),
        out_specs=(P(None, None, ("row", "col")), P(None, None, ("row", "col")), P()),
        check_vma=False,
    )
```

```python
import functools

import jax
import jax.numpy as jnp
from jax import lax
from jax.experimental import pallas as pl
from jax.experimental.pallas import tpu as pltpu
from jax.sharding import PartitionSpec as P

CHUNK = 1024
KEPT = 8 * 1024 * 1024
F32 = jnp.float32
BF16 = jnp.bfloat16


def halves(block):
    beads = block.shape[1] // 4
    middle = beads // 2
    parts = [block[:, part * beads : (part + 1) * beads] for part in range(4)]
    first = jnp.concatenate([part[:, :middle] for part in parts], axis=1)
    second = jnp.concatenate([part[:, middle:] for part in parts], axis=1)
    return first, second


def copy_halves(block, copies):
    for core, half in enumerate(halves(block)):
        copies[:, core] = jnp.broadcast_to(half[None], (copies.shape[0],) + half.shape)


def pack_kernel(rows, block, copies):
    vecs = block.shape[0]
    flat = jnp.concatenate([rows[part * vecs : (part + 1) * vecs] for part in range(4)], axis=1)
    block[...] = flat
    copy_halves(flat, copies)


def split_two(value):
    high = value.astype(BF16)
    return high, (value - high.astype(F32)).astype(BF16)


def matmul_nt(left, right, precision=None):
    return lax.dot_general(
        left, right, (((1,), (1,)), ((), ())), precision=precision, preferred_element_type=F32
    )


def small_matmul(left, right):
    total = left[:, 0:1] * right[0:1, :]
    for k in range(1, left.shape[1]):
        total = total + left[:, k : k + 1] * right[k : k + 1, :]
    return total


def unpack(blocks, wide):
    count, vecs, lanes = blocks.shape
    width = lanes // 4
    for at in range(0, count, 4):
        four = [blocks[at + index] for index in range(4)]
        for part in range(4):
            wide[part * vecs : (part + 1) * vecs, pl.ds(at * width, 4 * width)] = jnp.concatenate(
                [block[:, part * width : (part + 1) * width] for block in four], axis=1
            )


def target_columns(own):
    beads = own.shape[1] // 4
    targets = own[:, 3 * beads :].T
    return [jnp.broadcast_to(targets[:, axis : axis + 1], (beads, 128)) for axis in range(3)]


def fill_tensor(columns, wide, start, high, low, at):
    beads = columns[0].shape[0]
    sources = pl.ds(start, 128)
    to = pl.ds(at, 128)
    moved = [columns[axis] - wide[24 + axis : 25 + axis, sources] for axis in range(3)]
    square = moved[0] * moved[0] + moved[1] * moved[1] + moved[2] * moved[2]
    square = jnp.maximum(square, 1e-12)
    inverse = lax.rsqrt(square)
    inverse_sq = inverse * inverse
    near = square < 4.0
    iso = inverse * jnp.where(near, square * (inverse - 9.0 / 32.0), 0.75 + 0.5 * inverse_sq)
    along = inverse * jnp.where(near, 3.0 / 32.0, inverse_sq * (0.75 - 1.5 * inverse_sq))
    scaled = [along * item for item in moved]
    parts = [
        iso + scaled[0] * moved[0],
        scaled[0] * moved[1],
        scaled[0] * moved[2],
        iso + scaled[1] * moved[1],
        scaled[1] * moved[2],
        iso + scaled[2] * moved[2],
    ]
    for part, value in enumerate(parts):
        upper, lower = split_two(value)
        high[part * beads : (part + 1) * beads, to] = upper
        low[part * beads : (part + 1) * beads, to] = lower


def apply_tensor(both, high, low, at, step):
    lanes = pl.ds(at, step)
    half = both.shape[0] // 2
    first = matmul_nt(both, high[:, lanes])
    return first[:half] + first[half:] + matmul_nt(both[:half], low[:, lanes])


def split_rows(*values):
    highs, lows = zip(*[split_two(value) for value in values])
    return jnp.concatenate(highs + lows, axis=0)


def inner(both):
    half = both.shape[0] // 2
    first = matmul_nt(both, both[:half])
    return first[:half] + first[half:] + matmul_nt(both[:half], both[half:])


def assemble(products):
    beads = products.shape[1] // 6

    def part(row, component):
        return products[8 * row : 8 * row + 8, component * beads : (component + 1) * beads]

    x = part(0, 0) + part(1, 1) + part(2, 2)
    y = part(0, 1) + part(1, 3) + part(2, 4)
    z = part(0, 2) + part(1, 4) + part(2, 5)
    return jnp.concatenate([x, y, z, jnp.zeros(x.shape, F32)], axis=1)


def block_sum(matrix, row, column):
    parts = [
        matrix[row + 8 * part : row + 8 * part + 8, column + 8 * part : column + 8 * part + 8]
        for part in range(3)
    ]
    return parts[0] + parts[1] + parts[2]


def filled_product(columns, source, wide, start, high, low, with_gram):
    width = high.shape[1]
    products = jnp.zeros((32, high.shape[0]), F32)
    for at in range(0, width, 256):
        step = min(256, width - at)
        for part in range(at, at + step, 128):
            fill_tensor(columns, source, pl.multiple_of(start + part, 128), high, low, part)
        both = split_rows(wide[:, pl.ds(pl.multiple_of(start + at, 128), step)])
        products = products + apply_tensor(both, high, low, at, step)
    if with_gram:
        both = split_rows(wide[:, pl.ds(pl.multiple_of(start, 128), width)])
        return products, inner(both)
    return (products,)


def all_chunks(total, width, chunk):
    if total == width:
        return chunk(0)
    body = lambda index, sums: tuple(a + b for a, b in zip(sums, chunk(index * width)))
    return lax.fori_loop(1, total // width, body, chunk(0))


def first_product(own, wide, high, low):
    columns = target_columns(own)
    return all_chunks(
        wide.shape[1], high.shape[1], lambda start: filled_product(columns, wide, wide, start, high, low, True)
    )


def first_stage(last, own, blocks, *refs):
    refs = list(refs)
    if last:
        before, refs = refs[:2], refs[2:]
        image, copies = refs[:2]
    else:
        products_out, copies = refs[0], None
    gram, wide, high, low = refs[2:6] if last else refs[1:5]
    unpack(blocks, wide)
    products, grams = first_product(own[...], wide, high, low)
    if not last:
        products_out[...], gram[...] = products, grams
        return
    gram[...] = grams + before[1][...]
    block = assemble(products + before[0][...])
    image[...] = block
    copy_halves(block, copies)


def cholesky(matrix):
    size = matrix.shape[0]
    shape = (size, size)
    rows = lax.broadcasted_iota(jnp.int32, shape, 0)
    cols = lax.broadcasted_iota(jnp.int32, shape, 1)
    entry = {}
    for j in range(size):
        column = jnp.broadcast_to(matrix[:, j : j + 1], shape)
        for i in range(j, size):
            entry[i, j] = jnp.broadcast_to(column[i : i + 1, :], shape)
    factor_t = jnp.zeros(shape, F32)
    inverse = jnp.zeros(shape, F32)
    inverse_rows = []
    for j in range(size):
        scale = lax.rsqrt(entry[j, j])
        lower_row = entry[j, j] * scale
        entry[j, j] = scale
        for i in range(j + 1, size):
            entry[i, j] = entry[i, j] * scale
        for i in range(j + 1, size):
            for k in range(j + 1, i + 1):
                entry[i, k] = entry[i, k] - entry[i, j] * entry[k, j]
        lower_row = jnp.where(cols == j, lower_row, 0.0)
        for i in range(j + 1, size):
            lower_row = jnp.where(cols == i, entry[i, j], lower_row)
        factor_t = jnp.where(rows == j, lower_row, factor_t)
        row = jnp.where(cols == j, 1.0, 0.0)
        for k in range(j):
            row = row - entry[j, k] * inverse_rows[k]
        row = row * scale
        inverse_rows.append(row)
        inverse = jnp.where(rows == j, row, inverse)
    return factor_t, inverse


def start_kernel(size, image, own, gram, small, own_first, own_moved):
    _, inverse = cholesky(block_sum(gram[...], 0, 0) / size)
    own_first[...] = small_matmul(inverse, own[...])
    own_moved[...] = small_matmul(inverse, image[...])
    small[0] = inverse
    small[1] = inverse.T


def second_product(fill, own, wide, wide_image, high, low):
    grams = inner(split_rows(wide[...], wide_image[...]))
    if not fill:
        return apply_tensor(split_rows(wide_image[...]), high, low, 0, high.shape[1]), grams
    columns = target_columns(own)
    (products,) = all_chunks(
        wide.shape[1],
        high.shape[1],
        lambda start: filled_product(columns, wide, wide_image, start, high, low, False),
    )
    return products, grams


def second_stage(size, last, fill, own, wide, *refs):
    refs = list(refs)
    if not fill:
        (high, low), refs = refs[:2], refs[2:]
    images, refs = refs[0], refs[1:]
    if last:
        (before, before_gram, own_image, own_first, own_moved, small), refs = refs[:6], refs[6:]
    outs, refs = refs[: 4 if last else 2], refs[4 if last else 2 :]
    if fill:
        (high, low), refs = refs[:2], refs[2:]
    wide_image = refs[0]
    beads = own.shape[1] // 4
    unpack(images, wide_image)
    products, grams = second_product(fill, own[...], wide, wide_image, high, low)
    if not last:
        outs[0][...], outs[1][...] = products, grams
        return
    vectors_out, shifted, coefficients, partials = outs
    products = products + before[...]
    grams = (grams + before_gram[...]) / size
    inverse_zero, inverse_zero_t = small[0], small[1]
    cross_t = small_matmul(inverse_zero, block_sum(grams, 0, 32))
    cross = small_matmul(block_sum(grams, 32, 0), inverse_zero_t)
    factor_t, inverse = cholesky(block_sum(grams, 32, 32) - small_matmul(cross, cross_t))
    alpha = small_matmul(cross_t, inverse_zero_t)
    factor_one_t = small_matmul(factor_t, inverse_zero_t)
    first, moved = own_first[...], own_moved[...]
    vectors = small_matmul(inverse, own_image[...] - small_matmul(cross, first))
    shift = small_matmul(inverse, assemble(products) - small_matmul(cross, moved))
    shift = shift - small_matmul(factor_one_t, first)
    valid = lax.broadcasted_iota(jnp.int32, vectors.shape, 1) < 3 * beads
    vectors = jnp.where(valid, vectors, 0.0)
    shift = jnp.where(valid, shift, 0.0)
    partial = matmul_nt(vectors, shift, lax.Precision.HIGHEST)
    for row in range(8):
        partials[:, :, 8 * row : 8 * row + 8] = jnp.broadcast_to(
            partial[row : row + 1][None], (partials.shape[0], 1, 8)
        )
    vectors_out[...] = vectors
    shifted[...] = shift
    coefficients[0] = alpha
    coefficients[1] = factor_one_t.T


def last_kernel(size, vectors, shifted, both, partials, basis, residual, coefficients):
    beads = basis.shape[2]
    width = partials.shape[2]
    total = jnp.sum(partials[...], axis=0) / size
    spread = jnp.broadcast_to(total, (8, width))
    rows = lax.broadcasted_iota(jnp.int32, spread.shape, 0)
    cols = lax.broadcasted_iota(jnp.int32, spread.shape, 1)
    block = vectors[...]
    left = shifted[...]
    transposed = jnp.where(cols % 8 == rows, spread, 0.0)
    for k in range(8):
        column = jnp.sum(jnp.where(cols // 8 == k, transposed, 0.0), axis=1, keepdims=True)
        left = left - column * block[k : k + 1, :]
    coefficients[0:2] = both[...]
    for k in range(8):
        coefficients[2, k : k + 1, :] = total[:, 8 * k : 8 * k + 8]
    for part in range(3):
        basis[part] = block[:, part * beads : (part + 1) * beads]
        residual[part] = left[:, part * beads : (part + 1) * beads]


def array(*shape, dtype=F32):
    return jax.ShapeDtypeStruct(shape, dtype)


def call(kernel, outs, scratch=(), **options):
    return pl.pallas_call(
        kernel,
        out_shape=outs,
        scratch_shapes=list(scratch),
        compiler_params=pltpu.CompilerParams(vmem_limit_bytes=48 * 1024 * 1024),
        **options,
    )


def gather(copies):
    mine = lax.all_to_all(copies.reshape((-1,) + copies.shape[2:]), ("row", "col"), 0, 0, tiled=True)
    cols = lax.axis_size("col")
    return mine, lax.ppermute(mine, "col", [(col, col ^ 1) for col in range(cols)])


def local(positions, noise):
    vecs, _, beads = noise.shape
    devices = lax.axis_size("row") * lax.axis_size("col")
    total = beads * devices // 2
    size = 3.0 * beads * devices
    keep = 2 * 2 * 2 * 6 * beads * total <= KEPT
    width = total if keep else min(total, CHUNK)
    block = array(vecs, 4 * beads)
    copies = array(devices // 2, 2, vecs, 2 * beads)
    products = array(4 * vecs, 6 * beads)
    small_gram, large_gram = array(4 * vecs, 4 * vecs), array(8 * vecs, 8 * vecs)
    wide, held_wide = array(4 * vecs, total), pltpu.VMEM((4 * vecs, total), F32)
    kept = [array(6 * beads, width, dtype=BF16)] * 2 if keep else []
    held = [] if keep else [pltpu.VMEM((6 * beads, width), BF16)] * 2

    rows = noise.transpose(1, 0, 2).reshape(3 * vecs, beads)
    rows = jnp.concatenate([rows, jnp.pad(positions, ((0, vecs - 3), (0, 0)))], axis=0)
    own, own_copies = call(pack_kernel, [block, copies])(rows)
    one, two = gather(own_copies)
    partial, gram, one_wide, *one_tensor = call(
        functools.partial(first_stage, False), [products, small_gram, wide] + kept, held
    )(own, one)
    image, images, gram, two_wide, *two_tensor = call(
        functools.partial(first_stage, True), [block, copies, small_gram, wide] + kept, held
    )(own, two, partial, gram)
    one, two = gather(images)
    small, own_first, own_moved = call(
        functools.partial(start_kernel, size), [array(2, vecs, vecs), block, block]
    )(image, own, gram)
    partial, gram = call(
        functools.partial(second_stage, size, False, not keep), [products, large_gram], held + [held_wide]
    )(own, one_wide, *one_tensor, one)
    vectors, shifted, both, partials = call(
        functools.partial(second_stage, size, True, not keep),
        [block, block, array(2, vecs, vecs), array(devices, 1, vecs * vecs)],
        held + [held_wide],
    )(own, two_wide, *two_tensor, two, partial, gram, image, own_first, own_moved, small)
    partials = lax.all_to_all(partials, ("row", "col"), 0, 0, tiled=True)
    basis, residual, coefficients = call(
        functools.partial(last_kernel, size),
        [array(3, vecs, beads), array(3, vecs, beads), array(3, vecs, vecs)],
    )(vectors, shifted, both, partials)
    return (basis.transpose(1, 0, 2), residual.transpose(1, 0, 2), coefficients)


def solution(mesh):
    return jax.shard_map(
        local,
        mesh=mesh,
        in_specs=(P(None, ("row", "col")), P(None, None, ("row", "col"))),
        out_specs=(P(None, None, ("row", "col")), P(None, None, ("row", "col")), P()),
        check_vma=False,
    )
```

```python
import functools

import jax
import jax.numpy as jnp
from jax import lax
from jax.experimental import pallas as pl
from jax.experimental.pallas import tpu as pltpu
from jax.sharding import PartitionSpec as P

CHUNK = 1024
KEPT = 8 * 1024 * 1024
F32 = jnp.float32
BF16 = jnp.bfloat16


def halves(block):
    beads = block.shape[1] // 4
    middle = beads // 2
    parts = [block[:, part * beads : (part + 1) * beads] for part in range(4)]
    first = jnp.concatenate([part[:, :middle] for part in parts], axis=1)
    second = jnp.concatenate([part[:, middle:] for part in parts], axis=1)
    return first, second


def copy_halves(block, copies):
    for core, half in enumerate(halves(block)):
        copies[:, core] = jnp.broadcast_to(half[None], (copies.shape[0],) + half.shape)


def pack_kernel(rows, block, copies):
    vecs = block.shape[0]
    flat = jnp.concatenate([rows[part * vecs : (part + 1) * vecs] for part in range(4)], axis=1)
    block[...] = flat
    copy_halves(flat, copies)


def split_two(value):
    high = value.astype(BF16)
    return high, (value - high.astype(F32)).astype(BF16)


def matmul_nt(left, right, precision=None):
    return lax.dot_general(
        left, right, (((1,), (1,)), ((), ())), precision=precision, preferred_element_type=F32
    )


def small_matmul(left, right):
    total = left[:, 0:1] * right[0:1, :]
    for k in range(1, left.shape[1]):
        total = total + left[:, k : k + 1] * right[k : k + 1, :]
    return total


def unpack(blocks, wide):
    count, vecs, lanes = blocks.shape
    width = lanes // 4
    for at in range(0, count, 4):
        four = [blocks[at + index] for index in range(4)]
        for part in range(4):
            wide[part * vecs : (part + 1) * vecs, pl.ds(at * width, 4 * width)] = jnp.concatenate(
                [block[:, part * width : (part + 1) * width] for block in four], axis=1
            )


def target_columns(own):
    beads = own.shape[1] // 4
    targets = own[:, 3 * beads :].T
    return [jnp.broadcast_to(targets[:, axis : axis + 1], (beads, 128)) for axis in range(3)]


def fill_tensor(columns, wide, start, high, low, at):
    beads = columns[0].shape[0]
    block = 32 if beads % 32 == 0 else beads
    sources = [wide[24 + axis : 25 + axis, pl.ds(start, 128)] for axis in range(3)]
    to = pl.ds(at, 128)
    for row in range(0, beads, block):
        moved = [columns[axis][row : row + block] - sources[axis] for axis in range(3)]
        square = moved[0] * moved[0] + moved[1] * moved[1] + moved[2] * moved[2]
        square = jnp.maximum(square, 1e-12)
        inverse = lax.rsqrt(square)
        inverse_sq = inverse * inverse
        near = square < 4.0
        iso = inverse * jnp.where(near, square * (inverse - 9.0 / 32.0), 0.75 + 0.5 * inverse_sq)
        along = inverse * jnp.where(near, 3.0 / 32.0, inverse_sq * (0.75 - 1.5 * inverse_sq))
        scaled = [along * item for item in moved]
        parts = [
            iso + scaled[0] * moved[0],
            scaled[0] * moved[1],
            scaled[0] * moved[2],
            iso + scaled[1] * moved[1],
            scaled[1] * moved[2],
            iso + scaled[2] * moved[2],
        ]
        for part, value in enumerate(parts):
            upper, lower = split_two(value)
            rows = slice(part * beads + row, part * beads + row + block)
            high[rows, to] = upper
            low[rows, to] = lower


def apply_tensor(both, high, low, at, step):
    lanes = pl.ds(at, step)
    half = both.shape[0] // 2
    first = matmul_nt(both, high[:, lanes])
    return first[:half] + first[half:] + matmul_nt(both[:half], low[:, lanes])


def split_rows(*values):
    highs, lows = zip(*[split_two(value) for value in values])
    return jnp.concatenate(highs + lows, axis=0)


def inner(both):
    half = both.shape[0] // 2
    first = matmul_nt(both, both[:half])
    return first[:half] + first[half:] + matmul_nt(both[:half], both[half:])


def assemble(products):
    beads = products.shape[1] // 6

    def part(row, component):
        return products[8 * row : 8 * row + 8, component * beads : (component + 1) * beads]

    x = part(0, 0) + part(1, 1) + part(2, 2)
    y = part(0, 1) + part(1, 3) + part(2, 4)
    z = part(0, 2) + part(1, 4) + part(2, 5)
    return jnp.concatenate([x, y, z, jnp.zeros(x.shape, F32)], axis=1)


def block_sum(matrix, row, column):
    parts = [
        matrix[row + 8 * part : row + 8 * part + 8, column + 8 * part : column + 8 * part + 8]
        for part in range(3)
    ]
    return parts[0] + parts[1] + parts[2]


def filled_product(columns, source, wide, start, high, low, with_gram):
    width = high.shape[1]
    products = jnp.zeros((32, high.shape[0]), F32)
    for at in range(0, width, 256):
        step = min(256, width - at)
        for part in range(at, at + step, 128):
            fill_tensor(columns, source, pl.multiple_of(start + part, 128), high, low, part)
        both = split_rows(wide[:, pl.ds(pl.multiple_of(start + at, 128), step)])
        products = products + apply_tensor(both, high, low, at, step)
    if with_gram:
        both = split_rows(wide[:, pl.ds(pl.multiple_of(start, 128), width)])
        return products, inner(both)
    return (products,)


def all_chunks(total, width, chunk):
    if total == width:
        return chunk(0)
    body = lambda index, sums: tuple(a + b for a, b in zip(sums, chunk(index * width)))
    return lax.fori_loop(1, total // width, body, chunk(0))


def first_product(own, wide, high, low):
    columns = target_columns(own)
    return all_chunks(
        wide.shape[1], high.shape[1], lambda start: filled_product(columns, wide, wide, start, high, low, True)
    )


def first_stage(last, own, blocks, *refs):
    refs = list(refs)
    if last:
        before, refs = refs[:2], refs[2:]
        image, copies = refs[:2]
    else:
        products_out, copies = refs[0], None
    gram, wide, high, low = refs[2:6] if last else refs[1:5]
    unpack(blocks, wide)
    products, grams = first_product(own[...], wide, high, low)
    if not last:
        products_out[...], gram[...] = products, grams
        return
    gram[...] = grams + before[1][...]
    block = assemble(products + before[0][...])
    image[...] = block
    copy_halves(block, copies)


def cholesky(matrix):
    size = matrix.shape[0]
    shape = (size, size)
    rows = lax.broadcasted_iota(jnp.int32, shape, 0)
    cols = lax.broadcasted_iota(jnp.int32, shape, 1)
    entry = {}
    for j in range(size):
        column = jnp.broadcast_to(matrix[:, j : j + 1], shape)
        for i in range(j, size):
            entry[i, j] = jnp.broadcast_to(column[i : i + 1, :], shape)
    factor_t = jnp.zeros(shape, F32)
    inverse = jnp.zeros(shape, F32)
    inverse_rows = []
    for j in range(size):
        scale = lax.rsqrt(entry[j, j])
        lower_row = entry[j, j] * scale
        entry[j, j] = scale
        for i in range(j + 1, size):
            entry[i, j] = entry[i, j] * scale
        for i in range(j + 1, size):
            for k in range(j + 1, i + 1):
                entry[i, k] = entry[i, k] - entry[i, j] * entry[k, j]
        lower_row = jnp.where(cols == j, lower_row, 0.0)
        for i in range(j + 1, size):
            lower_row = jnp.where(cols == i, entry[i, j], lower_row)
        factor_t = jnp.where(rows == j, lower_row, factor_t)
        row = jnp.where(cols == j, 1.0, 0.0)
        for k in range(j):
            row = row - entry[j, k] * inverse_rows[k]
        row = row * scale
        inverse_rows.append(row)
        inverse = jnp.where(rows == j, row, inverse)
    return factor_t, inverse


def start_kernel(size, image, own, gram, small, own_first, own_moved):
    _, inverse = cholesky(block_sum(gram[...], 0, 0) / size)
    own_first[...] = small_matmul(inverse, own[...])
    own_moved[...] = small_matmul(inverse, image[...])
    small[0] = inverse
    small[1] = inverse.T


def second_product(fill, own, wide, wide_image, high, low):
    grams = inner(split_rows(wide[...], wide_image[...]))
    if not fill:
        return apply_tensor(split_rows(wide_image[...]), high, low, 0, high.shape[1]), grams
    columns = target_columns(own)
    (products,) = all_chunks(
        wide.shape[1],
        high.shape[1],
        lambda start: filled_product(columns, wide, wide_image, start, high, low, False),
    )
    return products, grams


def second_stage(size, last, fill, own, wide, *refs):
    refs = list(refs)
    if not fill:
        (high, low), refs = refs[:2], refs[2:]
    images, refs = refs[0], refs[1:]
    if last:
        (before, before_gram, own_image, own_first, own_moved, small), refs = refs[:6], refs[6:]
    outs, refs = refs[: 4 if last else 2], refs[4 if last else 2 :]
    if fill:
        (high, low), refs = refs[:2], refs[2:]
    wide_image = refs[0]
    beads = own.shape[1] // 4
    unpack(images, wide_image)
    products, grams = second_product(fill, own[...], wide, wide_image, high, low)
    if not last:
        outs[0][...], outs[1][...] = products, grams
        return
    vectors_out, shifted, coefficients, partials = outs
    products = products + before[...]
    grams = (grams + before_gram[...]) / size
    inverse_zero, inverse_zero_t = small[0], small[1]
    cross_t = small_matmul(inverse_zero, block_sum(grams, 0, 32))
    cross = small_matmul(block_sum(grams, 32, 0), inverse_zero_t)
    factor_t, inverse = cholesky(block_sum(grams, 32, 32) - small_matmul(cross, cross_t))
    alpha = small_matmul(cross_t, inverse_zero_t)
    factor_one_t = small_matmul(factor_t, inverse_zero_t)
    first, moved = own_first[...], own_moved[...]
    vectors = small_matmul(inverse, own_image[...] - small_matmul(cross, first))
    shift = small_matmul(inverse, assemble(products) - small_matmul(cross, moved))
    shift = shift - small_matmul(factor_one_t, first)
    valid = lax.broadcasted_iota(jnp.int32, vectors.shape, 1) < 3 * beads
    vectors = jnp.where(valid, vectors, 0.0)
    shift = jnp.where(valid, shift, 0.0)
    (vector_high, vector_low), (shift_high, shift_low) = split_two(vectors), split_two(shift)
    partial = matmul_nt(vector_high, shift_high) + (
        matmul_nt(vector_high, shift_low) + matmul_nt(vector_low, shift_high)
    )
    line = jnp.concatenate([partial[row : row + 1] for row in range(8)], axis=1)
    partials[...] = jnp.broadcast_to(line[None], partials.shape)
    vectors_out[...] = vectors
    shifted[...] = shift
    coefficients[0] = alpha
    coefficients[1] = factor_one_t.T


def last_kernel(size, vectors, shifted, both, partials, basis, residual, coefficients):
    beads = basis.shape[2]
    width = partials.shape[2]
    total = jnp.sum(partials[...], axis=0) / size
    spread = jnp.broadcast_to(total, (8, width))
    rows = lax.broadcasted_iota(jnp.int32, spread.shape, 0)
    cols = lax.broadcasted_iota(jnp.int32, spread.shape, 1)
    block = vectors[...]
    left = shifted[...]
    transposed = jnp.where(cols % 8 == rows, spread, 0.0)
    for k in range(8):
        column = jnp.sum(jnp.where(cols // 8 == k, transposed, 0.0), axis=1, keepdims=True)
        left = left - column * block[k : k + 1, :]
    coefficients[0:2] = both[...]
    for k in range(8):
        coefficients[2, k : k + 1, :] = total[:, 8 * k : 8 * k + 8]
    for part in range(3):
        basis[part] = block[:, part * beads : (part + 1) * beads]
        residual[part] = left[:, part * beads : (part + 1) * beads]


def array(*shape, dtype=F32):
    return jax.ShapeDtypeStruct(shape, dtype)


def call(kernel, outs, scratch=(), **options):
    return pl.pallas_call(
        kernel,
        out_shape=outs,
        scratch_shapes=list(scratch),
        compiler_params=pltpu.CompilerParams(vmem_limit_bytes=48 * 1024 * 1024),
        **options,
    )


def gather(copies):
    mine = lax.all_to_all(copies.reshape((-1,) + copies.shape[2:]), ("row", "col"), 0, 0, tiled=True)
    cols = lax.axis_size("col")
    return mine, lax.ppermute(mine, "col", [(col, col ^ 1) for col in range(cols)])


def local(positions, noise):
    vecs, _, beads = noise.shape
    devices = lax.axis_size("row") * lax.axis_size("col")
    total = beads * devices // 2
    size = 3.0 * beads * devices
    keep = 2 * 2 * 2 * 6 * beads * total <= KEPT
    width = total if keep else min(total, CHUNK)
    block = array(vecs, 4 * beads)
    copies = array(devices // 2, 2, vecs, 2 * beads)
    products = array(4 * vecs, 6 * beads)
    small_gram, large_gram = array(4 * vecs, 4 * vecs), array(8 * vecs, 8 * vecs)
    wide, held_wide = array(4 * vecs, total), pltpu.VMEM((4 * vecs, total), F32)
    kept = [array(6 * beads, width, dtype=BF16)] * 2 if keep else []
    held = [] if keep else [pltpu.VMEM((6 * beads, width), BF16)] * 2

    rows = noise.transpose(1, 0, 2).reshape(3 * vecs, beads)
    rows = jnp.concatenate([rows, jnp.pad(positions, ((0, vecs - 3), (0, 0)))], axis=0)
    own, own_copies = call(pack_kernel, [block, copies])(rows)
    one, two = gather(own_copies)
    partial, gram, one_wide, *one_tensor = call(
        functools.partial(first_stage, False), [products, small_gram, wide] + kept, held
    )(own, one)
    image, images, gram, two_wide, *two_tensor = call(
        functools.partial(first_stage, True), [block, copies, small_gram, wide] + kept, held
    )(own, two, partial, gram)
    one, two = gather(images)
    small, own_first, own_moved = call(
        functools.partial(start_kernel, size), [array(2, vecs, vecs), block, block]
    )(image, own, gram)
    partial, gram = call(
        functools.partial(second_stage, size, False, not keep), [products, large_gram], held + [held_wide]
    )(own, one_wide, *one_tensor, one)
    vectors, shifted, both, partials = call(
        functools.partial(second_stage, size, True, not keep),
        [block, block, array(2, vecs, vecs), array(devices, 1, vecs * vecs)],
        held + [held_wide],
    )(own, two_wide, *two_tensor, two, partial, gram, image, own_first, own_moved, small)
    partials = lax.all_to_all(partials, ("row", "col"), 0, 0, tiled=True)
    basis, residual, coefficients = call(
        functools.partial(last_kernel, size),
        [array(3, vecs, beads), array(3, vecs, beads), array(3, vecs, vecs)],
    )(vectors, shifted, both, partials)
    return (basis.transpose(1, 0, 2), residual.transpose(1, 0, 2), coefficients)


def solution(mesh):
    return jax.shard_map(
        local,
        mesh=mesh,
        in_specs=(P(None, ("row", "col")), P(None, None, ("row", "col"))),
        out_specs=(P(None, None, ("row", "col")), P(None, None, ("row", "col")), P()),
        check_vma=False,
    )
```

```python
import functools

import jax
import jax.numpy as jnp
from jax import lax
from jax.experimental import pallas as pl
from jax.experimental.pallas import tpu as pltpu
from jax.sharding import PartitionSpec as P

CHUNK = 1024
KEPT = 8 * 1024 * 1024
F32 = jnp.float32
BF16 = jnp.bfloat16


def copy_halves(block, copies, last=None):
    beads = block.shape[1] // 4
    middle = beads // 2
    for core in range(2):
        parts = [block[:, part * beads + core * middle : part * beads + (core + 1) * middle] for part in range(4)]
        if last is not None:
            parts[3] = last
        half = jnp.concatenate(parts, axis=1)
        copies[:, core] = jnp.broadcast_to(half[None], (copies.shape[0],) + half.shape)


def pack_kernel(rows, block, copies):
    vecs = block.shape[0]
    flat = jnp.concatenate([rows[part * vecs : (part + 1) * vecs] for part in range(4)], axis=1)
    block[...] = flat
    copy_halves(flat, copies)


def split_two(value):
    high = value.astype(BF16)
    return high, (value - high.astype(F32)).astype(BF16)


def matmul_nt(left, right, precision=None):
    return lax.dot_general(
        left, right, (((1,), (1,)), ((), ())), precision=precision, preferred_element_type=F32
    )


def small_matmul(left, right):
    total = left[:, 0:1] * right[0:1, :]
    for k in range(1, left.shape[1]):
        total = total + left[:, k : k + 1] * right[k : k + 1, :]
    return total


def unpack(blocks, wide):
    count, vecs, lanes = blocks.shape
    width = lanes // 4
    for at in range(0, count, 4):
        four = [blocks[at + index] for index in range(4)]
        for part in range(4):
            wide[part * vecs : (part + 1) * vecs, pl.ds(at * width, 4 * width)] = jnp.concatenate(
                [block[:, part * width : (part + 1) * width] for block in four], axis=1
            )


def target_columns(own):
    beads = own.shape[1] // 4
    targets = own[:, 3 * beads :].T
    return [jnp.broadcast_to(targets[:, axis : axis + 1], (beads, 128)) for axis in range(3)]


def fill_tensor(columns, wide, start, high, low, at):
    beads = columns[0].shape[0]
    block = 32 if beads % 32 == 0 else beads
    sources = [wide[24 + axis : 25 + axis, pl.ds(start, 128)] for axis in range(3)]
    to = pl.ds(at, 128)
    for row in range(0, beads, block):
        moved = [columns[axis][row : row + block] - sources[axis] for axis in range(3)]
        square = moved[0] * moved[0] + moved[1] * moved[1] + moved[2] * moved[2]
        square = jnp.maximum(square, 1e-12)
        inverse = lax.rsqrt(square)
        inverse_sq = inverse * inverse
        near = square < 4.0
        iso = inverse * jnp.where(near, square * (inverse - 9.0 / 32.0), 0.75 + 0.5 * inverse_sq)
        along = inverse * jnp.where(near, 3.0 / 32.0, inverse_sq * (0.75 - 1.5 * inverse_sq))
        scaled = [along * item for item in moved]
        parts = [
            iso + scaled[0] * moved[0],
            scaled[0] * moved[1],
            scaled[0] * moved[2],
            iso + scaled[1] * moved[1],
            scaled[1] * moved[2],
            iso + scaled[2] * moved[2],
        ]
        for part, value in enumerate(parts):
            upper, lower = split_two(value)
            rows = slice(part * beads + row, part * beads + row + block)
            high[rows, to] = upper
            low[rows, to] = lower


def apply_tensor(both, high, low, at, step):
    lanes = pl.ds(at, step)
    half = both.shape[0] // 2
    first = matmul_nt(both, high[:, lanes])
    return first[:half] + first[half:] + matmul_nt(both[:half], low[:, lanes])


def split_rows(*values):
    highs, lows = zip(*[split_two(value) for value in values])
    return jnp.concatenate(highs + lows, axis=0)


def inner(both):
    half = both.shape[0] // 2
    first = matmul_nt(both, both[:half])
    return first[:half] + first[half:] + matmul_nt(both[:half], both[half:])


def assemble(products):
    beads = products.shape[1] // 6

    def part(row, component):
        return products[8 * row : 8 * row + 8, component * beads : (component + 1) * beads]

    x = part(0, 0) + part(1, 1) + part(2, 2)
    y = part(0, 1) + part(1, 3) + part(2, 4)
    z = part(0, 2) + part(1, 4) + part(2, 5)
    return jnp.concatenate([x, y, z, jnp.zeros(x.shape, F32)], axis=1)


def filled_product(columns, source, wide, start, high, low):
    width = high.shape[1]
    products = jnp.zeros((32, high.shape[0]), F32)
    for at in range(0, width, 256):
        step = min(256, width - at)
        for part in range(at, at + step, 128):
            fill_tensor(columns, source, pl.multiple_of(start + part, 128), high, low, part)
        both = split_rows(wide[:, pl.ds(pl.multiple_of(start + at, 128), step)])
        products = products + apply_tensor(both, high, low, at, step)
    return products


def all_filled(own, source, wide, high, low):
    columns = target_columns(own)
    width = high.shape[1]
    chunk = lambda start: filled_product(columns, source, wide, start, high, low)
    if wide.shape[1] == width:
        return chunk(0)
    body = lambda index, total: total + chunk(index * width)
    return lax.fori_loop(1, wide.shape[1] // width, body, chunk(0))


def without_positions(block):
    lanes = lax.broadcasted_iota(jnp.int32, block.shape, 1)
    return jnp.where(lanes < block.shape[1] // 4 * 3, block, 0.0)


def first_stage(last, own, blocks, *refs):
    refs = list(refs)
    if last:
        before, image, copies, wide, high, low = refs
    else:
        out, wide, high, low = refs
    unpack(blocks, wide)
    products = all_filled(own[...], wide, wide, high, low)
    if not last:
        out[...] = products
        return
    block = assemble(products + before[...])
    image[...] = block
    sums = inner(split_rows(without_positions(own[...]), block))
    empty = jnp.zeros((8, block.shape[1] // 8 - 24), F32)
    copy_halves(block, copies, jnp.concatenate([sums[:8], sums[8:, 8:], empty], axis=1))


def cholesky(matrix):
    size = matrix.shape[0]
    shape = (size, size)
    rows = lax.broadcasted_iota(jnp.int32, shape, 0)
    cols = lax.broadcasted_iota(jnp.int32, shape, 1)
    entry = {}
    for j in range(size):
        column = jnp.broadcast_to(matrix[:, j : j + 1], shape)
        for i in range(j, size):
            entry[i, j] = jnp.broadcast_to(column[i : i + 1, :], shape)
    factor_t = jnp.zeros(shape, F32)
    inverse = jnp.zeros(shape, F32)
    inverse_rows = []
    for j in range(size):
        scale = lax.rsqrt(entry[j, j])
        lower_row = entry[j, j] * scale
        entry[j, j] = scale
        for i in range(j + 1, size):
            entry[i, j] = entry[i, j] * scale
        for i in range(j + 1, size):
            for k in range(j + 1, i + 1):
                entry[i, k] = entry[i, k] - entry[i, j] * entry[k, j]
        lower_row = jnp.where(cols == j, lower_row, 0.0)
        for i in range(j + 1, size):
            lower_row = jnp.where(cols == i, entry[i, j], lower_row)
        factor_t = jnp.where(rows == j, lower_row, factor_t)
        row = jnp.where(cols == j, 1.0, 0.0)
        for k in range(j):
            row = row - entry[j, k] * inverse_rows[k]
        row = row * scale
        inverse_rows.append(row)
        inverse = jnp.where(rows == j, row, inverse)
    return factor_t, inverse


def second_product(fill, own, wide, wide_image, high, low):
    if fill:
        return all_filled(own, wide, wide_image, high, low)
    return apply_tensor(split_rows(wide_image[...]), high, low, 0, high.shape[1])


def third_stage(size, fill, own, wide, *refs):
    refs = list(refs)
    if not fill:
        (high, low), refs = refs[:2], refs[2:]
    images, own_image, products, vectors, known, small, coefficients = refs[:7]
    if fill:
        high, low = refs[7:9]
    wide_image = refs[-1]
    unpack(images, wide_image)
    products[...] = second_product(fill, own[...], wide, wide_image, high, low)
    sums = wide_image[24:, :128]
    for at in range(128, wide_image.shape[1], 128):
        sums = sums + wide_image[24:, at : at + 128]
    width = own.shape[1] // 8
    sums = sum(sums[:, at : at + width] for at in range(width, 128, width)) + sums[:, :width]
    sums = sums / size
    _, inverse_zero = cholesky(sums[:, :8])
    inverse_zero_t = inverse_zero.T
    cross_t = small_matmul(inverse_zero, sums[:, 8:16])
    cross = cross_t.T
    factor_t, inverse = cholesky(sums[:, 16:24] - small_matmul(cross, cross_t))
    factor_one_t = small_matmul(factor_t, inverse_zero_t)
    first = small_matmul(inverse_zero, without_positions(own[...]))
    moved = small_matmul(inverse_zero, own_image[...])
    vectors[...] = small_matmul(inverse, own_image[...] - small_matmul(cross, first))
    known[...] = small_matmul(inverse, small_matmul(cross, moved)) + small_matmul(factor_one_t, first)
    small[...] = inverse
    coefficients[0] = small_matmul(cross_t, inverse_zero_t)
    coefficients[1] = factor_one_t.T


def fourth_stage(fill, own, wide, *refs):
    refs = list(refs)
    if not fill:
        (high, low), refs = refs[:2], refs[2:]
    images, before, vectors_in, known, small, shifted, partials = refs[:7]
    if fill:
        high, low = refs[7:9]
    wide_image = refs[-1]
    unpack(images, wide_image)
    products = second_product(fill, own[...], wide, wide_image, high, low) + before[...]
    vectors = vectors_in[...]
    shift = small_matmul(small[...], assemble(products)) - known[...]
    shifted[...] = shift
    (vector_high, vector_low), (shift_high, shift_low) = split_two(vectors), split_two(shift)
    partial = matmul_nt(vector_high, shift_high) + (
        matmul_nt(vector_high, shift_low) + matmul_nt(vector_low, shift_high)
    )
    line = jnp.concatenate([partial[row : row + 1] for row in range(8)], axis=1)
    partials[...] = jnp.broadcast_to(line[None], partials.shape)


def last_kernel(size, vectors, shifted, both, partials, basis, residual, coefficients):
    beads = basis.shape[2]
    width = partials.shape[2]
    total = jnp.sum(partials[...], axis=0) / size
    spread = jnp.broadcast_to(total, (8, width))
    rows = lax.broadcasted_iota(jnp.int32, spread.shape, 0)
    cols = lax.broadcasted_iota(jnp.int32, spread.shape, 1)
    block = vectors[...]
    left = shifted[...]
    transposed = jnp.where(cols % 8 == rows, spread, 0.0)
    for k in range(8):
        column = jnp.sum(jnp.where(cols // 8 == k, transposed, 0.0), axis=1, keepdims=True)
        left = left - column * block[k : k + 1, :]
    coefficients[0:2] = both[...]
    for k in range(8):
        coefficients[2, k : k + 1, :] = total[:, 8 * k : 8 * k + 8]
    for part in range(3):
        basis[part] = block[:, part * beads : (part + 1) * beads]
        residual[part] = left[:, part * beads : (part + 1) * beads]


def array(*shape, dtype=F32):
    return jax.ShapeDtypeStruct(shape, dtype)


def call(kernel, outs, scratch=(), **options):
    return pl.pallas_call(
        kernel,
        out_shape=outs,
        scratch_shapes=list(scratch),
        compiler_params=pltpu.CompilerParams(vmem_limit_bytes=48 * 1024 * 1024),
        **options,
    )


def gather(copies):
    mine = lax.all_to_all(copies.reshape((-1,) + copies.shape[2:]), ("row", "col"), 0, 0, tiled=True)
    cols = lax.axis_size("col")
    return mine, lax.ppermute(mine, "col", [(col, col ^ 1) for col in range(cols)])


def local(positions, noise):
    vecs, _, beads = noise.shape
    devices = lax.axis_size("row") * lax.axis_size("col")
    total = beads * devices // 2
    size = 3.0 * beads * devices
    keep = 2 * 2 * 2 * 6 * beads * total <= KEPT
    width = total if keep else min(total, CHUNK)
    block = array(vecs, 4 * beads)
    copies = array(devices // 2, 2, vecs, 2 * beads)
    products = array(4 * vecs, 6 * beads)
    wide, held_wide = array(4 * vecs, total), pltpu.VMEM((4 * vecs, total), F32)
    kept = [array(6 * beads, width, dtype=BF16)] * 2 if keep else []
    held = [] if keep else [pltpu.VMEM((6 * beads, width), BF16)] * 2

    rows = noise.transpose(1, 0, 2).reshape(3 * vecs, beads)
    rows = jnp.concatenate([rows, jnp.pad(positions, ((0, vecs - 3), (0, 0)))], axis=0)
    own, own_copies = call(pack_kernel, [block, copies])(rows)
    one, two = gather(own_copies)
    partial, one_wide, *one_tensor = call(
        functools.partial(first_stage, False), [products, wide] + kept, held
    )(own, one)
    image, images, two_wide, *two_tensor = call(
        functools.partial(first_stage, True), [block, copies, wide] + kept, held
    )(own, two, partial)
    one, two = gather(images)
    partial, vectors, known, small, both = call(
        functools.partial(third_stage, size, not keep),
        [products, block, block, array(vecs, vecs), array(2, vecs, vecs)],
        held + [held_wide],
    )(own, one_wide, *one_tensor, one, image)
    shifted, partials = call(
        functools.partial(fourth_stage, not keep), [block, array(devices, 1, vecs * vecs)], held + [held_wide]
    )(own, two_wide, *two_tensor, two, partial, vectors, known, small)
    partials = lax.all_to_all(partials, ("row", "col"), 0, 0, tiled=True)
    basis, residual, coefficients = call(
        functools.partial(last_kernel, size),
        [array(3, vecs, beads), array(3, vecs, beads), array(3, vecs, vecs)],
    )(vectors, shifted, both, partials)
    return (basis.transpose(1, 0, 2), residual.transpose(1, 0, 2), coefficients)


def solution(mesh):
    return jax.shard_map(
        local,
        mesh=mesh,
        in_specs=(P(None, ("row", "col")), P(None, None, ("row", "col"))),
        out_specs=(P(None, None, ("row", "col")), P(None, None, ("row", "col")), P()),
        check_vma=False,
    )
```

```python
import functools

import jax
import jax.numpy as jnp
from jax import lax
from jax.experimental import pallas as pl
from jax.experimental.pallas import tpu as pltpu
from jax.sharding import PartitionSpec as P

CHUNK = 1024
KEPT = 8 * 1024 * 1024
F32 = jnp.float32
BF16 = jnp.bfloat16


def copy_halves(block, copies, last=None):
    beads = block.shape[1] // 4
    middle = beads // 2
    for core in range(2):
        parts = [block[:, part * beads + core * middle : part * beads + (core + 1) * middle] for part in range(4)]
        if last is not None:
            parts[3] = last
        half = jnp.concatenate(parts, axis=1)
        copies[:, core] = jnp.broadcast_to(half[None], (copies.shape[0],) + half.shape)


def pack_kernel(rows, block, copies):
    vecs = block.shape[0]
    flat = jnp.concatenate([rows[part * vecs : (part + 1) * vecs] for part in range(4)], axis=1)
    block[...] = flat
    copy_halves(flat, copies)


def split_two(value):
    high = value.astype(BF16)
    return high, (value - high.astype(F32)).astype(BF16)


def matmul_nt(left, right, precision=None):
    return lax.dot_general(
        left, right, (((1,), (1,)), ((), ())), precision=precision, preferred_element_type=F32
    )


def small_matmul(left, right):
    total = left[:, 0:1] * right[0:1, :]
    for k in range(1, left.shape[1]):
        total = total + left[:, k : k + 1] * right[k : k + 1, :]
    return total


def unpack(blocks, wide):
    count, vecs, lanes = blocks.shape
    width = lanes // 4
    for at in range(0, count, 4):
        four = [blocks[at + index] for index in range(4)]
        for part in range(4):
            wide[part * vecs : (part + 1) * vecs, pl.ds(at * width, 4 * width)] = jnp.concatenate(
                [block[:, part * width : (part + 1) * width] for block in four], axis=1
            )


def target_columns(own):
    beads = own.shape[1] // 4
    targets = own[:, 3 * beads :].T
    return [jnp.broadcast_to(targets[:, axis : axis + 1], (beads, 128)) for axis in range(3)]


def fill_tensor(columns, wide, start, high, low, at):
    beads = columns[0].shape[0]
    block = 32 if beads % 32 == 0 else beads
    sources = [wide[24 + axis : 25 + axis, pl.ds(start, 128)] for axis in range(3)]
    to = pl.ds(at, 128)
    for row in range(0, beads, block):
        moved = [columns[axis][row : row + block] - sources[axis] for axis in range(3)]
        square = moved[0] * moved[0] + moved[1] * moved[1] + moved[2] * moved[2]
        square = jnp.maximum(square, 1e-12)
        inverse = lax.rsqrt(square)
        inverse_sq = inverse * inverse
        near = square < 4.0
        iso = inverse * jnp.where(near, square * (inverse - 9.0 / 32.0), 0.75 + 0.5 * inverse_sq)
        along = inverse * jnp.where(near, 3.0 / 32.0, inverse_sq * (0.75 - 1.5 * inverse_sq))
        scaled = [along * item for item in moved]
        parts = [
            iso + scaled[0] * moved[0],
            scaled[0] * moved[1],
            scaled[0] * moved[2],
            iso + scaled[1] * moved[1],
            scaled[1] * moved[2],
            iso + scaled[2] * moved[2],
        ]
        for part, value in enumerate(parts):
            upper, lower = split_two(value)
            rows = slice(part * beads + row, part * beads + row + block)
            high[rows, to] = upper
            low[rows, to] = lower


def apply_tensor(both, high, low, at, step):
    lanes = pl.ds(at, step)
    half = both.shape[0] // 2
    first = matmul_nt(both, high[:, lanes])
    return first[:half] + first[half:] + matmul_nt(both[:half], low[:, lanes])


def split_rows(*values):
    highs, lows = zip(*[split_two(value) for value in values])
    return jnp.concatenate(highs + lows, axis=0)


def inner(both):
    half = both.shape[0] // 2
    first = matmul_nt(both, both[:half])
    return first[:half] + first[half:] + matmul_nt(both[:half], both[half:])


def assemble(products):
    beads = products.shape[1] // 6

    def part(row, component):
        return products[8 * row : 8 * row + 8, component * beads : (component + 1) * beads]

    x = part(0, 0) + part(1, 1) + part(2, 2)
    y = part(0, 1) + part(1, 3) + part(2, 4)
    z = part(0, 2) + part(1, 4) + part(2, 5)
    return jnp.concatenate([x, y, z, jnp.zeros(x.shape, F32)], axis=1)


def filled_product(columns, source, wide, start, high, low):
    width = high.shape[1]
    products = jnp.zeros((32, high.shape[0]), F32)
    steps = [(at, min(256, width - at)) for at in range(0, width, 256)]
    vectors = [split_rows(wide[:, pl.ds(pl.multiple_of(start + at, 128), step)]) for at, step in steps]
    for index in range(len(steps) + 1):
        if index < len(steps):
            at, step = steps[index]
            for part in range(at, at + step, 128):
                fill_tensor(columns, source, pl.multiple_of(start + part, 128), high, low, part)
        if index > 0:
            products = products + apply_tensor(vectors[index - 1], high, low, *steps[index - 1])
    return products


def all_filled(own, source, wide, high, low):
    columns = target_columns(own)
    width = high.shape[1]
    chunk = lambda start: filled_product(columns, source, wide, start, high, low)
    if wide.shape[1] == width:
        return chunk(0)
    body = lambda index, total: total + chunk(index * width)
    return lax.fori_loop(1, wide.shape[1] // width, body, chunk(0))


def without_positions(block):
    lanes = lax.broadcasted_iota(jnp.int32, block.shape, 1)
    return jnp.where(lanes < block.shape[1] // 4 * 3, block, 0.0)


def first_stage(last, own, blocks, *refs):
    refs = list(refs)
    if last:
        before, image, copies, wide, high, low = refs
    else:
        out, wide, high, low = refs
    unpack(blocks, wide)
    products = all_filled(own[...], wide, wide, high, low)
    if not last:
        out[...] = products
        return
    block = assemble(products + before[...])
    image[...] = block
    sums = inner(split_rows(without_positions(own[...]), block))
    empty = jnp.zeros((8, block.shape[1] // 8 - 24), F32)
    copy_halves(block, copies, jnp.concatenate([sums[:8], sums[8:, 8:], empty], axis=1))


def cholesky(matrix):
    size = matrix.shape[0]
    shape = (size, size)
    rows = lax.broadcasted_iota(jnp.int32, shape, 0)
    cols = lax.broadcasted_iota(jnp.int32, shape, 1)
    entry = {}
    for j in range(size):
        column = jnp.broadcast_to(matrix[:, j : j + 1], shape)
        for i in range(j, size):
            entry[i, j] = jnp.broadcast_to(column[i : i + 1, :], shape)
    factor_t = jnp.zeros(shape, F32)
    inverse = jnp.zeros(shape, F32)
    inverse_rows = []
    for j in range(size):
        scale = lax.rsqrt(entry[j, j])
        lower_row = entry[j, j] * scale
        entry[j, j] = scale
        for i in range(j + 1, size):
            entry[i, j] = entry[i, j] * scale
        for i in range(j + 1, size):
            for k in range(j + 1, i + 1):
                entry[i, k] = entry[i, k] - entry[i, j] * entry[k, j]
        lower_row = jnp.where(cols == j, lower_row, 0.0)
        for i in range(j + 1, size):
            lower_row = jnp.where(cols == i, entry[i, j], lower_row)
        factor_t = jnp.where(rows == j, lower_row, factor_t)
        row = jnp.where(cols == j, 1.0, 0.0)
        for k in range(j):
            row = row - entry[j, k] * inverse_rows[k]
        row = row * scale
        inverse_rows.append(row)
        inverse = jnp.where(rows == j, row, inverse)
    return factor_t, inverse


def second_product(fill, own, wide, wide_image, high, low):
    if fill:
        return all_filled(own, wide, wide_image, high, low)
    return apply_tensor(split_rows(wide_image[...]), high, low, 0, high.shape[1])


def third_stage(size, fill, own, wide, *refs):
    refs = list(refs)
    if not fill:
        (high, low), refs = refs[:2], refs[2:]
    images, own_image, products, vectors, known, small, coefficients = refs[:7]
    if fill:
        high, low = refs[7:9]
    wide_image = refs[-1]
    unpack(images, wide_image)
    products[...] = second_product(fill, own[...], wide, wide_image, high, low)
    sums = wide_image[24:, :128]
    for at in range(128, wide_image.shape[1], 128):
        sums = sums + wide_image[24:, at : at + 128]
    width = own.shape[1] // 8
    sums = sum(sums[:, at : at + width] for at in range(width, 128, width)) + sums[:, :width]
    sums = sums / size
    _, inverse_zero = cholesky(sums[:, :8])
    inverse_zero_t = inverse_zero.T
    cross_t = small_matmul(inverse_zero, sums[:, 8:16])
    cross = cross_t.T
    factor_t, inverse = cholesky(sums[:, 16:24] - small_matmul(cross, cross_t))
    factor_one_t = small_matmul(factor_t, inverse_zero_t)
    first = small_matmul(inverse_zero, without_positions(own[...]))
    moved = small_matmul(inverse_zero, own_image[...])
    vectors[...] = small_matmul(inverse, own_image[...] - small_matmul(cross, first))
    known[...] = small_matmul(inverse, small_matmul(cross, moved)) + small_matmul(factor_one_t, first)
    small[...] = inverse
    coefficients[0] = small_matmul(cross_t, inverse_zero_t)
    coefficients[1] = factor_one_t.T


def fourth_stage(fill, own, wide, *refs):
    refs = list(refs)
    if not fill:
        (high, low), refs = refs[:2], refs[2:]
    images, before, vectors_in, known, small, shifted, partials = refs[:7]
    if fill:
        high, low = refs[7:9]
    wide_image = refs[-1]
    unpack(images, wide_image)
    products = second_product(fill, own[...], wide, wide_image, high, low) + before[...]
    vectors = vectors_in[...]
    shift = small_matmul(small[...], assemble(products)) - known[...]
    shifted[...] = shift
    (vector_high, vector_low), (shift_high, shift_low) = split_two(vectors), split_two(shift)
    partial = matmul_nt(vector_high, shift_high) + (
        matmul_nt(vector_high, shift_low) + matmul_nt(vector_low, shift_high)
    )
    line = jnp.concatenate([partial[row : row + 1] for row in range(8)], axis=1)
    partials[...] = jnp.broadcast_to(line[None], partials.shape)


def last_kernel(size, vectors, shifted, both, partials, basis, residual, coefficients):
    beads = basis.shape[2]
    width = partials.shape[2]
    total = jnp.sum(partials[...], axis=0) / size
    spread = jnp.broadcast_to(total, (8, width))
    rows = lax.broadcasted_iota(jnp.int32, spread.shape, 0)
    cols = lax.broadcasted_iota(jnp.int32, spread.shape, 1)
    block = vectors[...]
    left = shifted[...]
    transposed = jnp.where(cols % 8 == rows, spread, 0.0)
    for k in range(8):
        column = jnp.sum(jnp.where(cols // 8 == k, transposed, 0.0), axis=1, keepdims=True)
        left = left - column * block[k : k + 1, :]
    coefficients[0:2] = both[...]
    for k in range(8):
        coefficients[2, k : k + 1, :] = total[:, 8 * k : 8 * k + 8]
    for part in range(3):
        basis[part] = block[:, part * beads : (part + 1) * beads]
        residual[part] = left[:, part * beads : (part + 1) * beads]


def array(*shape, dtype=F32):
    return jax.ShapeDtypeStruct(shape, dtype)


def call(kernel, outs, scratch=(), **options):
    return pl.pallas_call(
        kernel,
        out_shape=outs,
        scratch_shapes=list(scratch),
        compiler_params=pltpu.CompilerParams(vmem_limit_bytes=48 * 1024 * 1024),
        **options,
    )


def gather(copies):
    mine = lax.all_to_all(copies.reshape((-1,) + copies.shape[2:]), ("row", "col"), 0, 0, tiled=True)
    cols = lax.axis_size("col")
    return mine, lax.ppermute(mine, "col", [(col, col ^ 1) for col in range(cols)])


def local(positions, noise):
    vecs, _, beads = noise.shape
    devices = lax.axis_size("row") * lax.axis_size("col")
    total = beads * devices // 2
    size = 3.0 * beads * devices
    keep = 2 * 2 * 2 * 6 * beads * total <= KEPT
    width = total if keep else min(total, CHUNK)
    block = array(vecs, 4 * beads)
    copies = array(devices // 2, 2, vecs, 2 * beads)
    products = array(4 * vecs, 6 * beads)
    wide, held_wide = array(4 * vecs, total), pltpu.VMEM((4 * vecs, total), F32)
    kept = [array(6 * beads, width, dtype=BF16)] * 2 if keep else []
    held = [] if keep else [pltpu.VMEM((6 * beads, width), BF16)] * 2

    rows = noise.transpose(1, 0, 2).reshape(3 * vecs, beads)
    rows = jnp.concatenate([rows, jnp.pad(positions, ((0, vecs - 3), (0, 0)))], axis=0)
    own, own_copies = call(pack_kernel, [block, copies])(rows)
    one, two = gather(own_copies)
    partial, one_wide, *one_tensor = call(
        functools.partial(first_stage, False), [products, wide] + kept, held
    )(own, one)
    image, images, two_wide, *two_tensor = call(
        functools.partial(first_stage, True), [block, copies, wide] + kept, held
    )(own, two, partial)
    one, two = gather(images)
    partial, vectors, known, small, both = call(
        functools.partial(third_stage, size, not keep),
        [products, block, block, array(vecs, vecs), array(2, vecs, vecs)],
        held + [held_wide],
    )(own, one_wide, *one_tensor, one, image)
    shifted, partials = call(
        functools.partial(fourth_stage, not keep), [block, array(devices, 1, vecs * vecs)], held + [held_wide]
    )(own, two_wide, *two_tensor, two, partial, vectors, known, small)
    partials = lax.all_to_all(partials, ("row", "col"), 0, 0, tiled=True)
    basis, residual, coefficients = call(
        functools.partial(last_kernel, size),
        [array(3, vecs, beads), array(3, vecs, beads), array(3, vecs, vecs)],
    )(vectors, shifted, both, partials)
    return (basis.transpose(1, 0, 2), residual.transpose(1, 0, 2), coefficients)


def solution(mesh):
    return jax.shard_map(
        local,
        mesh=mesh,
        in_specs=(P(None, ("row", "col")), P(None, None, ("row", "col"))),
        out_specs=(P(None, None, ("row", "col")), P(None, None, ("row", "col")), P()),
        check_vma=False,
    )
```

```python
import functools

import jax
import jax.numpy as jnp
from jax import lax
from jax.experimental import pallas as pl
from jax.experimental.pallas import tpu as pltpu
from jax.sharding import PartitionSpec as P

CHUNK = 1024
KEPT = 8 * 1024 * 1024
F32 = jnp.float32
BF16 = jnp.bfloat16


def copy_halves(block, copies, last=None):
    beads = block.shape[1] // 4
    middle = beads // 2
    for core in range(2):
        parts = [block[:, part * beads + core * middle : part * beads + (core + 1) * middle] for part in range(4)]
        if last is not None:
            parts[3] = last
        half = jnp.concatenate(parts, axis=1)
        copies[:, core] = jnp.broadcast_to(half[None], (copies.shape[0],) + half.shape)


def pack_kernel(rows, block, copies):
    vecs = block.shape[0]
    flat = jnp.concatenate([rows[part * vecs : (part + 1) * vecs] for part in range(4)], axis=1)
    block[...] = flat
    copy_halves(flat, copies)


def split_two(value):
    high = value.astype(BF16)
    return high, (value - high.astype(F32)).astype(BF16)


def matmul_nt(left, right, precision=None):
    return lax.dot_general(
        left, right, (((1,), (1,)), ((), ())), precision=precision, preferred_element_type=F32
    )


def small_matmul(left, right):
    total = left[:, 0:1] * right[0:1, :]
    for k in range(1, left.shape[1]):
        total = total + left[:, k : k + 1] * right[k : k + 1, :]
    return total


def unpack(blocks, wide):
    count, vecs, lanes = blocks.shape
    width = lanes // 4
    for at in range(0, count, 4):
        four = [blocks[at + index] for index in range(4)]
        for part in range(4):
            wide[part * vecs : (part + 1) * vecs, pl.ds(at * width, 4 * width)] = jnp.concatenate(
                [block[:, part * width : (part + 1) * width] for block in four], axis=1
            )


def target_columns(own):
    beads = own.shape[1] // 4
    targets = own[:, 3 * beads :].T
    return [jnp.broadcast_to(targets[:, axis : axis + 1], (beads, 128)) for axis in range(3)]


def fill_tensor(columns, wide, start, high, low, at):
    beads = columns[0].shape[0]
    block = 32 if beads % 32 == 0 else beads
    sources = [wide[24 + axis : 25 + axis, pl.ds(start, 128)] for axis in range(3)]
    to = pl.ds(at, 128)
    for row in range(0, beads, block):
        moved = [columns[axis][row : row + block] - sources[axis] for axis in range(3)]
        square = moved[0] * moved[0] + moved[1] * moved[1] + moved[2] * moved[2]
        square = jnp.maximum(square, 1e-12)
        inverse = lax.rsqrt(square)
        inverse_sq = inverse * inverse
        near = square < 4.0
        iso = inverse * jnp.where(near, square * (inverse - 9.0 / 32.0), 0.75 + 0.5 * inverse_sq)
        along = inverse * jnp.where(near, 3.0 / 32.0, inverse_sq * (0.75 - 1.5 * inverse_sq))
        scaled = [along * item for item in moved]
        parts = [
            iso + scaled[0] * moved[0],
            scaled[0] * moved[1],
            scaled[0] * moved[2],
            iso + scaled[1] * moved[1],
            scaled[1] * moved[2],
            iso + scaled[2] * moved[2],
        ]
        for part, value in enumerate(parts):
            upper, lower = split_two(value)
            rows = slice(part * beads + row, part * beads + row + block)
            high[rows, to] = upper
            low[rows, to] = lower


def apply_tensor(both, high, low, at, step):
    lanes = pl.ds(at, step)
    half = both.shape[0] // 2
    first = matmul_nt(both, high[:, lanes])
    return first[:half] + first[half:] + matmul_nt(both[:half], low[:, lanes])


def split_rows(*values):
    highs, lows = zip(*[split_two(value) for value in values])
    return jnp.concatenate(highs + lows, axis=0)


def inner(both):
    half = both.shape[0] // 2
    first = matmul_nt(both, both[:half])
    return first[:half] + first[half:] + matmul_nt(both[:half], both[half:])


def assemble(products):
    beads = products.shape[1] // 6

    def part(row, component):
        return products[8 * row : 8 * row + 8, component * beads : (component + 1) * beads]

    x = part(0, 0) + part(1, 1) + part(2, 2)
    y = part(0, 1) + part(1, 3) + part(2, 4)
    z = part(0, 2) + part(1, 4) + part(2, 5)
    return jnp.concatenate([x, y, z, jnp.zeros(x.shape, F32)], axis=1)


def filled_product(columns, source, wide, start, high, low):
    width = high.shape[1]
    products = jnp.zeros((32, high.shape[0]), F32)
    steps = [(at, min(256, width - at)) for at in range(0, width, 256)]
    vectors = [split_rows(wide[:, pl.ds(pl.multiple_of(start + at, 128), step)]) for at, step in steps]
    for index in range(len(steps) + 1):
        if index < len(steps):
            at, step = steps[index]
            for part in range(at, at + step, 128):
                fill_tensor(columns, source, pl.multiple_of(start + part, 128), high, low, part)
        if index > 0:
            products = products + apply_tensor(vectors[index - 1], high, low, *steps[index - 1])
    return products


def all_filled(own, source, wide, high, low):
    columns = target_columns(own)
    width = high.shape[1]
    chunk = lambda start: filled_product(columns, source, wide, start, high, low)
    if wide.shape[1] == width:
        return chunk(0)
    body = lambda index, total: total + chunk(index * width)
    return lax.fori_loop(1, wide.shape[1] // width, body, chunk(0))


def without_positions(block):
    lanes = lax.broadcasted_iota(jnp.int32, block.shape, 1)
    return jnp.where(lanes < block.shape[1] // 4 * 3, block, 0.0)


def first_stage(last, own, blocks, *refs):
    refs = list(refs)
    if last:
        before, image, copies, wide, high, low = refs
    else:
        out, wide, high, low = refs
    unpack(blocks, wide)
    products = all_filled(own[...], wide, wide, high, low)
    if not last:
        out[...] = products
        return
    block = assemble(products + before[...])
    image[...] = block
    sums = inner(split_rows(without_positions(own[...]), block))
    empty = jnp.zeros((8, block.shape[1] // 8 - 24), F32)
    copy_halves(block, copies, jnp.concatenate([sums[:8], sums[8:, 8:], empty], axis=1))


def cholesky(matrix):
    size = matrix.shape[0]
    shape = (size, size)
    rows = lax.broadcasted_iota(jnp.int32, shape, 0)
    cols = lax.broadcasted_iota(jnp.int32, shape, 1)
    entry = {}
    for j in range(size):
        column = jnp.broadcast_to(matrix[:, j : j + 1], shape)
        for i in range(j, size):
            entry[i, j] = jnp.broadcast_to(column[i : i + 1, :], shape)
    factor_t = jnp.zeros(shape, F32)
    inverse = jnp.zeros(shape, F32)
    inverse_rows = []
    for j in range(size):
        scale = lax.rsqrt(entry[j, j])
        lower_row = entry[j, j] * scale
        entry[j, j] = scale
        for i in range(j + 1, size):
            entry[i, j] = entry[i, j] * scale
        for i in range(j + 1, size):
            for k in range(j + 1, i + 1):
                entry[i, k] = entry[i, k] - entry[i, j] * entry[k, j]
        lower_row = jnp.where(cols == j, lower_row, 0.0)
        for i in range(j + 1, size):
            lower_row = jnp.where(cols == i, entry[i, j], lower_row)
        factor_t = jnp.where(rows == j, lower_row, factor_t)
        row = jnp.where(cols == j, 1.0, 0.0)
        for k in range(j):
            row = row - entry[j, k] * inverse_rows[k]
        row = row * scale
        inverse_rows.append(row)
        inverse = jnp.where(rows == j, row, inverse)
    return factor_t, inverse


def second_product(fill, own, wide, wide_image, high, low):
    if fill:
        return all_filled(own, wide, wide_image, high, low)
    return apply_tensor(split_rows(wide_image[...]), high, low, 0, high.shape[1])


def third_stage(size, fill, own, wide, *refs):
    refs = list(refs)
    if not fill:
        (high, low), refs = refs[:2], refs[2:]
    images, own_image, products, vectors, known, small, coefficients = refs[:7]
    if fill:
        high, low = refs[7:9]
    wide_image = refs[-1]
    unpack(images, wide_image)
    products[...] = second_product(fill, own[...], wide, wide_image, high, low)
    sums = wide_image[24:, :128]
    for at in range(128, wide_image.shape[1], 128):
        sums = sums + wide_image[24:, at : at + 128]
    width = own.shape[1] // 8
    sums = sum(sums[:, at : at + width] for at in range(width, 128, width)) + sums[:, :width]
    sums = sums / size
    _, inverse_zero = cholesky(sums[:, :8])
    inverse_zero_t = inverse_zero.T
    cross_t = small_matmul(inverse_zero, sums[:, 8:16])
    cross = cross_t.T
    factor_t, inverse = cholesky(sums[:, 16:24] - small_matmul(cross, cross_t))
    factor_one_t = small_matmul(factor_t, inverse_zero_t)
    first = small_matmul(inverse_zero, without_positions(own[...]))
    moved = small_matmul(inverse_zero, own_image[...])
    vectors[...] = small_matmul(inverse, own_image[...] - small_matmul(cross, first))
    known[...] = small_matmul(inverse, small_matmul(cross, moved)) + small_matmul(factor_one_t, first)
    small[...] = inverse
    coefficients[0] = small_matmul(cross_t, inverse_zero_t)
    coefficients[1] = factor_one_t.T


def fourth_stage(fill, own, wide, *refs):
    refs = list(refs)
    if not fill:
        (high, low), refs = refs[:2], refs[2:]
    images, before, vectors_in, known, small, shifted, partials = refs[:7]
    if fill:
        high, low = refs[7:9]
    wide_image = refs[-1]
    unpack(images, wide_image)
    products = second_product(fill, own[...], wide, wide_image, high, low) + before[...]
    vectors = vectors_in[...]
    shift = small_matmul(small[...], assemble(products)) - known[...]
    shifted[...] = shift
    (vector_high, vector_low), (shift_high, shift_low) = split_two(vectors), split_two(shift)
    partial = matmul_nt(vector_high, shift_high) + (
        matmul_nt(vector_high, shift_low) + matmul_nt(vector_low, shift_high)
    )
    line = jnp.concatenate([partial[row : row + 1] for row in range(8)], axis=1)
    partials[...] = jnp.broadcast_to(line[None], partials.shape)


def last_kernel(size, vectors, shifted, both, partials, basis, residual, coefficients):
    beads = basis.shape[2]
    width = partials.shape[2]
    total = jnp.sum(partials[...], axis=0) / size
    spread = jnp.broadcast_to(total, (8, width))
    rows = lax.broadcasted_iota(jnp.int32, spread.shape, 0)
    cols = lax.broadcasted_iota(jnp.int32, spread.shape, 1)
    block = vectors[...]
    left = shifted[...]
    transposed = jnp.where(cols % 8 == rows, spread, 0.0)
    for k in range(8):
        column = jnp.sum(jnp.where(cols // 8 == k, transposed, 0.0), axis=1, keepdims=True)
        left = left - column * block[k : k + 1, :]
    coefficients[0:2] = both[...]
    for k in range(8):
        coefficients[2, k : k + 1, :] = total[:, 8 * k : 8 * k + 8]
    for part in range(3):
        basis[part] = block[:, part * beads : (part + 1) * beads]
        residual[part] = left[:, part * beads : (part + 1) * beads]


def array(*shape, dtype=F32):
    return jax.ShapeDtypeStruct(shape, dtype)


def call(kernel, outs, scratch=(), **options):
    return pl.pallas_call(
        kernel,
        out_shape=outs,
        scratch_shapes=list(scratch),
        compiler_params=pltpu.CompilerParams(vmem_limit_bytes=48 * 1024 * 1024),
        **options,
    )


def to_all(copies):
    rows, cols = lax.axis_size("row"), lax.axis_size("col")
    layers, middle = range(cols // 2), rows // 2
    chips = [(row, layer) for layer in layers for row in range(middle)]
    chips = chips + [(row, layer) for layer in reversed(layers) for row in range(middle, rows)]
    ring = [row * cols + 2 * layer + core for row, layer in chips for core in range(2)]
    return lax.all_to_all(copies, ("row", "col"), 0, 0, axis_index_groups=[ring], tiled=True)


def gather(copies):
    mine = to_all(copies.reshape((-1,) + copies.shape[2:]))
    cols = lax.axis_size("col")
    return mine, lax.ppermute(mine, "col", [(col, col ^ 1) for col in range(cols)])


def local(positions, noise):
    vecs, _, beads = noise.shape
    devices = lax.axis_size("row") * lax.axis_size("col")
    total = beads * devices // 2
    size = 3.0 * beads * devices
    keep = 2 * 2 * 2 * 6 * beads * total <= KEPT
    width = total if keep else min(total, CHUNK)
    block = array(vecs, 4 * beads)
    copies = array(devices // 2, 2, vecs, 2 * beads)
    products = array(4 * vecs, 6 * beads)
    wide, held_wide = array(4 * vecs, total), pltpu.VMEM((4 * vecs, total), F32)
    kept = [array(6 * beads, width, dtype=BF16)] * 2 if keep else []
    held = [] if keep else [pltpu.VMEM((6 * beads, width), BF16)] * 2

    rows = noise.transpose(1, 0, 2).reshape(3 * vecs, beads)
    rows = jnp.concatenate([rows, jnp.pad(positions, ((0, vecs - 3), (0, 0)))], axis=0)
    own, own_copies = call(pack_kernel, [block, copies])(rows)
    one, two = gather(own_copies)
    partial, one_wide, *one_tensor = call(
        functools.partial(first_stage, False), [products, wide] + kept, held
    )(own, one)
    image, images, two_wide, *two_tensor = call(
        functools.partial(first_stage, True), [block, copies, wide] + kept, held
    )(own, two, partial)
    one, two = gather(images)
    partial, vectors, known, small, both = call(
        functools.partial(third_stage, size, not keep),
        [products, block, block, array(vecs, vecs), array(2, vecs, vecs)],
        held + [held_wide],
    )(own, one_wide, *one_tensor, one, image)
    shifted, partials = call(
        functools.partial(fourth_stage, not keep), [block, array(devices, 1, vecs * vecs)], held + [held_wide]
    )(own, two_wide, *two_tensor, two, partial, vectors, known, small)
    partials = to_all(partials)
    basis, residual, coefficients = call(
        functools.partial(last_kernel, size),
        [array(3, vecs, beads), array(3, vecs, beads), array(3, vecs, vecs)],
    )(vectors, shifted, both, partials)
    return (basis.transpose(1, 0, 2), residual.transpose(1, 0, 2), coefficients)


def solution(mesh):
    return jax.shard_map(
        local,
        mesh=mesh,
        in_specs=(P(None, ("row", "col")), P(None, None, ("row", "col"))),
        out_specs=(P(None, None, ("row", "col")), P(None, None, ("row", "col")), P()),
        check_vma=False,
    )
```

```python
import functools

import jax
import jax.numpy as jnp
from jax import lax
from jax.experimental import pallas as pl
from jax.experimental.pallas import tpu as pltpu
from jax.sharding import PartitionSpec as P

CHUNK = 1024
KEPT = 8 * 1024 * 1024
F32 = jnp.float32
BF16 = jnp.bfloat16


def copy_halves(block, copies, last=None):
    beads = block.shape[1] // 4
    middle = beads // 2
    for core in range(2):
        parts = [block[:, part * beads + core * middle : part * beads + (core + 1) * middle] for part in range(4)]
        if last is not None:
            parts[3] = last
        half = jnp.concatenate(parts, axis=1)
        copies[:, core] = jnp.broadcast_to(half[None], (copies.shape[0],) + half.shape)


def pack_kernel(rows, block, copies):
    vecs = block.shape[0]
    flat = jnp.concatenate([rows[part * vecs : (part + 1) * vecs] for part in range(4)], axis=1)
    block[...] = flat
    copy_halves(flat, copies)


def split_two(value):
    high = value.astype(BF16)
    return high, (value - high.astype(F32)).astype(BF16)


def matmul_nt(left, right, precision=None):
    return lax.dot_general(
        left, right, (((1,), (1,)), ((), ())), precision=precision, preferred_element_type=F32
    )


def small_matmul(left, right):
    total = left[:, 0:1] * right[0:1, :]
    for k in range(1, left.shape[1]):
        total = total + left[:, k : k + 1] * right[k : k + 1, :]
    return total


def unpack(blocks, wide):
    count, vecs, lanes = blocks.shape
    width = lanes // 4
    for at in range(0, count, 4):
        four = [blocks[at + index] for index in range(4)]
        for part in range(4):
            wide[part * vecs : (part + 1) * vecs, pl.ds(at * width, 4 * width)] = jnp.concatenate(
                [block[:, part * width : (part + 1) * width] for block in four], axis=1
            )


def target_columns(own):
    beads = own.shape[1] // 4
    targets = own[:, 3 * beads :].T
    return [jnp.broadcast_to(targets[:, axis : axis + 1], (beads, 128)) for axis in range(3)]


def fill_tensor(columns, wide, start, high, low, at):
    beads = columns[0].shape[0]
    block = 32 if beads % 32 == 0 else beads
    sources = [wide[24 + axis : 25 + axis, pl.ds(start, 128)] for axis in range(3)]
    to = pl.ds(at, 128)
    for row in range(0, beads, block):
        moved = [columns[axis][row : row + block] - sources[axis] for axis in range(3)]
        square = moved[0] * moved[0] + moved[1] * moved[1] + moved[2] * moved[2]
        square = jnp.maximum(square, 1e-12)
        inverse = lax.rsqrt(square)
        inverse_sq = inverse * inverse
        near = square < 4.0
        iso = inverse * jnp.where(near, square * (inverse - 9.0 / 32.0), 0.75 + 0.5 * inverse_sq)
        along = inverse * jnp.where(near, 3.0 / 32.0, inverse_sq * (0.75 - 1.5 * inverse_sq))
        scaled = [along * item for item in moved]
        parts = [
            iso + scaled[0] * moved[0],
            scaled[0] * moved[1],
            scaled[0] * moved[2],
            iso + scaled[1] * moved[1],
            scaled[1] * moved[2],
            iso + scaled[2] * moved[2],
        ]
        for part, value in enumerate(parts):
            upper, lower = split_two(value)
            rows = slice(part * beads + row, part * beads + row + block)
            high[rows, to] = upper
            low[rows, to] = lower


def apply_tensor(both, high, low, at, step):
    lanes = pl.ds(at, step)
    half = both.shape[0] // 2
    first = matmul_nt(both, high[:, lanes])
    return first[:half] + first[half:] + matmul_nt(both[:half], low[:, lanes])


def split_rows(*values):
    highs, lows = zip(*[split_two(value) for value in values])
    return jnp.concatenate(highs + lows, axis=0)


def inner(both):
    half = both.shape[0] // 2
    first = matmul_nt(both, both[:half])
    return first[:half] + first[half:] + matmul_nt(both[:half], both[half:])


def assemble(products):
    beads = products.shape[1] // 6

    def part(row, component):
        return products[8 * row : 8 * row + 8, component * beads : (component + 1) * beads]

    x = part(0, 0) + part(1, 1) + part(2, 2)
    y = part(0, 1) + part(1, 3) + part(2, 4)
    z = part(0, 2) + part(1, 4) + part(2, 5)
    return jnp.concatenate([x, y, z, jnp.zeros(x.shape, F32)], axis=1)


def filled_product(columns, source, wide, start, high, low):
    width = high.shape[1]
    products = jnp.zeros((32, high.shape[0]), F32)
    steps = [(at, min(256, width - at)) for at in range(0, width, 256)]
    vectors = [split_rows(wide[:, pl.ds(pl.multiple_of(start + at, 128), step)]) for at, step in steps]
    for index in range(len(steps) + 1):
        if index < len(steps):
            at, step = steps[index]
            for part in range(at, at + step, 128):
                fill_tensor(columns, source, pl.multiple_of(start + part, 128), high, low, part)
        if index > 0:
            products = products + apply_tensor(vectors[index - 1], high, low, *steps[index - 1])
    return products


def all_filled(own, source, wide, high, low):
    columns = target_columns(own)
    width = high.shape[1]
    chunk = lambda start: filled_product(columns, source, wide, start, high, low)
    if wide.shape[1] == width:
        return chunk(0)
    body = lambda index, total: total + chunk(index * width)
    return lax.fori_loop(1, wide.shape[1] // width, body, chunk(0))


def without_positions(block):
    lanes = lax.broadcasted_iota(jnp.int32, block.shape, 1)
    return jnp.where(lanes < block.shape[1] // 4 * 3, block, 0.0)


def first_stage(last, own, blocks, *refs):
    refs = list(refs)
    if last:
        before, image, copies, wide, high, low = refs
    else:
        out, wide, high, low = refs
    unpack(blocks, wide)
    products = all_filled(own[...], wide, wide, high, low)
    if not last:
        out[...] = products
        return
    block = assemble(products + before[...])
    image[...] = block
    sums = inner(split_rows(without_positions(own[...]), block))
    empty = jnp.zeros((8, block.shape[1] // 8 - 24), F32)
    copy_halves(block, copies, jnp.concatenate([sums[:8], sums[8:, 8:], empty], axis=1))


def cholesky(matrix):
    size = matrix.shape[0]
    shape = (size, size)
    rows = lax.broadcasted_iota(jnp.int32, shape, 0)
    cols = lax.broadcasted_iota(jnp.int32, shape, 1)
    entry = {}
    for j in range(size):
        column = jnp.broadcast_to(matrix[:, j : j + 1], shape)
        for i in range(j, size):
            entry[i, j] = jnp.broadcast_to(column[i : i + 1, :], shape)
    factor_t = jnp.zeros(shape, F32)
    inverse = jnp.zeros(shape, F32)
    inverse_rows = []
    for j in range(size):
        scale = lax.rsqrt(entry[j, j])
        lower_row = entry[j, j] * scale
        entry[j, j] = scale
        for i in range(j + 1, size):
            entry[i, j] = entry[i, j] * scale
        for i in range(j + 1, size):
            for k in range(j + 1, i + 1):
                entry[i, k] = entry[i, k] - entry[i, j] * entry[k, j]
        lower_row = jnp.where(cols == j, lower_row, 0.0)
        for i in range(j + 1, size):
            lower_row = jnp.where(cols == i, entry[i, j], lower_row)
        factor_t = jnp.where(rows == j, lower_row, factor_t)
        row = jnp.where(cols == j, 1.0, 0.0)
        for k in range(j):
            row = row - entry[j, k] * inverse_rows[k]
        row = row * scale
        inverse_rows.append(row)
        inverse = jnp.where(rows == j, row, inverse)
    return factor_t, inverse


def second_product(fill, own, wide, wide_image, high, low):
    if fill:
        return all_filled(own, wide, wide_image, high, low)
    return apply_tensor(split_rows(wide_image[...]), high, low, 0, high.shape[1])


def third_stage(size, fill, own, wide, *refs):
    refs = list(refs)
    if not fill:
        (high, low), refs = refs[:2], refs[2:]
    images, own_image, products, vectors, known, small, coefficients = refs[:7]
    if fill:
        high, low = refs[7:9]
    wide_image = refs[-1]
    unpack(images, wide_image)
    products[...] = second_product(fill, own[...], wide, wide_image, high, low)
    sums = wide_image[24:, :128]
    for at in range(128, wide_image.shape[1], 128):
        sums = sums + wide_image[24:, at : at + 128]
    width = own.shape[1] // 8
    sums = sum(sums[:, at : at + width] for at in range(width, 128, width)) + sums[:, :width]
    sums = sums / size
    _, inverse_zero = cholesky(sums[:, :8])
    inverse_zero_t = inverse_zero.T
    cross_t = small_matmul(inverse_zero, sums[:, 8:16])
    cross = cross_t.T
    factor_t, inverse = cholesky(sums[:, 16:24] - small_matmul(cross, cross_t))
    factor_one_t = small_matmul(factor_t, inverse_zero_t)
    first = small_matmul(inverse_zero, without_positions(own[...]))
    moved = small_matmul(inverse_zero, own_image[...])
    vectors[...] = small_matmul(inverse, own_image[...] - small_matmul(cross, first))
    known[...] = small_matmul(inverse, small_matmul(cross, moved)) + small_matmul(factor_one_t, first)
    small[...] = inverse
    coefficients[0] = small_matmul(cross_t, inverse_zero_t)
    coefficients[1] = factor_one_t.T


def fourth_stage(fill, own, wide, *refs):
    refs = list(refs)
    if not fill:
        (high, low), refs = refs[:2], refs[2:]
    images, before, vectors_in, known, small, shifted, partials = refs[:7]
    if fill:
        high, low = refs[7:9]
    wide_image = refs[-1]
    unpack(images, wide_image)
    products = second_product(fill, own[...], wide, wide_image, high, low) + before[...]
    vectors = vectors_in[...]
    shift = small_matmul(small[...], assemble(products)) - known[...]
    shifted[...] = shift
    (vector_high, vector_low), (shift_high, shift_low) = split_two(vectors), split_two(shift)
    partial = matmul_nt(vector_high, shift_high) + (
        matmul_nt(vector_high, shift_low) + matmul_nt(vector_low, shift_high)
    )
    line = jnp.concatenate([partial[row : row + 1] for row in range(8)], axis=1)
    partials[...] = jnp.broadcast_to(line[None], partials.shape)


def last_kernel(
    size, vectors, shifted, both, partials, basis, residual, coefficients, held_basis, held_residual, held_small, sems
):
    beads = basis.shape[2]
    width = partials.shape[2]
    copies = [
        pltpu.make_async_copy(held_basis, basis, sems.at[0]),
        pltpu.make_async_copy(held_residual, residual, sems.at[1]),
        pltpu.make_async_copy(held_small, coefficients, sems.at[2]),
    ]
    block = vectors[...]
    for part in range(3):
        held_basis[part] = block[:, part * beads : (part + 1) * beads]
    copies[0].start()
    total = jnp.sum(partials[...], axis=0) / size
    spread = jnp.broadcast_to(total, (8, width))
    rows = lax.broadcasted_iota(jnp.int32, spread.shape, 0)
    cols = lax.broadcasted_iota(jnp.int32, spread.shape, 1)
    left = shifted[...]
    transposed = jnp.where(cols % 8 == rows, spread, 0.0)
    for k in range(8):
        column = jnp.sum(jnp.where(cols // 8 == k, transposed, 0.0), axis=1, keepdims=True)
        left = left - column * block[k : k + 1, :]
    for part in range(3):
        held_residual[part] = left[:, part * beads : (part + 1) * beads]
    copies[1].start()
    held_small[0:2] = both[...]
    for k in range(8):
        held_small[2, k : k + 1, :] = total[:, 8 * k : 8 * k + 8]
    copies[2].start()
    for copy in copies:
        copy.wait()


def array(*shape, dtype=F32):
    return jax.ShapeDtypeStruct(shape, dtype)


def call(kernel, outs, scratch=(), fuse=None, **options):
    return pl.pallas_call(
        kernel,
        out_shape=outs,
        scratch_shapes=list(scratch),
        compiler_params=pltpu.CompilerParams(vmem_limit_bytes=48 * 1024 * 1024, allow_input_fusion=fuse),
        **options,
    )


def to_all(copies):
    rows, cols = lax.axis_size("row"), lax.axis_size("col")
    layers, middle = range(cols // 2), rows // 2
    chips = [(row, layer) for layer in layers for row in range(middle)]
    chips = chips + [(row, layer) for layer in reversed(layers) for row in range(middle, rows)]
    ring = [row * cols + 2 * layer + core for row, layer in chips for core in range(2)]
    return lax.all_to_all(copies, ("row", "col"), 0, 0, axis_index_groups=[ring], tiled=True)


def gather(copies):
    mine = to_all(copies.reshape((-1,) + copies.shape[2:]))
    cols = lax.axis_size("col")
    return mine, lax.ppermute(mine, "col", [(col, col ^ 1) for col in range(cols)])


def local(positions, noise):
    vecs, _, beads = noise.shape
    devices = lax.axis_size("row") * lax.axis_size("col")
    total = beads * devices // 2
    size = 3.0 * beads * devices
    keep = 2 * 2 * 2 * 6 * beads * total <= KEPT
    width = total if keep else min(total, CHUNK)
    block = array(vecs, 4 * beads)
    copies = array(devices // 2, 2, vecs, 2 * beads)
    products = array(4 * vecs, 6 * beads)
    wide, held_wide = array(4 * vecs, total), pltpu.VMEM((4 * vecs, total), F32)
    kept = [array(6 * beads, width, dtype=BF16)] * 2 if keep else []
    held = [] if keep else [pltpu.VMEM((6 * beads, width), BF16)] * 2

    rows = noise.transpose(1, 0, 2).reshape(3 * vecs, beads)
    rows = jnp.concatenate([rows, jnp.pad(positions, ((0, vecs - 3), (0, 0)))], axis=0)
    own, own_copies = call(pack_kernel, [block, copies], fuse=[True])(rows)
    one, two = gather(own_copies)
    partial, one_wide, *one_tensor = call(
        functools.partial(first_stage, False), [products, wide] + kept, held
    )(own, one)
    image, images, two_wide, *two_tensor = call(
        functools.partial(first_stage, True), [block, copies, wide] + kept, held
    )(own, two, partial)
    one, two = gather(images)
    partial, vectors, known, small, both = call(
        functools.partial(third_stage, size, not keep),
        [products, block, block, array(vecs, vecs), array(2, vecs, vecs)],
        held + [held_wide],
    )(own, one_wide, *one_tensor, one, image)
    shifted, partials = call(
        functools.partial(fourth_stage, not keep), [block, array(devices, 1, vecs * vecs)], held + [held_wide]
    )(own, two_wide, *two_tensor, two, partial, vectors, known, small)
    partials = to_all(partials)
    outs = [array(3, vecs, beads), array(3, vecs, beads), array(3, vecs, vecs)]
    basis, residual, coefficients = call(
        functools.partial(last_kernel, size),
        outs,
        [pltpu.VMEM(out.shape, F32) for out in outs] + [pltpu.SemaphoreType.DMA((3,))],
        out_specs=[pl.BlockSpec(memory_space=pltpu.HBM)] * 3,
    )(vectors, shifted, both, partials)
    return (basis.transpose(1, 0, 2), residual.transpose(1, 0, 2), coefficients)


def solution(mesh):
    return jax.shard_map(
        local,
        mesh=mesh,
        in_specs=(P(None, ("row", "col")), P(None, None, ("row", "col"))),
        out_specs=(P(None, None, ("row", "col")), P(None, None, ("row", "col")), P()),
        check_vma=False,
    )
```

```python
import functools

import jax
import jax.numpy as jnp
from jax import lax
from jax.experimental import pallas as pl
from jax.experimental.pallas import tpu as pltpu
from jax.sharding import PartitionSpec as P

CHUNK = 1024
KEPT = 8 * 1024 * 1024
F32 = jnp.float32
BF16 = jnp.bfloat16


def copy_halves(block, copies, last=None):
    beads = block.shape[1] // 4
    middle = beads // 2
    for core in range(2):
        parts = [block[:, part * beads + core * middle : part * beads + (core + 1) * middle] for part in range(4)]
        if last is not None:
            parts[3] = last
        half = jnp.concatenate(parts, axis=1)
        copies[:, core] = jnp.broadcast_to(half[None], (copies.shape[0],) + half.shape)


def pack_kernel(rows, block, copies):
    vecs = block.shape[0]
    flat = jnp.concatenate([rows[part * vecs : (part + 1) * vecs] for part in range(4)], axis=1)
    block[...] = flat
    copy_halves(flat, copies)


def split_two(value):
    high = value.astype(BF16)
    return high, (value - high.astype(F32)).astype(BF16)


def matmul_nt(left, right, precision=None):
    return lax.dot_general(
        left, right, (((1,), (1,)), ((), ())), precision=precision, preferred_element_type=F32
    )


def matmul(left, right):
    return lax.dot_general(left, right, (((1,), (0,)), ((), ())), preferred_element_type=F32)


def small_matmul(left, right):
    total = left[:, 0:1] * right[0:1, :]
    for k in range(1, left.shape[1]):
        total = total + left[:, k : k + 1] * right[k : k + 1, :]
    return total


def unpack(blocks, wide):
    count, vecs, lanes = blocks.shape
    width = lanes // 4
    for at in range(0, count, 4):
        four = [blocks[at + index] for index in range(4)]
        for part in range(4):
            wide[part * vecs : (part + 1) * vecs, pl.ds(at * width, 4 * width)] = jnp.concatenate(
                [block[:, part * width : (part + 1) * width] for block in four], axis=1
            )


def target_columns(own):
    beads = own.shape[1] // 4
    targets = own[:, 3 * beads :].T
    return [jnp.broadcast_to(targets[:, axis : axis + 1], (beads, 128)) for axis in range(3)]


def fill_tensor(columns, wide, start, high, low, at):
    beads = columns[0].shape[0]
    block = 32 if beads % 32 == 0 else beads
    sources = [wide[24 + axis : 25 + axis, pl.ds(start, 128)] for axis in range(3)]
    to = pl.ds(at, 128)
    for row in range(0, beads, block):
        moved = [columns[axis][row : row + block] - sources[axis] for axis in range(3)]
        square = moved[0] * moved[0] + moved[1] * moved[1] + moved[2] * moved[2]
        square = jnp.maximum(square, 1e-12)
        inverse = lax.rsqrt(square)
        inverse_sq = inverse * inverse
        near = square < 4.0
        iso = inverse * jnp.where(near, square * (inverse - 9.0 / 32.0), 0.75 + 0.5 * inverse_sq)
        along = inverse * jnp.where(near, 3.0 / 32.0, inverse_sq * (0.75 - 1.5 * inverse_sq))
        scaled = [along * item for item in moved]
        parts = [
            iso + scaled[0] * moved[0],
            scaled[0] * moved[1],
            scaled[0] * moved[2],
            iso + scaled[1] * moved[1],
            scaled[1] * moved[2],
            iso + scaled[2] * moved[2],
        ]
        for part, value in enumerate(parts):
            upper, lower = split_two(value)
            rows = slice(part * beads + row, part * beads + row + block)
            high[rows, to] = upper
            low[rows, to] = lower


def apply_tensor(both, high, low, at, step):
    lanes = pl.ds(at, step)
    half = both.shape[0] // 2
    first = matmul_nt(both, high[:, lanes])
    return first[:half] + first[half:] + matmul_nt(both[:half], low[:, lanes])


def split_rows(*values):
    highs, lows = zip(*[split_two(value) for value in values])
    return jnp.concatenate(highs + lows, axis=0)


def inner(both):
    half = both.shape[0] // 2
    first = matmul_nt(both, both[:half])
    return first[:half] + first[half:] + matmul_nt(both[:half], both[half:])


def assemble(products):
    beads = products.shape[1] // 6

    def part(row, component):
        return products[8 * row : 8 * row + 8, component * beads : (component + 1) * beads]

    x = part(0, 0) + part(1, 1) + part(2, 2)
    y = part(0, 1) + part(1, 3) + part(2, 4)
    z = part(0, 2) + part(1, 4) + part(2, 5)
    return jnp.concatenate([x, y, z, jnp.zeros(x.shape, F32)], axis=1)


def filled_product(columns, source, wide, start, high, low):
    width = high.shape[1]
    products = jnp.zeros((32, high.shape[0]), F32)
    steps = [(at, min(256, width - at)) for at in range(0, width, 256)]
    vectors = [split_rows(wide[:, pl.ds(pl.multiple_of(start + at, 128), step)]) for at, step in steps]
    for index in range(len(steps) + 1):
        if index < len(steps):
            at, step = steps[index]
            for part in range(at, at + step, 128):
                fill_tensor(columns, source, pl.multiple_of(start + part, 128), high, low, part)
        if index > 0:
            products = products + apply_tensor(vectors[index - 1], high, low, *steps[index - 1])
    return products


def all_filled(own, source, wide, high, low):
    columns = target_columns(own)
    width = high.shape[1]
    chunk = lambda start: filled_product(columns, source, wide, start, high, low)
    if wide.shape[1] == width:
        return chunk(0)
    body = lambda index, total: total + chunk(index * width)
    return lax.fori_loop(1, wide.shape[1] // width, body, chunk(0))


def without_positions(block):
    lanes = lax.broadcasted_iota(jnp.int32, block.shape, 1)
    return jnp.where(lanes < block.shape[1] // 4 * 3, block, 0.0)


def first_stage(last, own, blocks, *refs):
    refs = list(refs)
    if last:
        before, image, copies, wide, high, low = refs
    else:
        out, wide, high, low = refs
    unpack(blocks, wide)
    products = all_filled(own[...], wide, wide, high, low)
    if not last:
        out[...] = products
        return
    block = assemble(products + before[...])
    image[...] = block
    sums = inner(split_rows(without_positions(own[...]), block))
    empty = jnp.zeros((8, block.shape[1] // 8 - 24), F32)
    copy_halves(block, copies, jnp.concatenate([sums[:8], sums[8:, 8:], empty], axis=1))


def cholesky(matrix):
    size = matrix.shape[0]
    shape = (size, size)
    rows = lax.broadcasted_iota(jnp.int32, shape, 0)
    cols = lax.broadcasted_iota(jnp.int32, shape, 1)
    entry = {}
    for j in range(size):
        column = jnp.broadcast_to(matrix[:, j : j + 1], shape)
        for i in range(j, size):
            entry[i, j] = jnp.broadcast_to(column[i : i + 1, :], shape)
    factor_t = jnp.zeros(shape, F32)
    inverse = jnp.zeros(shape, F32)
    inverse_rows = []
    for j in range(size):
        scale = lax.rsqrt(entry[j, j])
        lower_row = entry[j, j] * scale
        entry[j, j] = scale
        for i in range(j + 1, size):
            entry[i, j] = entry[i, j] * scale
        for i in range(j + 1, size):
            for k in range(j + 1, i + 1):
                entry[i, k] = entry[i, k] - entry[i, j] * entry[k, j]
        lower_row = jnp.where(cols == j, lower_row, 0.0)
        for i in range(j + 1, size):
            lower_row = jnp.where(cols == i, entry[i, j], lower_row)
        factor_t = jnp.where(rows == j, lower_row, factor_t)
        row = jnp.where(cols == j, 1.0, 0.0)
        for k in range(j):
            row = row - entry[j, k] * inverse_rows[k]
        row = row * scale
        inverse_rows.append(row)
        inverse = jnp.where(rows == j, row, inverse)
    return factor_t, inverse


def second_product(fill, own, wide, wide_image, high, low):
    if fill:
        return all_filled(own, wide, wide_image, high, low)
    return apply_tensor(split_rows(wide_image[...]), high, low, 0, high.shape[1])


def spread_rows(block):
    beads = block.shape[1] // 4
    parts = [block[:, part * beads : (part + 1) * beads] for part in range(3)]
    empty = jnp.zeros(parts[0].shape, F32)
    rows = []
    for own in range(3):
        lanes = []
        for one, two in ((0, 0), (0, 1), (0, 2), (1, 1), (1, 2), (2, 2)):
            lanes.append(parts[two] if own == one else parts[one] if own == two else empty)
        rows.append(jnp.concatenate(lanes, axis=1))
    return jnp.concatenate(rows + [jnp.zeros(rows[0].shape, F32)], axis=0)


def backward_stage(fill, own, wide, *refs):
    refs = list(refs)
    if not fill:
        (high, low), refs = refs[:2], refs[2:]
    image, out = refs[:2]
    if fill:
        high, low = refs[2:4]
    both = split_rows(spread_rows(image[...]))
    half = both.shape[0] // 2

    def add(start):
        first = matmul(both, high[...])
        sums = first[:half] + first[half:] + matmul(both[:half], low[...])
        out[:, pl.ds(start, high.shape[1])] = sums

    if not fill:
        add(0)
        return
    columns = target_columns(own[...])

    def body(index, carry):
        start = pl.multiple_of(index * high.shape[1], 128)
        for at in range(0, high.shape[1], 128):
            fill_tensor(columns, wide, pl.multiple_of(start + at, 128), high, low, at)
        add(start)
        return carry

    lax.fori_loop(0, wide.shape[1] // high.shape[1], body, 0)


def cross_stage(images, own_sums, other_sums, partials, wide_image):
    unpack(images, wide_image)
    left = split_rows(wide_image[...])
    right = split_rows(own_sums[...] + other_sums[...])
    half = left.shape[0] // 2
    first = matmul_nt(left, right[:half])
    sums = first[:half] + first[half:] + matmul_nt(left[:half], right[half:])
    partial = sums[:8, :8] + sums[8:16, 8:16] + sums[16:24, 16:24]
    line = jnp.concatenate([partial[row : row + 1] for row in range(8)], axis=1)
    partials[...] = jnp.broadcast_to(line[None], partials.shape)


def third_stage(size, fill, own, wide, *refs):
    refs = list(refs)
    if not fill:
        (high, low), refs = refs[:2], refs[2:]
    images, own_image, products, vectors, known, small, coefficients = refs[:7]
    if fill:
        high, low = refs[7:9]
    wide_image = refs[-1]
    unpack(images, wide_image)
    products[...] = second_product(fill, own[...], wide, wide_image, high, low)
    sums = wide_image[24:, :128]
    for at in range(128, wide_image.shape[1], 128):
        sums = sums + wide_image[24:, at : at + 128]
    width = own.shape[1] // 8
    sums = sum(sums[:, at : at + width] for at in range(width, 128, width)) + sums[:, :width]
    sums = sums / size
    noise_sums, cross_sums, image_sums = sums[:, :8], sums[:, 8:16], sums[:, 16:24]
    _, inverse_zero = cholesky(noise_sums)
    inverse_zero_t = inverse_zero.T
    cross_t = small_matmul(inverse_zero, cross_sums)
    cross = cross_t.T
    factor_t, inverse = cholesky(image_sums - small_matmul(cross, cross_t))
    factor_one_t = small_matmul(factor_t, inverse_zero_t)
    factor_one = factor_one_t.T
    first = small_matmul(inverse_zero, without_positions(own[...]))
    moved = small_matmul(inverse_zero, own_image[...])
    alpha = small_matmul(cross_t, inverse_zero_t)
    vectors[...] = small_matmul(inverse, own_image[...] - small_matmul(cross, first))
    known[...] = small_matmul(inverse, small_matmul(cross, moved)) + small_matmul(factor_one_t, first)
    image_moved = small_matmul(image_sums, inverse_zero_t)
    moved_image = small_matmul(inverse_zero, image_sums)
    known_sums = small_matmul(small_matmul(cross, alpha), cross_t)
    known_sums = known_sums - small_matmul(image_moved, cross_t) - small_matmul(cross, moved_image)
    first_sums = small_matmul(small_matmul(inverse_zero, noise_sums), inverse_zero_t)
    vector_first = small_matmul(inverse, cross - small_matmul(cross, first_sums))
    small[0] = inverse
    small[1] = inverse.T
    small[2] = known_sums
    small[3] = small_matmul(vector_first, factor_one)
    coefficients[0] = alpha
    coefficients[1] = factor_one


def fourth_stage(fill, own, wide, *refs):
    refs = list(refs)
    if not fill:
        (high, low), refs = refs[:2], refs[2:]
    images, before, known, small, shifted = refs[:5]
    if fill:
        high, low = refs[5:7]
    wide_image = refs[-1]
    unpack(images, wide_image)
    products = second_product(fill, own[...], wide, wide_image, high, low) + before[...]
    shifted[...] = small_matmul(small[0], assemble(products)) - known[...]


def last_kernel(size, vectors, shifted, both, small, partials, basis, residual, coefficients):
    beads = basis.shape[2]
    total = jnp.sum(partials[...], axis=0) / size
    sums = jnp.concatenate([total[:, 8 * k : 8 * k + 8] for k in range(8)], axis=0)
    alpha = small_matmul(small_matmul(small[0], sums + small[2]), small[1]) - small[3]
    block = vectors[...]
    left = shifted[...] - small_matmul(alpha.T, block)
    coefficients[0:2] = both[...]
    coefficients[2] = alpha
    for part in range(3):
        basis[part] = block[:, part * beads : (part + 1) * beads]
        residual[part] = left[:, part * beads : (part + 1) * beads]


def array(*shape, dtype=F32):
    return jax.ShapeDtypeStruct(shape, dtype)


def call(kernel, outs, scratch=(), **options):
    return pl.pallas_call(
        kernel,
        out_shape=outs,
        scratch_shapes=list(scratch),
        compiler_params=pltpu.CompilerParams(vmem_limit_bytes=48 * 1024 * 1024),
        **options,
    )


def to_all(copies):
    rows, cols = lax.axis_size("row"), lax.axis_size("col")
    layers, middle = range(cols // 2), rows // 2
    chips = [(row, layer) for layer in layers for row in range(middle)]
    chips = chips + [(row, layer) for layer in reversed(layers) for row in range(middle, rows)]
    ring = [row * cols + 2 * layer + core for row, layer in chips for core in range(2)]
    return lax.all_to_all(copies, ("row", "col"), 0, 0, axis_index_groups=[ring], tiled=True)


def between_cores(block):
    cols = lax.axis_size("col")
    return lax.ppermute(block, "col", [(col, col ^ 1) for col in range(cols)])


def local(positions, noise):
    vecs, _, beads = noise.shape
    devices = lax.axis_size("row") * lax.axis_size("col")
    total = beads * devices // 2
    size = 3.0 * beads * devices
    keep = 2 * 2 * 2 * 6 * beads * total <= KEPT
    width = total if keep else min(total, CHUNK)
    block = array(vecs, 4 * beads)
    copies = array(devices // 2, 2, vecs, 2 * beads)
    products = array(4 * vecs, 6 * beads)
    wide, held_wide = array(4 * vecs, total), pltpu.VMEM((4 * vecs, total), F32)
    kept = [array(6 * beads, width, dtype=BF16)] * 2 if keep else []
    held = [] if keep else [pltpu.VMEM((6 * beads, width), BF16)] * 2

    rows = noise.transpose(1, 0, 2).reshape(3 * vecs, beads)
    rows = jnp.concatenate([rows, jnp.pad(positions, ((0, vecs - 3), (0, 0)))], axis=0)
    own, own_copies = call(pack_kernel, [block, copies])(rows)
    one = to_all(own_copies.reshape((-1,) + own_copies.shape[2:]))
    two = between_cores(one)
    partial, one_wide, *one_tensor = call(
        functools.partial(first_stage, False), [products, wide] + kept, held
    )(own, one)
    image, images, two_wide, *two_tensor = call(
        functools.partial(first_stage, True), [block, copies, wide] + kept, held
    )(own, two, partial)
    backward = call(functools.partial(backward_stage, not keep), wide, held)
    other_sums = between_cores(backward(own, two_wide, *two_tensor, image))
    own_sums = backward(own, one_wide, *one_tensor, image)
    one = to_all(images.reshape((-1,) + images.shape[2:]))
    partials = call(cross_stage, array(devices, 1, vecs * vecs), [held_wide])(one, own_sums, other_sums)
    partials = to_all(partials)
    two = between_cores(one)
    partial, vectors, known, small, both = call(
        functools.partial(third_stage, size, not keep),
        [products, block, block, array(4, vecs, vecs), array(2, vecs, vecs)],
        held + [held_wide],
    )(own, one_wide, *one_tensor, one, image)
    shifted = call(functools.partial(fourth_stage, not keep), block, held + [held_wide])(
        own, two_wide, *two_tensor, two, partial, known, small
    )
    basis, residual, coefficients = call(
        functools.partial(last_kernel, size),
        [array(3, vecs, beads), array(3, vecs, beads), array(3, vecs, vecs)],
    )(vectors, shifted, both, small, partials)
    return (basis.transpose(1, 0, 2), residual.transpose(1, 0, 2), coefficients)


def solution(mesh):
    return jax.shard_map(
        local,
        mesh=mesh,
        in_specs=(P(None, ("row", "col")), P(None, None, ("row", "col"))),
        out_specs=(P(None, None, ("row", "col")), P(None, None, ("row", "col")), P()),
        check_vma=False,
    )
```

```python
import functools

import jax
import jax.numpy as jnp
from jax import lax
from jax.experimental import pallas as pl
from jax.experimental.pallas import tpu as pltpu
from jax.sharding import PartitionSpec as P

CHUNK = 1024
KEPT = 8 * 1024 * 1024
VMEM = 16 * 1024 * 1024
F32 = jnp.float32
BF16 = jnp.bfloat16


def copy_halves(block, copies, last=None):
    beads = block.shape[1] // 4
    middle = beads // 2
    for core in range(2):
        parts = [block[:, part * beads + core * middle : part * beads + (core + 1) * middle] for part in range(4)]
        if last is not None:
            parts[3] = last
        half = jnp.concatenate(parts, axis=1)
        copies[:, core] = jnp.broadcast_to(half[None], (copies.shape[0],) + half.shape)


def pack_kernel(rows, block, copies):
    vecs = block.shape[0]
    flat = jnp.concatenate([rows[part * vecs : (part + 1) * vecs] for part in range(4)], axis=1)
    block[...] = flat
    copy_halves(flat, copies)


def split_two(value):
    high = value.astype(BF16)
    return high, (value - high.astype(F32)).astype(BF16)


def matmul_nt(left, right, precision=None):
    return lax.dot_general(
        left, right, (((1,), (1,)), ((), ())), precision=precision, preferred_element_type=F32
    )


def matmul(left, right):
    return lax.dot_general(left, right, (((1,), (0,)), ((), ())), preferred_element_type=F32)


def small_matmul(left, right):
    total = left[:, 0:1] * right[0:1, :]
    for k in range(1, left.shape[1]):
        total = total + left[:, k : k + 1] * right[k : k + 1, :]
    return total


def unpack(blocks, wide):
    count, vecs, lanes = blocks.shape
    width = lanes // 4
    for at in range(0, count, 4):
        four = [blocks[at + index] for index in range(4)]
        for part in range(4):
            wide[part * vecs : (part + 1) * vecs, pl.ds(at * width, 4 * width)] = jnp.concatenate(
                [block[:, part * width : (part + 1) * width] for block in four], axis=1
            )


def target_columns(own):
    beads = own.shape[1] // 4
    targets = own[:, 3 * beads :].T
    return [jnp.broadcast_to(targets[:, axis : axis + 1], (beads, 128)) for axis in range(3)]


def fill_tensor(columns, wide, start, high, low, at):
    beads = columns[0].shape[0]
    block = 32 if beads % 32 == 0 else beads
    sources = [wide[24 + axis : 25 + axis, pl.ds(start, 128)] for axis in range(3)]
    to = pl.ds(at, 128)
    for row in range(0, beads, block):
        moved = [columns[axis][row : row + block] - sources[axis] for axis in range(3)]
        square = moved[0] * moved[0] + moved[1] * moved[1] + moved[2] * moved[2]
        square = jnp.maximum(square, 1e-12)
        inverse = lax.rsqrt(square)
        inverse_sq = inverse * inverse
        near = square < 4.0
        iso = inverse * jnp.where(near, square * (inverse - 9.0 / 32.0), 0.75 + 0.5 * inverse_sq)
        along = inverse * jnp.where(near, 3.0 / 32.0, inverse_sq * (0.75 - 1.5 * inverse_sq))
        scaled = [along * item for item in moved]
        parts = [
            iso + scaled[0] * moved[0],
            scaled[0] * moved[1],
            scaled[0] * moved[2],
            iso + scaled[1] * moved[1],
            scaled[1] * moved[2],
            iso + scaled[2] * moved[2],
        ]
        for part, value in enumerate(parts):
            upper, lower = split_two(value)
            rows = slice(part * beads + row, part * beads + row + block)
            high[rows, to] = upper
            low[rows, to] = lower


def apply_tensor(both, high, low, at, step):
    lanes = pl.ds(at, step)
    half = both.shape[0] // 2
    first = matmul_nt(both, high[:, lanes])
    return first[:half] + first[half:] + matmul_nt(both[:half], low[:, lanes])


def split_rows(*values):
    highs, lows = zip(*[split_two(value) for value in values])
    return jnp.concatenate(highs + lows, axis=0)


def inner(both):
    half = both.shape[0] // 2
    first = matmul_nt(both, both[:half])
    return first[:half] + first[half:] + matmul_nt(both[:half], both[half:])


def assemble(products):
    beads = products.shape[1] // 6

    def part(row, component):
        return products[8 * row : 8 * row + 8, component * beads : (component + 1) * beads]

    x = part(0, 0) + part(1, 1) + part(2, 2)
    y = part(0, 1) + part(1, 3) + part(2, 4)
    z = part(0, 2) + part(1, 4) + part(2, 5)
    return jnp.concatenate([x, y, z, jnp.zeros(x.shape, F32)], axis=1)


def filled_product(columns, source, wide, start, high, low):
    width = high.shape[1]
    products = jnp.zeros((32, high.shape[0]), F32)
    steps = [(at, min(256, width - at)) for at in range(0, width, 256)]
    vectors = [split_rows(wide[:, pl.ds(pl.multiple_of(start + at, 128), step)]) for at, step in steps]
    for index in range(len(steps) + 1):
        if index < len(steps):
            at, step = steps[index]
            for part in range(at, at + step, 128):
                fill_tensor(columns, source, pl.multiple_of(start + part, 128), high, low, part)
        if index > 0:
            products = products + apply_tensor(vectors[index - 1], high, low, *steps[index - 1])
    return products


def all_filled(own, source, wide, high, low):
    columns = target_columns(own)
    width = high.shape[1]
    chunk = lambda start: filled_product(columns, source, wide, start, high, low)
    if wide.shape[1] == width:
        return chunk(0)
    body = lambda index, total: total + chunk(index * width)
    return lax.fori_loop(1, wide.shape[1] // width, body, chunk(0))


def without_positions(block):
    lanes = lax.broadcasted_iota(jnp.int32, block.shape, 1)
    return jnp.where(lanes < block.shape[1] // 4 * 3, block, 0.0)


def first_stage(last, own, blocks, *refs):
    refs = list(refs)
    if last:
        before, image, copies, wide, high, low = refs
    else:
        out, wide, high, low = refs
    unpack(blocks, wide)
    products = all_filled(own[...], wide, wide, high, low)
    if not last:
        out[...] = products
        return
    block = assemble(products + before[...])
    image[...] = block
    sums = inner(split_rows(without_positions(own[...]), block))
    empty = jnp.zeros((8, block.shape[1] // 8 - 24), F32)
    copy_halves(block, copies, jnp.concatenate([sums[:8], sums[8:, 8:], empty], axis=1))


def cholesky(matrix):
    size = matrix.shape[0]
    shape = (size, size)
    rows = lax.broadcasted_iota(jnp.int32, shape, 0)
    cols = lax.broadcasted_iota(jnp.int32, shape, 1)
    entry = {}
    for j in range(size):
        column = jnp.broadcast_to(matrix[:, j : j + 1], shape)
        for i in range(j, size):
            entry[i, j] = jnp.broadcast_to(column[i : i + 1, :], shape)
    factor_t = jnp.zeros(shape, F32)
    inverse = jnp.zeros(shape, F32)
    inverse_rows = []
    for j in range(size):
        scale = lax.rsqrt(entry[j, j])
        lower_row = entry[j, j] * scale
        entry[j, j] = scale
        for i in range(j + 1, size):
            entry[i, j] = entry[i, j] * scale
        for i in range(j + 1, size):
            for k in range(j + 1, i + 1):
                entry[i, k] = entry[i, k] - entry[i, j] * entry[k, j]
        lower_row = jnp.where(cols == j, lower_row, 0.0)
        for i in range(j + 1, size):
            lower_row = jnp.where(cols == i, entry[i, j], lower_row)
        factor_t = jnp.where(rows == j, lower_row, factor_t)
        row = jnp.where(cols == j, 1.0, 0.0)
        for k in range(j):
            row = row - entry[j, k] * inverse_rows[k]
        row = row * scale
        inverse_rows.append(row)
        inverse = jnp.where(rows == j, row, inverse)
    return factor_t, inverse


def second_product(fill, own, wide, wide_image, high, low):
    if fill:
        return all_filled(own, wide, wide_image, high, low)
    return apply_tensor(split_rows(wide_image[...]), high, low, 0, high.shape[1])


def spread_rows(block):
    beads = block.shape[1] // 4
    parts = [block[:, part * beads : (part + 1) * beads] for part in range(3)]
    empty = jnp.zeros(parts[0].shape, F32)
    rows = []
    for own in range(3):
        lanes = []
        for one, two in ((0, 0), (0, 1), (0, 2), (1, 1), (1, 2), (2, 2)):
            lanes.append(parts[two] if own == one else parts[one] if own == two else empty)
        rows.append(jnp.concatenate(lanes, axis=1))
    return jnp.concatenate(rows + [jnp.zeros(rows[0].shape, F32)], axis=0)


def backward_half(fill, own, wide, both, high, low, out):
    half = both.shape[0] // 2

    def add(start):
        first = matmul(both, high[...])
        sums = first[:half] + first[half:] + matmul(both[:half], low[...])
        out[:, pl.ds(start, high.shape[1])] = sums

    if not fill:
        add(0)
        return
    columns = target_columns(own[...])

    def body(index, carry):
        start = pl.multiple_of(index * high.shape[1], 128)
        for at in range(0, high.shape[1], 128):
            fill_tensor(columns, wide, pl.multiple_of(start + at, 128), high, low, at)
        add(start)
        return carry

    lax.fori_loop(0, wide.shape[1] // high.shape[1], body, 0)


def backward_stage(fill, own, image, one_wide, two_wide, *refs):
    if fill:
        one_sums, two_sums, high, low = refs
        tensors = [(high, low)] * 2
    else:
        *tensors, one_sums, two_sums = refs
        tensors = [tensors[:2], tensors[2:]]
    both = split_rows(spread_rows(image[...]))
    backward_half(fill, own, two_wide, both, *tensors[1], two_sums)
    backward_half(fill, own, one_wide, both, *tensors[0], one_sums)


def cross_stage(images, own_sums, other_sums, partials, wide_image):
    unpack(images, wide_image)
    left = split_rows(wide_image[...])
    right = split_rows(own_sums[...] + other_sums[...])
    half = left.shape[0] // 2
    first = matmul_nt(left, right[:half])
    sums = first[:half] + first[half:] + matmul_nt(left[:half], right[half:])
    partial = sums[:8, :8] + sums[8:16, 8:16] + sums[16:24, 16:24]
    line = jnp.concatenate([partial[row : row + 1] for row in range(8)], axis=1)
    partials[...] = jnp.broadcast_to(line[None], partials.shape)


def third_stage(size, fill, own, wide, *refs):
    refs = list(refs)
    if not fill:
        (high, low), refs = refs[:2], refs[2:]
    images, own_image, products, vectors, known, small, coefficients = refs[:7]
    if fill:
        high, low = refs[7:9]
    wide_image = refs[-1]
    unpack(images, wide_image)
    products[...] = second_product(fill, own[...], wide, wide_image, high, low)
    sums = wide_image[24:, :128]
    for at in range(128, wide_image.shape[1], 128):
        sums = sums + wide_image[24:, at : at + 128]
    width = own.shape[1] // 8
    sums = sum(sums[:, at : at + width] for at in range(width, 128, width)) + sums[:, :width]
    sums = sums / size
    noise_sums, cross_sums, image_sums = sums[:, :8], sums[:, 8:16], sums[:, 16:24]
    _, inverse_zero = cholesky(noise_sums)
    inverse_zero_t = inverse_zero.T
    cross_t = small_matmul(inverse_zero, cross_sums)
    cross = cross_t.T
    factor_t, inverse = cholesky(image_sums - small_matmul(cross, cross_t))
    factor_one_t = small_matmul(factor_t, inverse_zero_t)
    factor_one = factor_one_t.T
    first = small_matmul(inverse_zero, without_positions(own[...]))
    moved = small_matmul(inverse_zero, own_image[...])
    alpha = small_matmul(cross_t, inverse_zero_t)
    vectors[...] = small_matmul(inverse, own_image[...] - small_matmul(cross, first))
    known[...] = small_matmul(inverse, small_matmul(cross, moved)) + small_matmul(factor_one_t, first)
    image_moved = small_matmul(image_sums, inverse_zero_t)
    moved_image = small_matmul(inverse_zero, image_sums)
    known_sums = small_matmul(small_matmul(cross, alpha), cross_t)
    known_sums = known_sums - small_matmul(image_moved, cross_t) - small_matmul(cross, moved_image)
    first_sums = small_matmul(small_matmul(inverse_zero, noise_sums), inverse_zero_t)
    vector_first = small_matmul(inverse, cross - small_matmul(cross, first_sums))
    small[0] = inverse
    small[1] = inverse.T
    small[2] = known_sums
    small[3] = small_matmul(vector_first, factor_one)
    coefficients[0] = alpha
    coefficients[1] = factor_one


def fourth_stage(fill, own, wide, *refs):
    refs = list(refs)
    if not fill:
        (high, low), refs = refs[:2], refs[2:]
    images, before, known, small, shifted = refs[:5]
    if fill:
        high, low = refs[5:7]
    wide_image = refs[-1]
    unpack(images, wide_image)
    products = second_product(fill, own[...], wide, wide_image, high, low) + before[...]
    shifted[...] = small_matmul(small[0], assemble(products)) - known[...]


def last_kernel(size, vectors, shifted, both, small, partials, basis, residual, coefficients):
    beads = basis.shape[2]
    total = jnp.sum(partials[...], axis=0) / size
    sums = jnp.concatenate([total[:, 8 * k : 8 * k + 8] for k in range(8)], axis=0)
    alpha = small_matmul(small_matmul(small[0], sums + small[2]), small[1]) - small[3]
    block = vectors[...]
    left = shifted[...] - small_matmul(alpha.T, block)
    coefficients[0:2] = both[...]
    coefficients[2] = alpha
    for part in range(3):
        basis[part] = block[:, part * beads : (part + 1) * beads]
        residual[part] = left[:, part * beads : (part + 1) * beads]


def array(*shape, dtype=F32):
    return jax.ShapeDtypeStruct(shape, dtype)


def call(kernel, outs, scratch=(), **options):
    return pl.pallas_call(
        kernel,
        out_shape=outs,
        scratch_shapes=list(scratch),
        compiler_params=pltpu.CompilerParams(vmem_limit_bytes=VMEM),
        **options,
    )


def to_all(copies):
    rows, cols = lax.axis_size("row"), lax.axis_size("col")
    layers, middle = range(cols // 2), rows // 2
    chips = [(row, layer) for layer in layers for row in range(middle)]
    chips = chips + [(row, layer) for layer in reversed(layers) for row in range(middle, rows)]
    ring = [row * cols + 2 * layer + core for row, layer in chips for core in range(2)]
    return lax.all_to_all(copies, ("row", "col"), 0, 0, axis_index_groups=[ring], tiled=True)


def between_cores(block):
    cols = lax.axis_size("col")
    return lax.ppermute(block, "col", [(col, col ^ 1) for col in range(cols)])


def local(positions, noise):
    vecs, _, beads = noise.shape
    devices = lax.axis_size("row") * lax.axis_size("col")
    total = beads * devices // 2
    size = 3.0 * beads * devices
    keep = 2 * 2 * 2 * 6 * beads * total <= KEPT
    width = total if keep else min(total, CHUNK)
    block = array(vecs, 4 * beads)
    copies = array(devices // 2, 2, vecs, 2 * beads)
    products = array(4 * vecs, 6 * beads)
    wide, held_wide = array(4 * vecs, total), pltpu.VMEM((4 * vecs, total), F32)
    kept = [array(6 * beads, width, dtype=BF16)] * 2 if keep else []
    held = [] if keep else [pltpu.VMEM((6 * beads, width), BF16)] * 2

    rows = noise.transpose(1, 0, 2).reshape(3 * vecs, beads)
    rows = jnp.concatenate([rows, jnp.pad(positions, ((0, vecs - 3), (0, 0)))], axis=0)
    own, own_copies = call(pack_kernel, [block, copies])(rows)
    one = to_all(own_copies.reshape((-1,) + own_copies.shape[2:]))
    two = between_cores(one)
    partial, one_wide, *one_tensor = call(
        functools.partial(first_stage, False), [products, wide] + kept, held
    )(own, one)
    image, images, two_wide, *two_tensor = call(
        functools.partial(first_stage, True), [block, copies, wide] + kept, held
    )(own, two, partial)
    own_sums, other_sums = call(functools.partial(backward_stage, not keep), [wide, wide], held)(
        own, image, one_wide, two_wide, *one_tensor, *two_tensor
    )
    other_sums = between_cores(other_sums)
    one = to_all(images.reshape((-1,) + images.shape[2:]))
    partials = call(cross_stage, array(devices, 1, vecs * vecs), [held_wide])(one, own_sums, other_sums)
    one, partials = lax.optimization_barrier((one, partials))
    partials = to_all(partials)
    two = between_cores(one)
    partial, vectors, known, small, both = call(
        functools.partial(third_stage, size, not keep),
        [products, block, block, array(4, vecs, vecs), array(2, vecs, vecs)],
        held + [held_wide],
    )(own, one_wide, *one_tensor, one, image)
    shifted = call(functools.partial(fourth_stage, not keep), block, held + [held_wide])(
        own, two_wide, *two_tensor, two, partial, known, small
    )
    basis, residual, coefficients = call(
        functools.partial(last_kernel, size),
        [array(3, vecs, beads), array(3, vecs, beads), array(3, vecs, vecs)],
    )(vectors, shifted, both, small, partials)
    return (basis.transpose(1, 0, 2), residual.transpose(1, 0, 2), coefficients)


def solution(mesh):
    return jax.shard_map(
        local,
        mesh=mesh,
        in_specs=(P(None, ("row", "col")), P(None, None, ("row", "col"))),
        out_specs=(P(None, None, ("row", "col")), P(None, None, ("row", "col")), P()),
        check_vma=False,
    )
```

```python
import functools

import jax
import jax.numpy as jnp
from jax import lax
from jax.experimental import pallas as pl
from jax.experimental.pallas import tpu as pltpu
from jax.sharding import PartitionSpec as P

CHUNK = 1024
KEPT = 2 * 1024 * 1024
VMEM = 16 * 1024 * 1024
F32 = jnp.float32
BF16 = jnp.bfloat16


def copy_halves(block, copies, last=None):
    beads = block.shape[1] // 4
    middle = beads // 2
    for core in range(2):
        parts = [block[:, part * beads + core * middle : part * beads + (core + 1) * middle] for part in range(4)]
        if last is not None:
            parts[3] = last
        half = jnp.concatenate(parts, axis=1)
        copies[:, core] = jnp.broadcast_to(half[None], (copies.shape[0],) + half.shape)


def pack_kernel(rows, block, copies):
    vecs = block.shape[0]
    flat = jnp.concatenate([rows[part * vecs : (part + 1) * vecs] for part in range(4)], axis=1)
    block[...] = flat
    copy_halves(flat, copies)


def split_two(value):
    high = value.astype(BF16)
    return high, (value - high.astype(F32)).astype(BF16)


def matmul_nt(left, right, precision=None):
    return lax.dot_general(
        left, right, (((1,), (1,)), ((), ())), precision=precision, preferred_element_type=F32
    )


def matmul(left, right):
    return lax.dot_general(left, right, (((1,), (0,)), ((), ())), preferred_element_type=F32)


def small_matmul(left, right):
    total = left[:, 0:1] * right[0:1, :]
    for k in range(1, left.shape[1]):
        total = total + left[:, k : k + 1] * right[k : k + 1, :]
    return total


def unpack(blocks, wide):
    count, vecs, lanes = blocks.shape
    width = lanes // 4
    for at in range(0, count, 4):
        four = [blocks[at + index] for index in range(4)]
        for part in range(4):
            wide[part * vecs : (part + 1) * vecs, pl.ds(at * width, 4 * width)] = jnp.concatenate(
                [block[:, part * width : (part + 1) * width] for block in four], axis=1
            )


def target_columns(own):
    beads = own.shape[1] // 4
    targets = own[:, 3 * beads :].T
    return [jnp.broadcast_to(targets[:, axis : axis + 1], (beads, 128)) for axis in range(3)]


def fill_tensor(columns, wide, start, high, low, at):
    beads = columns[0].shape[0]
    block = 32 if beads % 32 == 0 else beads
    sources = [wide[24 + axis : 25 + axis, pl.ds(start, 128)] for axis in range(3)]
    to = pl.ds(at, 128)
    for row in range(0, beads, block):
        moved = [columns[axis][row : row + block] - sources[axis] for axis in range(3)]
        square = moved[0] * moved[0] + moved[1] * moved[1] + moved[2] * moved[2]
        square = jnp.maximum(square, 1e-12)
        inverse = lax.rsqrt(square)
        inverse_sq = inverse * inverse
        near = square < 4.0
        iso = inverse * jnp.where(near, square * (inverse - 9.0 / 32.0), 0.75 + 0.5 * inverse_sq)
        along = inverse * jnp.where(near, 3.0 / 32.0, inverse_sq * (0.75 - 1.5 * inverse_sq))
        scaled = [along * item for item in moved]
        parts = [
            iso + scaled[0] * moved[0],
            scaled[0] * moved[1],
            scaled[0] * moved[2],
            iso + scaled[1] * moved[1],
            scaled[1] * moved[2],
            iso + scaled[2] * moved[2],
        ]
        for part, value in enumerate(parts):
            upper, lower = split_two(value)
            rows = slice(part * beads + row, part * beads + row + block)
            high[rows, to] = upper
            low[rows, to] = lower


def apply_tensor(both, high, low, at, step):
    lanes = pl.ds(at, step)
    half = both.shape[0] // 2
    first = matmul_nt(both, high[:, lanes])
    return first[:half] + first[half:] + matmul_nt(both[:half], low[:, lanes])


def split_rows(*values):
    highs, lows = zip(*[split_two(value) for value in values])
    return jnp.concatenate(highs + lows, axis=0)


def inner(both):
    half = both.shape[0] // 2
    first = matmul_nt(both, both[:half])
    return first[:half] + first[half:] + matmul_nt(both[:half], both[half:])


def assemble(products):
    beads = products.shape[1] // 6

    def part(row, component):
        return products[8 * row : 8 * row + 8, component * beads : (component + 1) * beads]

    x = part(0, 0) + part(1, 1) + part(2, 2)
    y = part(0, 1) + part(1, 3) + part(2, 4)
    z = part(0, 2) + part(1, 4) + part(2, 5)
    return jnp.concatenate([x, y, z, jnp.zeros(x.shape, F32)], axis=1)


def filled_product(columns, source, wide, start, high, low):
    width = high.shape[1]
    products = jnp.zeros((32, high.shape[0]), F32)
    steps = [(at, min(256, width - at)) for at in range(0, width, 256)]
    vectors = [split_rows(wide[:, pl.ds(pl.multiple_of(start + at, 128), step)]) for at, step in steps]
    for index in range(len(steps) + 1):
        if index < len(steps):
            at, step = steps[index]
            for part in range(at, at + step, 128):
                fill_tensor(columns, source, pl.multiple_of(start + part, 128), high, low, part)
        if index > 0:
            products = products + apply_tensor(vectors[index - 1], high, low, *steps[index - 1])
    return products


def all_filled(own, source, wide, high, low):
    columns = target_columns(own)
    width = high.shape[1]
    chunk = lambda start: filled_product(columns, source, wide, start, high, low)
    if wide.shape[1] == width:
        return chunk(0)
    body = lambda index, total: total + chunk(index * width)
    return lax.fori_loop(1, wide.shape[1] // width, body, chunk(0))


def without_positions(block):
    lanes = lax.broadcasted_iota(jnp.int32, block.shape, 1)
    return jnp.where(lanes < block.shape[1] // 4 * 3, block, 0.0)


def first_stage(last, own, blocks, *refs):
    refs = list(refs)
    if last:
        before, image, copies, wide, high, low = refs
    else:
        out, wide, high, low = refs
    unpack(blocks, wide)
    products = all_filled(own[...], wide, wide, high, low)
    if not last:
        out[...] = products
        return
    block = assemble(products + before[...])
    image[...] = block
    sums = inner(split_rows(without_positions(own[...]), block))
    empty = jnp.zeros((8, block.shape[1] // 8 - 24), F32)
    copy_halves(block, copies, jnp.concatenate([sums[:8], sums[8:, 8:], empty], axis=1))


def cholesky(matrix):
    size = matrix.shape[0]
    shape = (size, size)
    rows = lax.broadcasted_iota(jnp.int32, shape, 0)
    cols = lax.broadcasted_iota(jnp.int32, shape, 1)
    entry = {}
    for j in range(size):
        column = jnp.broadcast_to(matrix[:, j : j + 1], shape)
        for i in range(j, size):
            entry[i, j] = jnp.broadcast_to(column[i : i + 1, :], shape)
    factor_t = jnp.zeros(shape, F32)
    inverse = jnp.zeros(shape, F32)
    inverse_rows = []
    for j in range(size):
        scale = lax.rsqrt(entry[j, j])
        lower_row = entry[j, j] * scale
        entry[j, j] = scale
        for i in range(j + 1, size):
            entry[i, j] = entry[i, j] * scale
        for i in range(j + 1, size):
            for k in range(j + 1, i + 1):
                entry[i, k] = entry[i, k] - entry[i, j] * entry[k, j]
        lower_row = jnp.where(cols == j, lower_row, 0.0)
        for i in range(j + 1, size):
            lower_row = jnp.where(cols == i, entry[i, j], lower_row)
        factor_t = jnp.where(rows == j, lower_row, factor_t)
        row = jnp.where(cols == j, 1.0, 0.0)
        for k in range(j):
            row = row - entry[j, k] * inverse_rows[k]
        row = row * scale
        inverse_rows.append(row)
        inverse = jnp.where(rows == j, row, inverse)
    return factor_t, inverse


def second_product(fill, own, wide, wide_image, high, low):
    if fill:
        return all_filled(own, wide, wide_image, high, low)
    return apply_tensor(split_rows(wide_image[...]), high, low, 0, high.shape[1])


def spread_rows(block):
    beads = block.shape[1] // 4
    parts = [block[:, part * beads : (part + 1) * beads] for part in range(3)]
    empty = jnp.zeros(parts[0].shape, F32)
    rows = []
    for own in range(3):
        lanes = []
        for one, two in ((0, 0), (0, 1), (0, 2), (1, 1), (1, 2), (2, 2)):
            lanes.append(parts[two] if own == one else parts[one] if own == two else empty)
        rows.append(jnp.concatenate(lanes, axis=1))
    return jnp.concatenate(rows + [jnp.zeros(rows[0].shape, F32)], axis=0)


def backward_half(own, wide, both, high, low, out):
    half, width = both.shape[0] // 2, high.shape[1]
    columns = target_columns(own[...])

    def chunk(start):
        for at in range(0, width, 128):
            fill_tensor(columns, wide, pl.multiple_of(start + at, 128), high, low, at)
        for at in range(0, width, 256):
            lanes = pl.ds(at, min(256, width - at))
            first = matmul(both, high[:, lanes])
            sums = first[:half] + first[half:] + matmul(both[:half], low[:, lanes])
            out[:, pl.ds(pl.multiple_of(start + at, 128), sums.shape[1])] = sums

    if wide.shape[1] == width:
        chunk(0)
        return

    def body(index, carry):
        chunk(pl.multiple_of(index * width, 128))
        return carry

    lax.fori_loop(0, wide.shape[1] // width, body, 0)


def backward_stage(own, image, one_wide, two_wide, one_sums, two_sums, *tensors):
    both = split_rows(spread_rows(image[...]))
    backward_half(own, two_wide, both, *tensors[-2:], two_sums)
    backward_half(own, one_wide, both, *tensors[:2], one_sums)


def cross_stage(images, own_sums, other_sums, partials, wide_image):
    unpack(images, wide_image)
    left = split_rows(wide_image[...])
    right = split_rows(own_sums[...] + other_sums[...])
    half = left.shape[0] // 2
    first = matmul_nt(left, right[:half])
    sums = first[:half] + first[half:] + matmul_nt(left[:half], right[half:])
    partial = sums[:8, :8] + sums[8:16, 8:16] + sums[16:24, 16:24]
    line = jnp.concatenate([partial[row : row + 1] for row in range(8)], axis=1)
    partials[...] = jnp.broadcast_to(line[None], partials.shape)


def third_stage(size, fill, own, wide, *refs):
    refs = list(refs)
    if not fill:
        (high, low), refs = refs[:2], refs[2:]
    images, own_image, products, vectors, known, small, coefficients = refs[:7]
    if fill:
        high, low = refs[7:9]
    wide_image = refs[-1]
    unpack(images, wide_image)
    products[...] = second_product(fill, own[...], wide, wide_image, high, low)
    sums = wide_image[24:, :128]
    for at in range(128, wide_image.shape[1], 128):
        sums = sums + wide_image[24:, at : at + 128]
    width = own.shape[1] // 8
    sums = sum(sums[:, at : at + width] for at in range(width, 128, width)) + sums[:, :width]
    sums = sums / size
    noise_sums, cross_sums, image_sums = sums[:, :8], sums[:, 8:16], sums[:, 16:24]
    _, inverse_zero = cholesky(noise_sums)
    inverse_zero_t = inverse_zero.T
    cross_t = small_matmul(inverse_zero, cross_sums)
    cross = cross_t.T
    factor_t, inverse = cholesky(image_sums - small_matmul(cross, cross_t))
    factor_one_t = small_matmul(factor_t, inverse_zero_t)
    factor_one = factor_one_t.T
    first = small_matmul(inverse_zero, without_positions(own[...]))
    moved = small_matmul(inverse_zero, own_image[...])
    alpha = small_matmul(cross_t, inverse_zero_t)
    vectors[...] = small_matmul(inverse, own_image[...] - small_matmul(cross, first))
    known[...] = small_matmul(inverse, small_matmul(cross, moved)) + small_matmul(factor_one_t, first)
    image_moved = small_matmul(image_sums, inverse_zero_t)
    moved_image = small_matmul(inverse_zero, image_sums)
    known_sums = small_matmul(small_matmul(cross, alpha), cross_t)
    known_sums = known_sums - small_matmul(image_moved, cross_t) - small_matmul(cross, moved_image)
    first_sums = small_matmul(small_matmul(inverse_zero, noise_sums), inverse_zero_t)
    vector_first = small_matmul(inverse, cross - small_matmul(cross, first_sums))
    small[0] = inverse
    small[1] = inverse.T
    small[2] = known_sums
    small[3] = small_matmul(vector_first, factor_one)
    coefficients[0] = alpha
    coefficients[1] = factor_one


def fourth_stage(own, wide, images, before, known, small, shifted, high, low, wide_image):
    unpack(images, wide_image)
    products = all_filled(own[...], wide, wide_image, high, low) + before[...]
    shifted[...] = small_matmul(small[0], assemble(products)) - known[...]


def last_kernel(size, vectors, shifted, both, small, partials, basis, residual, coefficients):
    beads = basis.shape[2]
    total = jnp.sum(partials[...], axis=0) / size
    sums = jnp.concatenate([total[:, 8 * k : 8 * k + 8] for k in range(8)], axis=0)
    alpha = small_matmul(small_matmul(small[0], sums + small[2]), small[1]) - small[3]
    block = vectors[...]
    left = shifted[...] - small_matmul(alpha.T, block)
    coefficients[0:2] = both[...]
    coefficients[2] = alpha
    for part in range(3):
        basis[part] = block[:, part * beads : (part + 1) * beads]
        residual[part] = left[:, part * beads : (part + 1) * beads]


def array(*shape, dtype=F32):
    return jax.ShapeDtypeStruct(shape, dtype)


def call(kernel, outs, scratch=(), **options):
    return pl.pallas_call(
        kernel,
        out_shape=outs,
        scratch_shapes=list(scratch),
        compiler_params=pltpu.CompilerParams(vmem_limit_bytes=VMEM),
        **options,
    )


def to_all(copies):
    rows, cols = lax.axis_size("row"), lax.axis_size("col")
    layers, middle = range(cols // 2), rows // 2
    chips = [(row, layer) for layer in layers for row in range(middle)]
    chips = chips + [(row, layer) for layer in reversed(layers) for row in range(middle, rows)]
    ring = [row * cols + 2 * layer + core for row, layer in chips for core in range(2)]
    return lax.all_to_all(copies, ("row", "col"), 0, 0, axis_index_groups=[ring], tiled=True)


def between_cores(block):
    cols = lax.axis_size("col")
    return lax.ppermute(block, "col", [(col, col ^ 1) for col in range(cols)])


def local(positions, noise):
    vecs, _, beads = noise.shape
    devices = lax.axis_size("row") * lax.axis_size("col")
    total = beads * devices // 2
    size = 3.0 * beads * devices
    keep = 2 * 2 * 6 * beads * total <= KEPT
    width = total if keep else min(total, CHUNK)
    block = array(vecs, 4 * beads)
    copies = array(devices // 2, 2, vecs, 2 * beads)
    products = array(4 * vecs, 6 * beads)
    wide, held_wide = array(4 * vecs, total), pltpu.VMEM((4 * vecs, total), F32)
    kept = [array(6 * beads, width, dtype=BF16)] * 2 if keep else []
    held = [pltpu.VMEM((6 * beads, width), BF16)] * 2

    rows = noise.transpose(1, 0, 2).reshape(3 * vecs, beads)
    rows = jnp.concatenate([rows, jnp.pad(positions, ((0, vecs - 3), (0, 0)))], axis=0)
    own, own_copies = call(pack_kernel, [block, copies])(rows)
    one = to_all(own_copies.reshape((-1,) + own_copies.shape[2:]))
    two = between_cores(one)
    partial, one_wide = call(functools.partial(first_stage, False), [products, wide], held)(own, one)
    image, images, two_wide = call(functools.partial(first_stage, True), [block, copies, wide], held)(
        own, two, partial
    )
    own_sums, other_sums, *one_tensor = call(backward_stage, [wide, wide] + kept, held)(
        own, image, one_wide, two_wide
    )
    other_sums = between_cores(other_sums)
    one = to_all(images.reshape((-1,) + images.shape[2:]))
    partials = call(cross_stage, array(devices, 1, vecs * vecs), [held_wide])(one, own_sums, other_sums)
    one, partials = lax.optimization_barrier((one, partials))
    partials = to_all(partials)
    two = between_cores(one)
    partial, vectors, known, small, both = call(
        functools.partial(third_stage, size, not keep),
        [products, block, block, array(4, vecs, vecs), array(2, vecs, vecs)],
        (held if not keep else []) + [held_wide],
    )(own, one_wide, *one_tensor, one, image)
    shifted = call(fourth_stage, block, held + [held_wide])(own, two_wide, two, partial, known, small)
    basis, residual, coefficients = call(
        functools.partial(last_kernel, size),
        [array(3, vecs, beads), array(3, vecs, beads), array(3, vecs, vecs)],
    )(vectors, shifted, both, small, partials)
    return (basis.transpose(1, 0, 2), residual.transpose(1, 0, 2), coefficients)


def solution(mesh):
    return jax.shard_map(
        local,
        mesh=mesh,
        in_specs=(P(None, ("row", "col")), P(None, None, ("row", "col"))),
        out_specs=(P(None, None, ("row", "col")), P(None, None, ("row", "col")), P()),
        check_vma=False,
    )
```

```python
import functools

import jax
import jax.numpy as jnp
from jax import lax
from jax.experimental import pallas as pl
from jax.experimental.pallas import tpu as pltpu
from jax.sharding import PartitionSpec as P

CHUNK = 1024
KEPT = 8 * 1024 * 1024
F32 = jnp.float32
BF16 = jnp.bfloat16


def copy_halves(block, copies, last=None):
    beads = block.shape[1] // 4
    middle = beads // 2
    for core in range(2):
        parts = [block[:, part * beads + core * middle : part * beads + (core + 1) * middle] for part in range(4)]
        if last is not None:
            parts[3] = last
        half = jnp.concatenate(parts, axis=1)
        copies[:, core] = jnp.broadcast_to(half[None], (copies.shape[0],) + half.shape)


def pack_kernel(rows, block, copies):
    vecs = block.shape[0]
    flat = jnp.concatenate([rows[part * vecs : (part + 1) * vecs] for part in range(4)], axis=1)
    block[...] = flat
    copy_halves(flat, copies)


def split_two(value):
    high = value.astype(BF16)
    return high, (value - high.astype(F32)).astype(BF16)


def matmul_nt(left, right, precision=None):
    return lax.dot_general(
        left, right, (((1,), (1,)), ((), ())), precision=precision, preferred_element_type=F32
    )


def small_matmul(left, right):
    total = left[:, 0:1] * right[0:1, :]
    for k in range(1, left.shape[1]):
        total = total + left[:, k : k + 1] * right[k : k + 1, :]
    return total


def unpack(blocks, wide):
    count, vecs, lanes = blocks.shape
    width = lanes // 4
    for at in range(0, count, 4):
        four = [blocks[at + index] for index in range(4)]
        for part in range(4):
            wide[part * vecs : (part + 1) * vecs, pl.ds(at * width, 4 * width)] = jnp.concatenate(
                [block[:, part * width : (part + 1) * width] for block in four], axis=1
            )


def target_columns(own):
    beads = own.shape[1] // 4
    targets = own[:, 3 * beads :].T
    return [jnp.broadcast_to(targets[:, axis : axis + 1], (beads, 128)) for axis in range(3)]


def tensor(columns, wide, start):
    moved = [columns[axis] - wide[24 + axis : 25 + axis, pl.ds(start, 128)] for axis in range(3)]
    square = moved[0] * moved[0] + moved[1] * moved[1] + moved[2] * moved[2]
    square = jnp.maximum(square, 1e-12)
    inverse = lax.rsqrt(square)
    inverse_sq = inverse * inverse
    near = square < 4.0
    iso = inverse * jnp.where(near, square * (inverse - 9.0 / 32.0), 0.75 + 0.5 * inverse_sq)
    along = inverse * jnp.where(near, 3.0 / 32.0, inverse_sq * (0.75 - 1.5 * inverse_sq))
    scaled = [along * item for item in moved]
    parts = [
        iso + scaled[0] * moved[0],
        scaled[0] * moved[1],
        scaled[0] * moved[2],
        iso + scaled[1] * moved[1],
        scaled[1] * moved[2],
        iso + scaled[2] * moved[2],
    ]
    highs, lows = zip(*[split_two(value) for value in parts])
    return jnp.concatenate(highs, axis=0), jnp.concatenate(lows, axis=0)


def apply_tensor(both, high, low):
    half = both.shape[0] // 2
    first = matmul_nt(both, high)
    return first[:half] + first[half:] + matmul_nt(both[:half], low)


def split_rows(*values):
    highs, lows = zip(*[split_two(value) for value in values])
    return jnp.concatenate(highs + lows, axis=0)


def inner(both):
    half = both.shape[0] // 2
    first = matmul_nt(both, both[:half])
    return first[:half] + first[half:] + matmul_nt(both[:half], both[half:])


def assemble(products):
    beads = products.shape[1] // 6

    def part(row, component):
        return products[8 * row : 8 * row + 8, component * beads : (component + 1) * beads]

    x = part(0, 0) + part(1, 1) + part(2, 2)
    y = part(0, 1) + part(1, 3) + part(2, 4)
    z = part(0, 2) + part(1, 4) + part(2, 5)
    return jnp.concatenate([x, y, z, jnp.zeros(x.shape, F32)], axis=1)


def filled_product(columns, source, wide, start, high, low):
    width = high.shape[1]
    products = jnp.zeros((32, high.shape[0]), F32)
    for at in range(0, width, 256):
        step = min(256, width - at)
        lanes = pl.ds(at, step)
        both = split_rows(wide[:, pl.ds(pl.multiple_of(start + at, 128), step)])
        pieces = [
            tensor(columns, source, pl.multiple_of(start + part, 128)) for part in range(at, at + step, 128)
        ]
        upper, lower = [jnp.concatenate(piece, axis=1) for piece in zip(*pieces)]
        high[:, lanes] = upper
        low[:, lanes] = lower
        products = products + apply_tensor(both, upper, lower)
    return products


def all_filled(own, source, wide, high, low):
    columns = target_columns(own)
    width = high.shape[1]
    chunk = lambda start: filled_product(columns, source, wide, start, high, low)
    if wide.shape[1] == width:
        return chunk(0)
    body = lambda index, total: total + chunk(index * width)
    return lax.fori_loop(1, wide.shape[1] // width, body, chunk(0))


def without_positions(block):
    lanes = lax.broadcasted_iota(jnp.int32, block.shape, 1)
    return jnp.where(lanes < block.shape[1] // 4 * 3, block, 0.0)


def first_stage(last, own, blocks, *refs):
    refs = list(refs)
    if last:
        before, image, copies, wide, high, low = refs
    else:
        out, wide, high, low = refs
    unpack(blocks, wide)
    products = all_filled(own[...], wide, wide, high, low)
    if not last:
        out[...] = products
        return
    block = assemble(products + before[...])
    image[...] = block
    sums = inner(split_rows(without_positions(own[...]), block))
    empty = jnp.zeros((8, block.shape[1] // 8 - 24), F32)
    copy_halves(block, copies, jnp.concatenate([sums[:8], sums[8:, 8:], empty], axis=1))


def cholesky(matrix):
    size = matrix.shape[0]
    shape = (size, size)
    rows = lax.broadcasted_iota(jnp.int32, shape, 0)
    cols = lax.broadcasted_iota(jnp.int32, shape, 1)
    entry = {}
    for j in range(size):
        column = jnp.broadcast_to(matrix[:, j : j + 1], shape)
        for i in range(j, size):
            entry[i, j] = jnp.broadcast_to(column[i : i + 1, :], shape)
    factor_t = jnp.zeros(shape, F32)
    inverse = jnp.zeros(shape, F32)
    inverse_rows = []
    for j in range(size):
        scale = lax.rsqrt(entry[j, j])
        lower_row = entry[j, j] * scale
        entry[j, j] = scale
        for i in range(j + 1, size):
            entry[i, j] = entry[i, j] * scale
        for i in range(j + 1, size):
            for k in range(j + 1, i + 1):
                entry[i, k] = entry[i, k] - entry[i, j] * entry[k, j]
        lower_row = jnp.where(cols == j, lower_row, 0.0)
        for i in range(j + 1, size):
            lower_row = jnp.where(cols == i, entry[i, j], lower_row)
        factor_t = jnp.where(rows == j, lower_row, factor_t)
        row = jnp.where(cols == j, 1.0, 0.0)
        for k in range(j):
            row = row - entry[j, k] * inverse_rows[k]
        row = row * scale
        inverse_rows.append(row)
        inverse = jnp.where(rows == j, row, inverse)
    return factor_t, inverse


def second_product(fill, own, wide, wide_image, high, low):
    if fill:
        return all_filled(own, wide, wide_image, high, low)
    return apply_tensor(split_rows(wide_image[...]), high[...], low[...])


def third_stage(size, fill, own, wide, *refs):
    refs = list(refs)
    if not fill:
        (high, low), refs = refs[:2], refs[2:]
    images, own_image, products, vectors, known, small, coefficients = refs[:7]
    if fill:
        high, low = refs[7:9]
    wide_image = refs[-1]
    unpack(images, wide_image)
    products[...] = second_product(fill, own[...], wide, wide_image, high, low)
    sums = wide_image[24:, :128]
    for at in range(128, wide_image.shape[1], 128):
        sums = sums + wide_image[24:, at : at + 128]
    width = own.shape[1] // 8
    sums = sum(sums[:, at : at + width] for at in range(width, 128, width)) + sums[:, :width]
    sums = sums / size
    _, inverse_zero = cholesky(sums[:, :8])
    inverse_zero_t = inverse_zero.T
    cross_t = small_matmul(inverse_zero, sums[:, 8:16])
    cross = cross_t.T
    factor_t, inverse = cholesky(sums[:, 16:24] - small_matmul(cross, cross_t))
    factor_one_t = small_matmul(factor_t, inverse_zero_t)
    first = small_matmul(inverse_zero, without_positions(own[...]))
    moved = small_matmul(inverse_zero, own_image[...])
    vectors[...] = small_matmul(inverse, own_image[...] - small_matmul(cross, first))
    known[...] = small_matmul(inverse, small_matmul(cross, moved)) + small_matmul(factor_one_t, first)
    small[...] = inverse
    coefficients[0] = small_matmul(cross_t, inverse_zero_t)
    coefficients[1] = factor_one_t.T


def fourth_stage(fill, own, wide, *refs):
    refs = list(refs)
    if not fill:
        (high, low), refs = refs[:2], refs[2:]
    images, before, vectors_in, known, small, shifted, partials = refs[:7]
    if fill:
        high, low = refs[7:9]
    wide_image = refs[-1]
    unpack(images, wide_image)
    products = second_product(fill, own[...], wide, wide_image, high, low) + before[...]
    vectors = vectors_in[...]
    shift = small_matmul(small[...], assemble(products)) - known[...]
    shifted[...] = shift
    (vector_high, vector_low), (shift_high, shift_low) = split_two(vectors), split_two(shift)
    partial = matmul_nt(vector_high, shift_high) + (
        matmul_nt(vector_high, shift_low) + matmul_nt(vector_low, shift_high)
    )
    line = jnp.concatenate([partial[row : row + 1] for row in range(8)], axis=1)
    partials[...] = jnp.broadcast_to(line[None], partials.shape)


def last_kernel(size, vectors, shifted, both, partials, basis, residual, coefficients):
    beads = basis.shape[2]
    width = partials.shape[2]
    total = jnp.sum(partials[...], axis=0) / size
    spread = jnp.broadcast_to(total, (8, width))
    rows = lax.broadcasted_iota(jnp.int32, spread.shape, 0)
    cols = lax.broadcasted_iota(jnp.int32, spread.shape, 1)
    block = vectors[...]
    left = shifted[...]
    transposed = jnp.where(cols % 8 == rows, spread, 0.0)
    for k in range(8):
        column = jnp.sum(jnp.where(cols // 8 == k, transposed, 0.0), axis=1, keepdims=True)
        left = left - column * block[k : k + 1, :]
    coefficients[0:2] = both[...]
    for k in range(8):
        coefficients[2, k : k + 1, :] = total[:, 8 * k : 8 * k + 8]
    for part in range(3):
        basis[part] = block[:, part * beads : (part + 1) * beads]
        residual[part] = left[:, part * beads : (part + 1) * beads]


def array(*shape, dtype=F32):
    return jax.ShapeDtypeStruct(shape, dtype)


def call(kernel, outs, scratch=(), **options):
    return pl.pallas_call(
        kernel,
        out_shape=outs,
        scratch_shapes=list(scratch),
        compiler_params=pltpu.CompilerParams(vmem_limit_bytes=48 * 1024 * 1024),
        **options,
    )


def to_all(copies):
    rows, cols = lax.axis_size("row"), lax.axis_size("col")
    layers, middle = range(cols // 2), rows // 2
    chips = [(row, layer) for layer in layers for row in range(middle)]
    chips = chips + [(row, layer) for layer in reversed(layers) for row in range(middle, rows)]
    ring = [row * cols + 2 * layer + core for row, layer in chips for core in range(2)]
    return lax.all_to_all(copies, ("row", "col"), 0, 0, axis_index_groups=[ring], tiled=True)


def gather(copies):
    mine = to_all(copies.reshape((-1,) + copies.shape[2:]))
    cols = lax.axis_size("col")
    return mine, lax.ppermute(mine, "col", [(col, col ^ 1) for col in range(cols)])


def local(positions, noise):
    vecs, _, beads = noise.shape
    devices = lax.axis_size("row") * lax.axis_size("col")
    total = beads * devices // 2
    size = 3.0 * beads * devices
    keep = 2 * 2 * 2 * 6 * beads * total <= KEPT
    width = total if keep else min(total, CHUNK)
    block = array(vecs, 4 * beads)
    copies = array(devices // 2, 2, vecs, 2 * beads)
    products = array(4 * vecs, 6 * beads)
    wide, held_wide = array(4 * vecs, total), pltpu.VMEM((4 * vecs, total), F32)
    kept = [array(6 * beads, width, dtype=BF16)] * 2 if keep else []
    held = [] if keep else [pltpu.VMEM((6 * beads, width), BF16)] * 2

    rows = noise.transpose(1, 0, 2).reshape(3 * vecs, beads)
    rows = jnp.concatenate([rows, jnp.pad(positions, ((0, vecs - 3), (0, 0)))], axis=0)
    own, own_copies = call(pack_kernel, [block, copies])(rows)
    one, two = gather(own_copies)
    partial, one_wide, *one_tensor = call(
        functools.partial(first_stage, False), [products, wide] + kept, held
    )(own, one)
    image, images, two_wide, *two_tensor = call(
        functools.partial(first_stage, True), [block, copies, wide] + kept, held
    )(own, two, partial)
    one, two = gather(images)
    partial, vectors, known, small, both = call(
        functools.partial(third_stage, size, not keep),
        [products, block, block, array(vecs, vecs), array(2, vecs, vecs)],
        held + [held_wide],
    )(own, one_wide, *one_tensor, one, image)
    shifted, partials = call(
        functools.partial(fourth_stage, not keep), [block, array(devices, 1, vecs * vecs)], held + [held_wide]
    )(own, two_wide, *two_tensor, two, partial, vectors, known, small)
    partials = to_all(partials)
    basis, residual, coefficients = call(
        functools.partial(last_kernel, size),
        [array(3, vecs, beads), array(3, vecs, beads), array(3, vecs, vecs)],
    )(vectors, shifted, both, partials)
    return (basis.transpose(1, 0, 2), residual.transpose(1, 0, 2), coefficients)


def solution(mesh):
    return jax.shard_map(
        local,
        mesh=mesh,
        in_specs=(P(None, ("row", "col")), P(None, None, ("row", "col"))),
        out_specs=(P(None, None, ("row", "col")), P(None, None, ("row", "col")), P()),
        check_vma=False,
    )
```

```python
import functools

import jax
import jax.numpy as jnp
from jax import lax
from jax.experimental import pallas as pl
from jax.experimental.pallas import tpu as pltpu
from jax.sharding import PartitionSpec as P

CHUNK = 1024
KEPT = 8 * 1024 * 1024
F32 = jnp.float32
BF16 = jnp.bfloat16


def copy_halves(block, copies, last=None):
    beads = block.shape[1] // 4
    middle = beads // 2
    for core in range(2):
        parts = [block[:, part * beads + core * middle : part * beads + (core + 1) * middle] for part in range(4)]
        if last is not None:
            parts[3] = last
        half = jnp.concatenate(parts, axis=1)
        copies[:, core] = jnp.broadcast_to(half[None], (copies.shape[0],) + half.shape)


def pack_kernel(rows, block, copies):
    vecs = block.shape[0]
    flat = jnp.concatenate([rows[part * vecs : (part + 1) * vecs] for part in range(4)], axis=1)
    block[...] = flat
    copy_halves(flat, copies)


def split_two(value):
    high = value.astype(BF16)
    return high, (value - high.astype(F32)).astype(BF16)


def matmul_nt(left, right, precision=None):
    return lax.dot_general(
        left, right, (((1,), (1,)), ((), ())), precision=precision, preferred_element_type=F32
    )


def small_matmul(left, right):
    total = left[:, 0:1] * right[0:1, :]
    for k in range(1, left.shape[1]):
        total = total + left[:, k : k + 1] * right[k : k + 1, :]
    return total


def unpack(blocks, wide):
    count, vecs, lanes = blocks.shape
    width = lanes // 4
    for at in range(0, count, 4):
        four = [blocks[at + index] for index in range(4)]
        for part in range(4):
            wide[part * vecs : (part + 1) * vecs, pl.ds(at * width, 4 * width)] = jnp.concatenate(
                [block[:, part * width : (part + 1) * width] for block in four], axis=1
            )


def target_columns(own):
    beads = own.shape[1] // 4
    targets = own[:, 3 * beads :].T
    return [jnp.broadcast_to(targets[:, axis : axis + 1], (beads, 128)) for axis in range(3)]


def tensor(columns, wide, start):
    moved = [columns[axis] - wide[24 + axis : 25 + axis, pl.ds(start, 128)] for axis in range(3)]
    square = moved[0] * moved[0] + moved[1] * moved[1] + moved[2] * moved[2]
    square = jnp.maximum(square, 1e-12)
    inverse = lax.rsqrt(square)
    inverse_sq = inverse * inverse
    near = square < 4.0
    iso = inverse * jnp.where(near, square * (inverse - 9.0 / 32.0), 0.75 + 0.5 * inverse_sq)
    along = inverse * jnp.where(near, 3.0 / 32.0, inverse_sq * (0.75 - 1.5 * inverse_sq))
    scaled = [along * item for item in moved]
    parts = [
        iso + scaled[0] * moved[0],
        scaled[0] * moved[1],
        scaled[0] * moved[2],
        iso + scaled[1] * moved[1],
        scaled[1] * moved[2],
        iso + scaled[2] * moved[2],
    ]
    highs, lows = zip(*[split_two(value) for value in parts])
    return jnp.concatenate(highs, axis=0), jnp.concatenate(lows, axis=0)


def apply_tensor(both, high, low):
    half = both.shape[0] // 2
    first = matmul_nt(both, high)
    return first[:half] + first[half:] + matmul_nt(both[:half], low)


def split_rows(*values):
    highs, lows = zip(*[split_two(value) for value in values])
    return jnp.concatenate(highs + lows, axis=0)


def inner(both):
    half = both.shape[0] // 2
    first = matmul_nt(both, both[:half])
    return first[:half] + first[half:] + matmul_nt(both[:half], both[half:])


def assemble(products):
    beads = products.shape[1] // 6

    def part(row, component):
        return products[8 * row : 8 * row + 8, component * beads : (component + 1) * beads]

    x = part(0, 0) + part(1, 1) + part(2, 2)
    y = part(0, 1) + part(1, 3) + part(2, 4)
    z = part(0, 2) + part(1, 4) + part(2, 5)
    return jnp.concatenate([x, y, z, jnp.zeros(x.shape, F32)], axis=1)


def filled_product(columns, source, wide, start, high, low):
    width = high.shape[1]
    products = jnp.zeros((32, high.shape[0]), F32)
    for at in range(0, width, 256):
        step = min(256, width - at)
        lanes = pl.ds(at, step)
        both = split_rows(wide[:, pl.ds(pl.multiple_of(start + at, 128), step)])
        pieces = [
            tensor(columns, source, pl.multiple_of(start + part, 128)) for part in range(at, at + step, 128)
        ]
        upper, lower = [jnp.concatenate(piece, axis=1) for piece in zip(*pieces)]
        high[:, lanes] = upper
        low[:, lanes] = lower
        products = products + apply_tensor(both, upper, lower)
    return products


def all_filled(own, source, wide, high, low):
    columns = target_columns(own)
    width = high.shape[1]
    chunk = lambda start: filled_product(columns, source, wide, start, high, low)
    if wide.shape[1] == width:
        return chunk(0)
    body = lambda index, total: total + chunk(index * width)
    return lax.fori_loop(1, wide.shape[1] // width, body, chunk(0))


def without_positions(block):
    lanes = lax.broadcasted_iota(jnp.int32, block.shape, 1)
    return jnp.where(lanes < block.shape[1] // 4 * 3, block, 0.0)


def first_stage(last, own, blocks, *refs):
    refs = list(refs)
    if last:
        before, image, copies, wide, high, low = refs
    else:
        out, wide, high, low = refs
    unpack(blocks, wide)
    products = all_filled(own[...], wide, wide, high, low)
    if not last:
        out[...] = products
        return
    block = assemble(products + before[...])
    image[...] = block
    sums = inner(split_rows(without_positions(own[...]), block))
    empty = jnp.zeros((8, block.shape[1] // 8 - 24), F32)
    copy_halves(block, copies, jnp.concatenate([sums[:8], sums[8:, 8:], empty], axis=1))


def cholesky(matrix):
    size = matrix.shape[0]
    shape = (size, size)
    rows = lax.broadcasted_iota(jnp.int32, shape, 0)
    cols = lax.broadcasted_iota(jnp.int32, shape, 1)
    entry = {}
    for j in range(size):
        column = jnp.broadcast_to(matrix[:, j : j + 1], shape)
        for i in range(j, size):
            entry[i, j] = jnp.broadcast_to(column[i : i + 1, :], shape)
    factor_t = jnp.zeros(shape, F32)
    inverse = jnp.zeros(shape, F32)
    inverse_rows = []
    for j in range(size):
        scale = lax.rsqrt(entry[j, j])
        lower_row = entry[j, j] * scale
        entry[j, j] = scale
        for i in range(j + 1, size):
            entry[i, j] = entry[i, j] * scale
        for i in range(j + 1, size):
            for k in range(j + 1, i + 1):
                entry[i, k] = entry[i, k] - entry[i, j] * entry[k, j]
        lower_row = jnp.where(cols == j, lower_row, 0.0)
        for i in range(j + 1, size):
            lower_row = jnp.where(cols == i, entry[i, j], lower_row)
        factor_t = jnp.where(rows == j, lower_row, factor_t)
        row = jnp.where(cols == j, 1.0, 0.0)
        for k in range(j):
            row = row - entry[j, k] * inverse_rows[k]
        row = row * scale
        inverse_rows.append(row)
        inverse = jnp.where(rows == j, row, inverse)
    return factor_t, inverse


def second_product(fill, own, wide, wide_image, high, low):
    if fill:
        return all_filled(own, wide, wide_image, high, low)
    return apply_tensor(split_rows(wide_image[...]), high[...], low[...])


def third_stage(size, fill, own, wide, *refs):
    refs = list(refs)
    if not fill:
        (high, low), refs = refs[:2], refs[2:]
    images, own_image, products, vectors, known, small, coefficients = refs[:7]
    if fill:
        high, low = refs[7:9]
    wide_image = refs[-1]
    unpack(images, wide_image)
    products[...] = second_product(fill, own[...], wide, wide_image, high, low)
    sums = wide_image[24:, :128]
    for at in range(128, wide_image.shape[1], 128):
        sums = sums + wide_image[24:, at : at + 128]
    width = own.shape[1] // 8
    sums = sum(sums[:, at : at + width] for at in range(width, 128, width)) + sums[:, :width]
    sums = sums / size
    _, inverse_zero = cholesky(sums[:, :8])
    inverse_zero_t = inverse_zero.T
    cross_t = small_matmul(inverse_zero, sums[:, 8:16])
    cross = cross_t.T
    factor_t, inverse = cholesky(sums[:, 16:24] - small_matmul(cross, cross_t))
    factor_one_t = small_matmul(factor_t, inverse_zero_t)
    first = small_matmul(inverse_zero, without_positions(own[...]))
    moved = small_matmul(inverse_zero, own_image[...])
    vectors[...] = small_matmul(inverse, own_image[...] - small_matmul(cross, first))
    known[...] = small_matmul(inverse, small_matmul(cross, moved)) + small_matmul(factor_one_t, first)
    small[...] = inverse
    coefficients[0] = small_matmul(cross_t, inverse_zero_t)
    coefficients[1] = factor_one_t.T


def fourth_stage(fill, own, wide, *refs):
    refs = list(refs)
    if not fill:
        (high, low), refs = refs[:2], refs[2:]
    images, before, vectors_in, known, small, shifted, partials = refs[:7]
    if fill:
        high, low = refs[7:9]
    wide_image = refs[-1]
    unpack(images, wide_image)
    products = second_product(fill, own[...], wide, wide_image, high, low) + before[...]
    vectors = vectors_in[...]
    shift = small_matmul(small[...], assemble(products)) - known[...]
    shifted[...] = shift
    (vector_high, vector_low), (shift_high, shift_low) = split_two(vectors), split_two(shift)
    partial = matmul_nt(vector_high, shift_high) + (
        matmul_nt(vector_high, shift_low) + matmul_nt(vector_low, shift_high)
    )
    line = jnp.concatenate([partial[row : row + 1] for row in range(8)], axis=1)
    partials[...] = jnp.broadcast_to(line[None], partials.shape)


def last_kernel(size, vectors, shifted, both, partials, basis, residual, coefficients):
    beads = basis.shape[2]
    width = partials.shape[2]
    total = jnp.sum(partials[...], axis=0) / size
    spread = jnp.broadcast_to(total, (8, width))
    rows = lax.broadcasted_iota(jnp.int32, spread.shape, 0)
    cols = lax.broadcasted_iota(jnp.int32, spread.shape, 1)
    block = vectors[...]
    left = shifted[...]
    transposed = jnp.where(cols % 8 == rows, spread, 0.0)
    for k in range(8):
        column = jnp.sum(jnp.where(cols // 8 == k, transposed, 0.0), axis=1, keepdims=True)
        left = left - column * block[k : k + 1, :]
    coefficients[0:2] = both[...]
    for k in range(8):
        coefficients[2, k : k + 1, :] = total[:, 8 * k : 8 * k + 8]
    for part in range(3):
        basis[part] = block[:, part * beads : (part + 1) * beads]
        residual[part] = left[:, part * beads : (part + 1) * beads]


def array(*shape, dtype=F32):
    return jax.ShapeDtypeStruct(shape, dtype)


def call(kernel, outs, scratch=(), **options):
    return pl.pallas_call(
        kernel,
        out_shape=outs,
        scratch_shapes=list(scratch),
        compiler_params=pltpu.CompilerParams(vmem_limit_bytes=48 * 1024 * 1024),
        **options,
    )


def to_all(copies):
    rows, cols = lax.axis_size("row"), lax.axis_size("col")
    order = [row * cols + 2 * layer + core for layer in range(cols // 2) for row in range(rows) for core in range(2)]
    return lax.all_to_all(copies, ("row", "col"), 0, 0, axis_index_groups=[order], tiled=True)


def gather(copies):
    mine = to_all(copies.reshape((-1,) + copies.shape[2:]))
    cols = lax.axis_size("col")
    return mine, lax.ppermute(mine, "col", [(col, col ^ 1) for col in range(cols)])


def local(positions, noise):
    vecs, _, beads = noise.shape
    devices = lax.axis_size("row") * lax.axis_size("col")
    total = beads * devices // 2
    size = 3.0 * beads * devices
    keep = 2 * 2 * 2 * 6 * beads * total <= KEPT
    width = total if keep else min(total, CHUNK)
    block = array(vecs, 4 * beads)
    copies = array(devices // 2, 2, vecs, 2 * beads)
    products = array(4 * vecs, 6 * beads)
    wide, held_wide = array(4 * vecs, total), pltpu.VMEM((4 * vecs, total), F32)
    kept = [array(6 * beads, width, dtype=BF16)] * 2 if keep else []
    held = [] if keep else [pltpu.VMEM((6 * beads, width), BF16)] * 2

    rows = noise.transpose(1, 0, 2).reshape(3 * vecs, beads)
    rows = jnp.concatenate([rows, jnp.pad(positions, ((0, vecs - 3), (0, 0)))], axis=0)
    own, own_copies = call(pack_kernel, [block, copies])(rows)
    one, two = gather(own_copies)
    partial, one_wide, *one_tensor = call(
        functools.partial(first_stage, False), [products, wide] + kept, held
    )(own, one)
    image, images, two_wide, *two_tensor = call(
        functools.partial(first_stage, True), [block, copies, wide] + kept, held
    )(own, two, partial)
    one, two = gather(images)
    partial, vectors, known, small, both = call(
        functools.partial(third_stage, size, not keep),
        [products, block, block, array(vecs, vecs), array(2, vecs, vecs)],
        held + [held_wide],
    )(own, one_wide, *one_tensor, one, image)
    shifted, partials = call(
        functools.partial(fourth_stage, not keep), [block, array(devices, 1, vecs * vecs)], held + [held_wide]
    )(own, two_wide, *two_tensor, two, partial, vectors, known, small)
    partials = to_all(partials)
    basis, residual, coefficients = call(
        functools.partial(last_kernel, size),
        [array(3, vecs, beads), array(3, vecs, beads), array(3, vecs, vecs)],
    )(vectors, shifted, both, partials)
    return (basis.transpose(1, 0, 2), residual.transpose(1, 0, 2), coefficients)


def solution(mesh):
    return jax.shard_map(
        local,
        mesh=mesh,
        in_specs=(P(None, ("row", "col")), P(None, None, ("row", "col"))),
        out_specs=(P(None, None, ("row", "col")), P(None, None, ("row", "col")), P()),
        check_vma=False,
    )
```

```python
import functools

import jax
import jax.numpy as jnp
from jax import lax
from jax.experimental import pallas as pl
from jax.experimental.pallas import tpu as pltpu
from jax.sharding import PartitionSpec as P

CHUNK = 1024
KEPT = 8 * 1024 * 1024
F32 = jnp.float32
BF16 = jnp.bfloat16


def copy_halves(block, copies, extra=None):
    beads = block.shape[1] // 4
    middle = beads // 2
    for core in range(2):
        parts = [block[:, part * beads + core * middle : part * beads + (core + 1) * middle] for part in range(4)]
        half = jnp.concatenate(parts, axis=1)
        if extra is not None:
            half = half + extra
        copies[:, core] = jnp.broadcast_to(half[None], (copies.shape[0],) + half.shape)


def pack_kernel(rows, block, copies):
    vecs = block.shape[0]
    flat = jnp.concatenate([rows[part * vecs : (part + 1) * vecs] for part in range(4)], axis=1)
    block[...] = flat
    copy_halves(flat, copies)


def split_two(value):
    high = value.astype(BF16)
    return high, (value - high.astype(F32)).astype(BF16)


def matmul_nt(left, right, precision=None):
    return lax.dot_general(
        left, right, (((1,), (1,)), ((), ())), precision=precision, preferred_element_type=F32
    )


def small_matmul(left, right):
    total = left[:, 0:1] * right[0:1, :]
    for k in range(1, left.shape[1]):
        total = total + left[:, k : k + 1] * right[k : k + 1, :]
    return total


def unpack(blocks, wide):
    count, vecs, lanes = blocks.shape
    width = lanes // 4
    for at in range(0, count, 4):
        four = [blocks[at + index] for index in range(4)]
        for part in range(4):
            wide[part * vecs : (part + 1) * vecs, pl.ds(at * width, 4 * width)] = jnp.concatenate(
                [block[:, part * width : (part + 1) * width] for block in four], axis=1
            )


def target_columns(own):
    beads = own.shape[1] // 4
    targets = own[:, 3 * beads :].T
    return [jnp.broadcast_to(targets[:, axis : axis + 1], (beads, 128)) for axis in range(3)]


def tensor(columns, wide, start):
    moved = [columns[axis] - wide[24 + axis : 25 + axis, pl.ds(start, 128)] for axis in range(3)]
    square = moved[0] * moved[0] + moved[1] * moved[1] + moved[2] * moved[2]
    square = jnp.maximum(square, 1e-12)
    inverse = lax.rsqrt(square)
    inverse_sq = inverse * inverse
    near = square < 4.0
    iso = inverse * jnp.where(near, square * (inverse - 9.0 / 32.0), 0.75 + 0.5 * inverse_sq)
    along = inverse * jnp.where(near, 3.0 / 32.0, inverse_sq * (0.75 - 1.5 * inverse_sq))
    scaled = [along * item for item in moved]
    parts = [
        iso + scaled[0] * moved[0],
        scaled[0] * moved[1],
        scaled[0] * moved[2],
        iso + scaled[1] * moved[1],
        scaled[1] * moved[2],
        iso + scaled[2] * moved[2],
    ]
    highs, lows = zip(*[split_two(value) for value in parts])
    return jnp.concatenate(highs, axis=0), jnp.concatenate(lows, axis=0)


def apply_tensor(both, high, low):
    half = both.shape[0] // 2
    first = matmul_nt(both, high)
    return first[:half] + first[half:] + matmul_nt(both[:half], low)


def split_rows(*values):
    highs, lows = zip(*[split_two(value) for value in values])
    return jnp.concatenate(highs + lows, axis=0)


def inner(left, right):
    return [jnp.sum(left * right[row : row + 1], axis=1, keepdims=True) for row in range(right.shape[0])]


def assemble(products):
    beads = products.shape[1] // 6

    def part(row, component):
        return products[8 * row : 8 * row + 8, component * beads : (component + 1) * beads]

    x = part(0, 0) + part(1, 1) + part(2, 2)
    y = part(0, 1) + part(1, 3) + part(2, 4)
    z = part(0, 2) + part(1, 4) + part(2, 5)
    return jnp.concatenate([x, y, z, jnp.zeros(x.shape, F32)], axis=1)


def filled_product(columns, source, wide, start, high, low):
    width = high.shape[1]
    products = jnp.zeros((32, high.shape[0]), F32)
    for at in range(0, width, 256):
        step = min(256, width - at)
        lanes = pl.ds(at, step)
        both = split_rows(wide[:, pl.ds(pl.multiple_of(start + at, 128), step)])
        pieces = [
            tensor(columns, source, pl.multiple_of(start + part, 128)) for part in range(at, at + step, 128)
        ]
        upper, lower = [jnp.concatenate(piece, axis=1) for piece in zip(*pieces)]
        high[:, lanes] = upper
        low[:, lanes] = lower
        products = products + apply_tensor(both, upper, lower)
    return products


def all_filled(own, source, wide, high, low):
    columns = target_columns(own)
    width = high.shape[1]
    chunk = lambda start: filled_product(columns, source, wide, start, high, low)
    if wide.shape[1] == width:
        return chunk(0)
    body = lambda index, total: total + chunk(index * width)
    return lax.fori_loop(1, wide.shape[1] // width, body, chunk(0))


def without_positions(block):
    lanes = lax.broadcasted_iota(jnp.int32, block.shape, 1)
    return jnp.where(lanes < block.shape[1] // 4 * 3, block, 0.0)


def first_stage(last, own, blocks, *refs):
    refs = list(refs)
    if last:
        before, image, copies, wide, high, low = refs
    else:
        out, wide, high, low = refs
    unpack(blocks, wide)
    products = all_filled(own[...], wide, wide, high, low)
    if not last:
        out[...] = products
        return
    block = assemble(products + before[...])
    image[...] = block
    noise = without_positions(own[...])
    columns = inner(noise, noise) + inner(noise, block) + inner(block, block)
    lanes = lax.broadcasted_iota(jnp.int32, (block.shape[0], block.shape[1] // 2), 1)
    sums = jnp.zeros(lanes.shape, F32)
    for index, column in enumerate(columns):
        sums = jnp.where(lanes == block.shape[1] // 8 * 3 + index, column, sums)
    copy_halves(block, copies, sums)


def cholesky(matrix):
    size = matrix.shape[0]
    shape = (size, size)
    rows = lax.broadcasted_iota(jnp.int32, shape, 0)
    cols = lax.broadcasted_iota(jnp.int32, shape, 1)
    entry = {}
    for j in range(size):
        column = jnp.broadcast_to(matrix[:, j : j + 1], shape)
        for i in range(j, size):
            entry[i, j] = jnp.broadcast_to(column[i : i + 1, :], shape)
    factor_t = jnp.zeros(shape, F32)
    inverse = jnp.zeros(shape, F32)
    inverse_rows = []
    for j in range(size):
        scale = lax.rsqrt(entry[j, j])
        lower_row = entry[j, j] * scale
        entry[j, j] = scale
        for i in range(j + 1, size):
            entry[i, j] = entry[i, j] * scale
        for i in range(j + 1, size):
            for k in range(j + 1, i + 1):
                entry[i, k] = entry[i, k] - entry[i, j] * entry[k, j]
        lower_row = jnp.where(cols == j, lower_row, 0.0)
        for i in range(j + 1, size):
            lower_row = jnp.where(cols == i, entry[i, j], lower_row)
        factor_t = jnp.where(rows == j, lower_row, factor_t)
        row = jnp.where(cols == j, 1.0, 0.0)
        for k in range(j):
            row = row - entry[j, k] * inverse_rows[k]
        row = row * scale
        inverse_rows.append(row)
        inverse = jnp.where(rows == j, row, inverse)
    return factor_t, inverse


def second_product(fill, own, wide, wide_image, high, low):
    if fill:
        return all_filled(own, wide, wide_image, high, low)
    return apply_tensor(split_rows(wide_image[...]), high[...], low[...])


def third_stage(size, fill, own, wide, *refs):
    refs = list(refs)
    if not fill:
        (high, low), refs = refs[:2], refs[2:]
    images, own_image, products, vectors, known, small, coefficients = refs[:7]
    if fill:
        high, low = refs[7:9]
    wide_image = refs[-1]
    unpack(images, wide_image)
    products[...] = second_product(fill, own[...], wide, wide_image, high, low)
    sums = wide_image[24:, :128]
    for at in range(128, wide_image.shape[1], 128):
        sums = sums + wide_image[24:, at : at + 128]
    width = own.shape[1] // 8
    sums = sum(sums[:, at : at + width] for at in range(width, 128, width)) + sums[:, :width]
    sums = sums / size
    _, inverse_zero = cholesky(sums[:, :8])
    inverse_zero_t = inverse_zero.T
    cross_t = small_matmul(inverse_zero, sums[:, 8:16])
    cross = cross_t.T
    factor_t, inverse = cholesky(sums[:, 16:24] - small_matmul(cross, cross_t))
    factor_one_t = small_matmul(factor_t, inverse_zero_t)
    first = small_matmul(inverse_zero, without_positions(own[...]))
    moved = small_matmul(inverse_zero, own_image[...])
    vectors[...] = small_matmul(inverse, own_image[...] - small_matmul(cross, first))
    known[...] = small_matmul(inverse, small_matmul(cross, moved)) + small_matmul(factor_one_t, first)
    small[...] = inverse
    coefficients[0] = small_matmul(cross_t, inverse_zero_t)
    coefficients[1] = factor_one_t.T


def fourth_stage(fill, own, wide, *refs):
    refs = list(refs)
    if not fill:
        (high, low), refs = refs[:2], refs[2:]
    images, before, vectors_in, known, small, shifted, partials = refs[:7]
    if fill:
        high, low = refs[7:9]
    wide_image = refs[-1]
    unpack(images, wide_image)
    products = second_product(fill, own[...], wide, wide_image, high, low) + before[...]
    vectors = vectors_in[...]
    shift = small_matmul(small[...], assemble(products)) - known[...]
    shifted[...] = shift
    lanes = lax.broadcasted_iota(jnp.int32, (8, partials.shape[2]), 1)
    rows = lax.broadcasted_iota(jnp.int32, lanes.shape, 0)
    line = jnp.zeros(lanes.shape, F32)
    for row, column in enumerate(inner(shift, vectors)):
        line = jnp.where(lanes == 8 * row + rows, column, line)
    line = jnp.sum(line, axis=0, keepdims=True)
    partials[...] = jnp.broadcast_to(line[None], partials.shape)


def last_kernel(size, vectors, shifted, both, partials, basis, residual, coefficients):
    beads = basis.shape[2]
    width = partials.shape[2]
    total = jnp.sum(partials[...], axis=0) / size
    spread = jnp.broadcast_to(total, (8, width))
    rows = lax.broadcasted_iota(jnp.int32, spread.shape, 0)
    cols = lax.broadcasted_iota(jnp.int32, spread.shape, 1)
    block = vectors[...]
    left = shifted[...]
    transposed = jnp.where(cols % 8 == rows, spread, 0.0)
    for k in range(8):
        column = jnp.sum(jnp.where(cols // 8 == k, transposed, 0.0), axis=1, keepdims=True)
        left = left - column * block[k : k + 1, :]
    coefficients[0:2] = both[...]
    for k in range(8):
        coefficients[2, k : k + 1, :] = total[:, 8 * k : 8 * k + 8]
    for part in range(3):
        basis[part] = block[:, part * beads : (part + 1) * beads]
        residual[part] = left[:, part * beads : (part + 1) * beads]


def array(*shape, dtype=F32):
    return jax.ShapeDtypeStruct(shape, dtype)


def call(kernel, outs, scratch=(), **options):
    return pl.pallas_call(
        kernel,
        out_shape=outs,
        scratch_shapes=list(scratch),
        compiler_params=pltpu.CompilerParams(vmem_limit_bytes=48 * 1024 * 1024),
        **options,
    )


def to_all(copies):
    return lax.all_to_all(copies, ("row", "col"), 0, 0, tiled=True)


def gather(copies):
    mine = to_all(copies.reshape((-1,) + copies.shape[2:]))
    cols = lax.axis_size("col")
    return mine, lax.ppermute(mine, "col", [(col, col ^ 1) for col in range(cols)])


def local(positions, noise):
    vecs, _, beads = noise.shape
    devices = lax.axis_size("row") * lax.axis_size("col")
    total = beads * devices // 2
    size = 3.0 * beads * devices
    keep = 2 * 2 * 2 * 6 * beads * total <= KEPT
    width = total if keep else min(total, CHUNK)
    block = array(vecs, 4 * beads)
    copies = array(devices // 2, 2, vecs, 2 * beads)
    products = array(4 * vecs, 6 * beads)
    wide, held_wide = array(4 * vecs, total), pltpu.VMEM((4 * vecs, total), F32)
    kept = [array(6 * beads, width, dtype=BF16)] * 2 if keep else []
    held = [] if keep else [pltpu.VMEM((6 * beads, width), BF16)] * 2

    rows = noise.transpose(1, 0, 2).reshape(3 * vecs, beads)
    rows = jnp.concatenate([rows, jnp.pad(positions, ((0, vecs - 3), (0, 0)))], axis=0)
    own, own_copies = call(pack_kernel, [block, copies])(rows)
    one, two = gather(own_copies)
    partial, one_wide, *one_tensor = call(
        functools.partial(first_stage, False), [products, wide] + kept, held
    )(own, one)
    image, images, two_wide, *two_tensor = call(
        functools.partial(first_stage, True), [block, copies, wide] + kept, held
    )(own, two, partial)
    one, two = gather(images)
    partial, vectors, known, small, both = call(
        functools.partial(third_stage, size, not keep),
        [products, block, block, array(vecs, vecs), array(2, vecs, vecs)],
        held + [held_wide],
    )(own, one_wide, *one_tensor, one, image)
    shifted, partials = call(
        functools.partial(fourth_stage, not keep), [block, array(devices, 1, vecs * vecs)], held + [held_wide]
    )(own, two_wide, *two_tensor, two, partial, vectors, known, small)
    partials = to_all(partials)
    basis, residual, coefficients = call(
        functools.partial(last_kernel, size),
        [array(3, vecs, beads), array(3, vecs, beads), array(3, vecs, vecs)],
    )(vectors, shifted, both, partials)
    return (basis.transpose(1, 0, 2), residual.transpose(1, 0, 2), coefficients)


def solution(mesh):
    return jax.shard_map(
        local,
        mesh=mesh,
        in_specs=(P(None, ("row", "col")), P(None, None, ("row", "col"))),
        out_specs=(P(None, None, ("row", "col")), P(None, None, ("row", "col")), P()),
        check_vma=False,
    )
```

```python
import functools

import jax
import jax.numpy as jnp
from jax import lax
from jax.experimental import pallas as pl
from jax.experimental.pallas import tpu as pltpu
from jax.sharding import PartitionSpec as P

CHUNK = 1024
KEPT = 8 * 1024 * 1024
F32 = jnp.float32
BF16 = jnp.bfloat16


def copy_halves(block, copies, extra=None):
    beads = block.shape[1] // 4
    middle = beads // 2
    for core in range(2):
        parts = [block[:, part * beads + core * middle : part * beads + (core + 1) * middle] for part in range(4)]
        half = jnp.concatenate(parts, axis=1)
        if extra is not None:
            half = half + extra
        copies[:, core] = jnp.broadcast_to(half[None], (copies.shape[0],) + half.shape)


def pack_kernel(rows, block, copies):
    vecs = block.shape[0]
    flat = jnp.concatenate([rows[part * vecs : (part + 1) * vecs] for part in range(4)], axis=1)
    block[...] = flat
    copy_halves(flat, copies)


def split_two(value):
    high = value.astype(BF16)
    return high, (value - high.astype(F32)).astype(BF16)


def matmul_nt(left, right, precision=None):
    return lax.dot_general(
        left, right, (((1,), (1,)), ((), ())), precision=precision, preferred_element_type=F32
    )


def small_matmul(left, right):
    total = left[:, 0:1] * right[0:1, :]
    for k in range(1, left.shape[1]):
        total = total + left[:, k : k + 1] * right[k : k + 1, :]
    return total


def unpack(blocks, wide):
    count, vecs, lanes = blocks.shape
    width = lanes // 4
    for at in range(0, count, 4):
        four = [blocks[at + index] for index in range(4)]
        for part in range(4):
            wide[part * vecs : (part + 1) * vecs, pl.ds(at * width, 4 * width)] = jnp.concatenate(
                [block[:, part * width : (part + 1) * width] for block in four], axis=1
            )


def target_columns(own):
    beads = own.shape[1] // 4
    targets = own[:, 3 * beads :].T
    return [jnp.broadcast_to(targets[:, axis : axis + 1], (beads, 128)) for axis in range(3)]


def tensor(columns, wide, start):
    moved = [columns[axis] - wide[24 + axis : 25 + axis, pl.ds(start, 128)] for axis in range(3)]
    square = moved[0] * moved[0] + moved[1] * moved[1] + moved[2] * moved[2]
    square = jnp.maximum(square, 1e-12)
    inverse = lax.rsqrt(square)
    inverse_sq = inverse * inverse
    near = square < 4.0
    iso = inverse * jnp.where(near, square * (inverse - 9.0 / 32.0), 0.75 + 0.5 * inverse_sq)
    along = inverse * jnp.where(near, 3.0 / 32.0, inverse_sq * (0.75 - 1.5 * inverse_sq))
    scaled = [along * item for item in moved]
    parts = [
        iso + scaled[0] * moved[0],
        scaled[0] * moved[1],
        scaled[0] * moved[2],
        iso + scaled[1] * moved[1],
        scaled[1] * moved[2],
        iso + scaled[2] * moved[2],
    ]
    highs, lows = zip(*[split_two(value) for value in parts])
    return jnp.concatenate(highs, axis=0), jnp.concatenate(lows, axis=0)


def apply_tensor(both, high, low):
    half = both.shape[0] // 2
    first = matmul_nt(both, high)
    return first[:half] + first[half:] + matmul_nt(both[:half], low)


def split_rows(*values):
    highs, lows = zip(*[split_two(value) for value in values])
    return jnp.concatenate(highs + lows, axis=0)


def inner(left, right):
    return [jnp.sum(left * right[row : row + 1], axis=1, keepdims=True) for row in range(right.shape[0])]


def assemble(products):
    beads = products.shape[1] // 6

    def part(row, component):
        return products[8 * row : 8 * row + 8, component * beads : (component + 1) * beads]

    x = part(0, 0) + part(1, 1) + part(2, 2)
    y = part(0, 1) + part(1, 3) + part(2, 4)
    z = part(0, 2) + part(1, 4) + part(2, 5)
    return jnp.concatenate([x, y, z, jnp.zeros(x.shape, F32)], axis=1)


def filled_product(columns, source, wide, start, high, low):
    width = high.shape[1]
    products = jnp.zeros((32, high.shape[0]), F32)
    for at in range(0, width, 256):
        step = min(256, width - at)
        lanes = pl.ds(at, step)
        both = split_rows(wide[:, pl.ds(pl.multiple_of(start + at, 128), step)])
        pieces = [
            tensor(columns, source, pl.multiple_of(start + part, 128)) for part in range(at, at + step, 128)
        ]
        upper, lower = [jnp.concatenate(piece, axis=1) for piece in zip(*pieces)]
        high[:, lanes] = upper
        low[:, lanes] = lower
        products = products + apply_tensor(both, upper, lower)
    return products


def all_filled(own, source, wide, high, low):
    columns = target_columns(own)
    width = high.shape[1]
    chunk = lambda start: filled_product(columns, source, wide, start, high, low)
    if wide.shape[1] == width:
        return chunk(0)
    body = lambda index, total: total + chunk(index * width)
    return lax.fori_loop(1, wide.shape[1] // width, body, chunk(0))


def without_positions(block):
    lanes = lax.broadcasted_iota(jnp.int32, block.shape, 1)
    return jnp.where(lanes < block.shape[1] // 4 * 3, block, 0.0)


def row_sums(wide):
    total = jnp.zeros((wide.shape[0], wide.shape[0]), F32)
    for at in range(0, wide.shape[1], CHUNK):
        both = split_rows(wide[:, at : min(at + CHUNK, wide.shape[1])])
        half = both.shape[0] // 2
        first, second = matmul_nt(both, both[:half]), matmul_nt(both, both[half:])
        total = total + ((first[:half] + first[half:]) + (second[:half] + second[half:]))
    return total


def first_stage(size, last, own, blocks, *refs):
    refs = list(refs)
    if last:
        before, before_sums, first_out, image, copies, wide, high, low = refs
    else:
        out, sums_out, wide, high, low = refs
    unpack(blocks, wide)
    sums = row_sums(wide)
    products = all_filled(own[...], wide, wide, high, low)
    if not last:
        out[...], sums_out[...] = products, sums
        return
    sums = (sums + before_sums[...]) / size
    _, inverse = cholesky(sums[:8, :8] + sums[8:16, 8:16] + sums[16:24, 16:24])
    first = small_matmul(inverse, without_positions(own[...]))
    block = small_matmul(inverse, assemble(products + before[...]))
    first_out[...] = first
    image[...] = block
    columns = inner(first, block) + inner(block, block)
    lanes = lax.broadcasted_iota(jnp.int32, (block.shape[0], block.shape[1] // 2), 1)
    shares = jnp.zeros(lanes.shape, F32)
    for index, column in enumerate(columns):
        shares = jnp.where(lanes == block.shape[1] // 8 * 3 + index, column, shares)
    copy_halves(block, copies, shares)


def cholesky(matrix):
    size = matrix.shape[0]
    shape = (size, size)
    rows = lax.broadcasted_iota(jnp.int32, shape, 0)
    cols = lax.broadcasted_iota(jnp.int32, shape, 1)
    entry = {}
    for j in range(size):
        column = jnp.broadcast_to(matrix[:, j : j + 1], shape)
        for i in range(j, size):
            entry[i, j] = jnp.broadcast_to(column[i : i + 1, :], shape)
    factor_t = jnp.zeros(shape, F32)
    inverse = jnp.zeros(shape, F32)
    inverse_rows = []
    for j in range(size):
        scale = lax.rsqrt(entry[j, j])
        lower_row = entry[j, j] * scale
        entry[j, j] = scale
        for i in range(j + 1, size):
            entry[i, j] = entry[i, j] * scale
        for i in range(j + 1, size):
            for k in range(j + 1, i + 1):
                entry[i, k] = entry[i, k] - entry[i, j] * entry[k, j]
        lower_row = jnp.where(cols == j, lower_row, 0.0)
        for i in range(j + 1, size):
            lower_row = jnp.where(cols == i, entry[i, j], lower_row)
        factor_t = jnp.where(rows == j, lower_row, factor_t)
        row = jnp.where(cols == j, 1.0, 0.0)
        for k in range(j):
            row = row - entry[j, k] * inverse_rows[k]
        row = row * scale
        inverse_rows.append(row)
        inverse = jnp.where(rows == j, row, inverse)
    return factor_t, inverse


def second_product(fill, own, wide, wide_image, high, low):
    if fill:
        return all_filled(own, wide, wide_image, high, low)
    return apply_tensor(split_rows(wide_image[...]), high[...], low[...])


def third_stage(size, fill, own, wide, *refs):
    refs = list(refs)
    if not fill:
        (high, low), refs = refs[:2], refs[2:]
    images, own_first, own_image, products, vectors, known, small, coefficients = refs[:8]
    if fill:
        high, low = refs[8:10]
    wide_image = refs[-1]
    unpack(images, wide_image)
    products[...] = second_product(fill, own[...], wide, wide_image, high, low)
    sums = wide_image[24:, :128]
    for at in range(128, wide_image.shape[1], 128):
        sums = sums + wide_image[24:, at : at + 128]
    width = own.shape[1] // 8
    sums = sum(sums[:, at : at + width] for at in range(width, 128, width)) + sums[:, :width]
    sums = sums / size
    alpha = sums[:, :8]
    alpha_t = alpha.T
    factor_t, inverse = cholesky(sums[:, 8:16] - small_matmul(alpha_t, alpha))
    first, image = own_first[...], own_image[...]
    vectors[...] = small_matmul(inverse, image - small_matmul(alpha_t, first))
    known[...] = small_matmul(inverse, small_matmul(alpha_t, image)) + small_matmul(factor_t, first)
    small[...] = inverse
    coefficients[0] = alpha
    coefficients[1] = factor_t.T


def fourth_stage(fill, own, wide, *refs):
    refs = list(refs)
    if not fill:
        (high, low), refs = refs[:2], refs[2:]
    images, before, vectors_in, known, small, shifted, partials = refs[:7]
    if fill:
        high, low = refs[7:9]
    wide_image = refs[-1]
    unpack(images, wide_image)
    products = second_product(fill, own[...], wide, wide_image, high, low) + before[...]
    vectors = vectors_in[...]
    shift = small_matmul(small[...], assemble(products)) - known[...]
    shifted[...] = shift
    lanes = lax.broadcasted_iota(jnp.int32, (8, partials.shape[2]), 1)
    rows = lax.broadcasted_iota(jnp.int32, lanes.shape, 0)
    line = jnp.zeros(lanes.shape, F32)
    for row, column in enumerate(inner(shift, vectors)):
        line = jnp.where(lanes == 8 * row + rows, column, line)
    line = jnp.sum(line, axis=0, keepdims=True)
    partials[...] = jnp.broadcast_to(line[None], partials.shape)


def last_kernel(size, vectors, shifted, both, partials, basis, residual, coefficients):
    beads = basis.shape[2]
    width = partials.shape[2]
    total = jnp.sum(partials[...], axis=0) / size
    spread = jnp.broadcast_to(total, (8, width))
    rows = lax.broadcasted_iota(jnp.int32, spread.shape, 0)
    cols = lax.broadcasted_iota(jnp.int32, spread.shape, 1)
    block = vectors[...]
    left = shifted[...]
    transposed = jnp.where(cols % 8 == rows, spread, 0.0)
    for k in range(8):
        column = jnp.sum(jnp.where(cols // 8 == k, transposed, 0.0), axis=1, keepdims=True)
        left = left - column * block[k : k + 1, :]
    coefficients[0:2] = both[...]
    for k in range(8):
        coefficients[2, k : k + 1, :] = total[:, 8 * k : 8 * k + 8]
    for part in range(3):
        basis[part] = block[:, part * beads : (part + 1) * beads]
        residual[part] = left[:, part * beads : (part + 1) * beads]


def array(*shape, dtype=F32):
    return jax.ShapeDtypeStruct(shape, dtype)


def call(kernel, outs, scratch=(), **options):
    return pl.pallas_call(
        kernel,
        out_shape=outs,
        scratch_shapes=list(scratch),
        compiler_params=pltpu.CompilerParams(vmem_limit_bytes=48 * 1024 * 1024),
        **options,
    )


def to_all(copies):
    return lax.all_to_all(copies, ("row", "col"), 0, 0, tiled=True)


def gather(copies):
    mine = to_all(copies.reshape((-1,) + copies.shape[2:]))
    cols = lax.axis_size("col")
    return mine, lax.ppermute(mine, "col", [(col, col ^ 1) for col in range(cols)])


def local(positions, noise):
    vecs, _, beads = noise.shape
    devices = lax.axis_size("row") * lax.axis_size("col")
    total = beads * devices // 2
    size = 3.0 * beads * devices
    keep = 2 * 2 * 2 * 6 * beads * total <= KEPT
    width = total if keep else min(total, CHUNK)
    block = array(vecs, 4 * beads)
    copies = array(devices // 2, 2, vecs, 2 * beads)
    products = array(4 * vecs, 6 * beads)
    wide, held_wide = array(4 * vecs, total), pltpu.VMEM((4 * vecs, total), F32)
    kept = [array(6 * beads, width, dtype=BF16)] * 2 if keep else []
    held = [] if keep else [pltpu.VMEM((6 * beads, width), BF16)] * 2

    rows = noise.transpose(1, 0, 2).reshape(3 * vecs, beads)
    rows = jnp.concatenate([rows, jnp.pad(positions, ((0, vecs - 3), (0, 0)))], axis=0)
    own, own_copies = call(pack_kernel, [block, copies])(rows)
    one, two = gather(own_copies)
    partial, sums, one_wide, *one_tensor = call(
        functools.partial(first_stage, size, False), [products, array(4 * vecs, 4 * vecs), wide] + kept, held
    )(own, one)
    first, image, images, two_wide, *two_tensor = call(
        functools.partial(first_stage, size, True), [block, block, copies, wide] + kept, held
    )(own, two, partial, sums)
    one, two = gather(images)
    partial, vectors, known, small, both = call(
        functools.partial(third_stage, size, not keep),
        [products, block, block, array(vecs, vecs), array(2, vecs, vecs)],
        held + [held_wide],
    )(own, one_wide, *one_tensor, one, first, image)
    shifted, partials = call(
        functools.partial(fourth_stage, not keep), [block, array(devices, 1, vecs * vecs)], held + [held_wide]
    )(own, two_wide, *two_tensor, two, partial, vectors, known, small)
    partials = to_all(partials)
    basis, residual, coefficients = call(
        functools.partial(last_kernel, size),
        [array(3, vecs, beads), array(3, vecs, beads), array(3, vecs, vecs)],
    )(vectors, shifted, both, partials)
    return (basis.transpose(1, 0, 2), residual.transpose(1, 0, 2), coefficients)


def solution(mesh):
    return jax.shard_map(
        local,
        mesh=mesh,
        in_specs=(P(None, ("row", "col")), P(None, None, ("row", "col"))),
        out_specs=(P(None, None, ("row", "col")), P(None, None, ("row", "col")), P()),
        check_vma=False,
    )
```

```python
import functools

import jax
import jax.numpy as jnp
from jax import lax
from jax.experimental import pallas as pl
from jax.experimental.pallas import tpu as pltpu
from jax.sharding import PartitionSpec as P

CHUNK = 1024
KEPT = 8 * 1024 * 1024
F32 = jnp.float32
BF16 = jnp.bfloat16


def copy_halves(block, copies, extra=None):
    beads = block.shape[1] // 4
    middle = beads // 2
    for core in range(2):
        parts = [block[:, part * beads + core * middle : part * beads + (core + 1) * middle] for part in range(4)]
        half = jnp.concatenate(parts, axis=1)
        if extra is not None:
            half = half + extra
        copies[:, core] = jnp.broadcast_to(half[None], (copies.shape[0],) + half.shape)


def pack_kernel(positions, noise, block, copies, held_positions, held_noise, sems):
    reads = [
        pltpu.make_async_copy(positions, held_positions, sems.at[0]),
        pltpu.make_async_copy(noise, held_noise, sems.at[1]),
    ]
    for read in reads:
        read.start()
    beads = block.shape[1] // 4
    block[...] = jnp.zeros(block.shape, F32)
    for read in reads:
        read.wait()
    for part in range(3):
        block[:, part * beads : (part + 1) * beads] = held_noise[part]
    block[:3, 3 * beads :] = held_positions[...]
    copy_halves(block[...], copies)


def split_two(value):
    high = value.astype(BF16)
    return high, (value - high.astype(F32)).astype(BF16)


def matmul_nt(left, right, precision=None):
    return lax.dot_general(
        left, right, (((1,), (1,)), ((), ())), precision=precision, preferred_element_type=F32
    )


def small_matmul(left, right):
    total = left[:, 0:1] * right[0:1, :]
    for k in range(1, left.shape[1]):
        total = total + left[:, k : k + 1] * right[k : k + 1, :]
    return total


def unpack(blocks, wide):
    count, vecs, lanes = blocks.shape
    width = lanes // 4
    for at in range(0, count, 4):
        four = [blocks[at + index] for index in range(4)]
        for part in range(4):
            wide[part * vecs : (part + 1) * vecs, pl.ds(at * width, 4 * width)] = jnp.concatenate(
                [block[:, part * width : (part + 1) * width] for block in four], axis=1
            )


def target_columns(own):
    beads = own.shape[1] // 4
    targets = own[:, 3 * beads :].T
    return [jnp.broadcast_to(targets[:, axis : axis + 1], (beads, 128)) for axis in range(3)]


def tensor(columns, wide, start):
    moved = [columns[axis] - wide[24 + axis : 25 + axis, pl.ds(start, 128)] for axis in range(3)]
    square = moved[0] * moved[0] + moved[1] * moved[1] + moved[2] * moved[2]
    square = jnp.maximum(square, 1e-12)
    inverse = lax.rsqrt(square)
    inverse_sq = inverse * inverse
    near = square < 4.0
    iso = inverse * jnp.where(near, square * (inverse - 9.0 / 32.0), 0.75 + 0.5 * inverse_sq)
    along = inverse * jnp.where(near, 3.0 / 32.0, inverse_sq * (0.75 - 1.5 * inverse_sq))
    scaled = [along * item for item in moved]
    parts = [
        iso + scaled[0] * moved[0],
        scaled[0] * moved[1],
        scaled[0] * moved[2],
        iso + scaled[1] * moved[1],
        scaled[1] * moved[2],
        iso + scaled[2] * moved[2],
    ]
    highs, lows = zip(*[split_two(value) for value in parts])
    return jnp.concatenate(highs, axis=0), jnp.concatenate(lows, axis=0)


def apply_tensor(both, high, low):
    half = both.shape[0] // 2
    first = matmul_nt(both, high)
    return first[:half] + first[half:] + matmul_nt(both[:half], low)


def split_rows(*values):
    highs, lows = zip(*[split_two(value) for value in values])
    return jnp.concatenate(highs + lows, axis=0)


def inner(left, right):
    return [jnp.sum(left * right[row : row + 1], axis=1, keepdims=True) for row in range(right.shape[0])]


def assemble(products):
    beads = products.shape[1] // 6

    def part(row, component):
        return products[8 * row : 8 * row + 8, component * beads : (component + 1) * beads]

    x = part(0, 0) + part(1, 1) + part(2, 2)
    y = part(0, 1) + part(1, 3) + part(2, 4)
    z = part(0, 2) + part(1, 4) + part(2, 5)
    return jnp.concatenate([x, y, z, jnp.zeros(x.shape, F32)], axis=1)


def filled_product(columns, source, wide, start, high, low):
    width = high.shape[1]
    products = jnp.zeros((32, high.shape[0]), F32)
    for at in range(0, width, 256):
        step = min(256, width - at)
        lanes = pl.ds(at, step)
        both = split_rows(wide[:, pl.ds(pl.multiple_of(start + at, 128), step)])
        pieces = [
            tensor(columns, source, pl.multiple_of(start + part, 128)) for part in range(at, at + step, 128)
        ]
        upper, lower = [jnp.concatenate(piece, axis=1) for piece in zip(*pieces)]
        high[:, lanes] = upper
        low[:, lanes] = lower
        products = products + apply_tensor(both, upper, lower)
    return products


def all_filled(own, source, wide, high, low):
    columns = target_columns(own)
    width = high.shape[1]
    chunk = lambda start: filled_product(columns, source, wide, start, high, low)
    if wide.shape[1] == width:
        return chunk(0)
    body = lambda index, total: total + chunk(index * width)
    return lax.fori_loop(1, wide.shape[1] // width, body, chunk(0))


def without_positions(block):
    lanes = lax.broadcasted_iota(jnp.int32, block.shape, 1)
    return jnp.where(lanes < block.shape[1] // 4 * 3, block, 0.0)


def row_sums(wide):
    total = jnp.zeros((wide.shape[0], wide.shape[0]), F32)
    for at in range(0, wide.shape[1], CHUNK):
        both = split_rows(wide[:, at : min(at + CHUNK, wide.shape[1])])
        half = both.shape[0] // 2
        first, second = matmul_nt(both, both[:half]), matmul_nt(both, both[half:])
        total = total + ((first[:half] + first[half:]) + (second[:half] + second[half:]))
    return total


def first_stage(size, last, own, blocks, *refs):
    refs = list(refs)
    if last:
        before, before_sums, first_out, image, copies, wide, high, low = refs
    else:
        out, sums_out, wide, high, low = refs
    unpack(blocks, wide)
    sums = row_sums(wide)
    products = all_filled(own[...], wide, wide, high, low)
    if not last:
        out[...], sums_out[...] = products, sums
        return
    sums = (sums + before_sums[...]) / size
    _, inverse = cholesky(sums[:8, :8] + sums[8:16, 8:16] + sums[16:24, 16:24])
    first = small_matmul(inverse, without_positions(own[...]))
    block = small_matmul(inverse, assemble(products + before[...]))
    first_out[...] = first
    image[...] = block
    columns = inner(first, block) + inner(block, block)
    lanes = lax.broadcasted_iota(jnp.int32, (block.shape[0], block.shape[1] // 2), 1)
    shares = jnp.zeros(lanes.shape, F32)
    for index, column in enumerate(columns):
        shares = jnp.where(lanes == block.shape[1] // 8 * 3 + index, column, shares)
    copy_halves(block, copies, shares)


def cholesky(matrix):
    size = matrix.shape[0]
    shape = (size, size)
    rows = lax.broadcasted_iota(jnp.int32, shape, 0)
    cols = lax.broadcasted_iota(jnp.int32, shape, 1)
    entry = {}
    for j in range(size):
        column = jnp.broadcast_to(matrix[:, j : j + 1], shape)
        for i in range(j, size):
            entry[i, j] = jnp.broadcast_to(column[i : i + 1, :], shape)
    factor_t = jnp.zeros(shape, F32)
    inverse = jnp.zeros(shape, F32)
    inverse_rows = []
    for j in range(size):
        scale = lax.rsqrt(entry[j, j])
        lower_row = entry[j, j] * scale
        entry[j, j] = scale
        for i in range(j + 1, size):
            entry[i, j] = entry[i, j] * scale
        for i in range(j + 1, size):
            for k in range(j + 1, i + 1):
                entry[i, k] = entry[i, k] - entry[i, j] * entry[k, j]
        lower_row = jnp.where(cols == j, lower_row, 0.0)
        for i in range(j + 1, size):
            lower_row = jnp.where(cols == i, entry[i, j], lower_row)
        factor_t = jnp.where(rows == j, lower_row, factor_t)
        row = jnp.where(cols == j, 1.0, 0.0)
        for k in range(j):
            row = row - entry[j, k] * inverse_rows[k]
        row = row * scale
        inverse_rows.append(row)
        inverse = jnp.where(rows == j, row, inverse)
    return factor_t, inverse


def second_product(fill, own, wide, wide_image, high, low):
    if fill:
        return all_filled(own, wide, wide_image, high, low)
    return apply_tensor(split_rows(wide_image[...]), high[...], low[...])


def third_stage(size, fill, own, wide, *refs):
    refs = list(refs)
    if not fill:
        (high, low), refs = refs[:2], refs[2:]
    images, own_first, own_image, products, vectors, known, small, coefficients = refs[:8]
    if fill:
        high, low = refs[8:10]
    wide_image = refs[-1]
    unpack(images, wide_image)
    products[...] = second_product(fill, own[...], wide, wide_image, high, low)
    sums = wide_image[24:, :128]
    for at in range(128, wide_image.shape[1], 128):
        sums = sums + wide_image[24:, at : at + 128]
    width = own.shape[1] // 8
    sums = sum(sums[:, at : at + width] for at in range(width, 128, width)) + sums[:, :width]
    sums = sums / size
    alpha = sums[:, :8]
    alpha_t = alpha.T
    factor_t, inverse = cholesky(sums[:, 8:16] - small_matmul(alpha_t, alpha))
    first, image = own_first[...], own_image[...]
    vectors[...] = small_matmul(inverse, image - small_matmul(alpha_t, first))
    known[...] = small_matmul(inverse, small_matmul(alpha_t, image)) + small_matmul(factor_t, first)
    small[...] = inverse
    coefficients[0] = alpha
    coefficients[1] = factor_t.T


def fourth_stage(fill, own, wide, *refs):
    refs = list(refs)
    if not fill:
        (high, low), refs = refs[:2], refs[2:]
    images, before, vectors_in, known, small, shifted, partials = refs[:7]
    if fill:
        high, low = refs[7:9]
    wide_image = refs[-1]
    unpack(images, wide_image)
    products = second_product(fill, own[...], wide, wide_image, high, low) + before[...]
    vectors = vectors_in[...]
    shift = small_matmul(small[...], assemble(products)) - known[...]
    shifted[...] = shift
    lanes = lax.broadcasted_iota(jnp.int32, (8, partials.shape[2]), 1)
    rows = lax.broadcasted_iota(jnp.int32, lanes.shape, 0)
    line = jnp.zeros(lanes.shape, F32)
    for row, column in enumerate(inner(shift, vectors)):
        line = jnp.where(lanes == 8 * row + rows, column, line)
    line = jnp.sum(line, axis=0, keepdims=True)
    partials[...] = jnp.broadcast_to(line[None], partials.shape)


def last_kernel(size, vectors, shifted, both, partials, basis, residual, coefficients):
    beads = basis.shape[2]
    width = partials.shape[2]
    total = jnp.sum(partials[...], axis=0) / size
    spread = jnp.broadcast_to(total, (8, width))
    rows = lax.broadcasted_iota(jnp.int32, spread.shape, 0)
    cols = lax.broadcasted_iota(jnp.int32, spread.shape, 1)
    block = vectors[...]
    left = shifted[...]
    transposed = jnp.where(cols % 8 == rows, spread, 0.0)
    for k in range(8):
        column = jnp.sum(jnp.where(cols // 8 == k, transposed, 0.0), axis=1, keepdims=True)
        left = left - column * block[k : k + 1, :]
    coefficients[0:2] = both[...]
    for k in range(8):
        coefficients[2, k : k + 1, :] = total[:, 8 * k : 8 * k + 8]
    for part in range(3):
        basis[part] = block[:, part * beads : (part + 1) * beads]
        residual[part] = left[:, part * beads : (part + 1) * beads]


def array(*shape, dtype=F32):
    return jax.ShapeDtypeStruct(shape, dtype)


def call(kernel, outs, scratch=(), **options):
    return pl.pallas_call(
        kernel,
        out_shape=outs,
        scratch_shapes=list(scratch),
        compiler_params=pltpu.CompilerParams(vmem_limit_bytes=48 * 1024 * 1024),
        **options,
    )


def to_all(copies):
    return lax.all_to_all(copies, ("row", "col"), 0, 0, tiled=True)


def gather(copies):
    mine = to_all(copies.reshape((-1,) + copies.shape[2:]))
    cols = lax.axis_size("col")
    return mine, lax.ppermute(mine, "col", [(col, col ^ 1) for col in range(cols)])


def local(positions, noise):
    vecs, _, beads = noise.shape
    devices = lax.axis_size("row") * lax.axis_size("col")
    total = beads * devices // 2
    size = 3.0 * beads * devices
    keep = 2 * 2 * 2 * 6 * beads * total <= KEPT
    width = total if keep else min(total, CHUNK)
    block = array(vecs, 4 * beads)
    copies = array(devices // 2, 2, vecs, 2 * beads)
    products = array(4 * vecs, 6 * beads)
    wide, held_wide = array(4 * vecs, total), pltpu.VMEM((4 * vecs, total), F32)
    kept = [array(6 * beads, width, dtype=BF16)] * 2 if keep else []
    held = [] if keep else [pltpu.VMEM((6 * beads, width), BF16)] * 2

    arguments = [
        pltpu.with_memory_space_constraint(item, pltpu.HBM) for item in (positions, noise.transpose(1, 0, 2))
    ]
    own, own_copies = call(
        pack_kernel,
        [block, copies],
        [pltpu.VMEM(item.shape, F32) for item in arguments] + [pltpu.SemaphoreType.DMA((2,))],
        in_specs=[pl.BlockSpec(memory_space=pltpu.HBM)] * 2,
    )(*arguments)
    one, two = gather(own_copies)
    partial, sums, one_wide, *one_tensor = call(
        functools.partial(first_stage, size, False), [products, array(4 * vecs, 4 * vecs), wide] + kept, held
    )(own, one)
    first, image, images, two_wide, *two_tensor = call(
        functools.partial(first_stage, size, True), [block, block, copies, wide] + kept, held
    )(own, two, partial, sums)
    one, two = gather(images)
    partial, vectors, known, small, both = call(
        functools.partial(third_stage, size, not keep),
        [products, block, block, array(vecs, vecs), array(2, vecs, vecs)],
        held + [held_wide],
    )(own, one_wide, *one_tensor, one, first, image)
    shifted, partials = call(
        functools.partial(fourth_stage, not keep), [block, array(devices, 1, vecs * vecs)], held + [held_wide]
    )(own, two_wide, *two_tensor, two, partial, vectors, known, small)
    partials = to_all(partials)
    basis, residual, coefficients = call(
        functools.partial(last_kernel, size),
        [array(3, vecs, beads), array(3, vecs, beads), array(3, vecs, vecs)],
    )(vectors, shifted, both, partials)
    return (basis.transpose(1, 0, 2), residual.transpose(1, 0, 2), coefficients)


def solution(mesh):
    return jax.shard_map(
        local,
        mesh=mesh,
        in_specs=(P(None, ("row", "col")), P(None, None, ("row", "col"))),
        out_specs=(P(None, None, ("row", "col")), P(None, None, ("row", "col")), P()),
        check_vma=False,
    )
```

```python
import functools

import jax
import jax.numpy as jnp
from jax import lax
from jax.experimental import pallas as pl
from jax.experimental.pallas import tpu as pltpu
from jax.sharding import PartitionSpec as P

CHUNK = 1024
KEPT = 8 * 1024 * 1024
F32 = jnp.float32
BF16 = jnp.bfloat16


def copy_halves(block, copies, extra=None):
    beads = block.shape[1] // 4
    middle = beads // 2
    for core in range(2):
        parts = [block[:, part * beads + core * middle : part * beads + (core + 1) * middle] for part in range(4)]
        half = jnp.concatenate(parts, axis=1)
        if extra is not None:
            half = half + extra
        copies[:, core] = jnp.broadcast_to(half[None], (copies.shape[0],) + half.shape)


def pack_kernel(positions, noise, block, copies, held_positions, held_noise, sems):
    reads = [
        pltpu.make_async_copy(positions, held_positions, sems.at[0]),
        pltpu.make_async_copy(noise, held_noise, sems.at[1]),
    ]
    for read in reads:
        read.start()
    beads = block.shape[1] // 4
    block[...] = jnp.zeros(block.shape, F32)
    for read in reads:
        read.wait()
    for part in range(3):
        block[:, part * beads : (part + 1) * beads] = held_noise[part]
    block[:3, 3 * beads :] = held_positions[...]
    copy_halves(block[...], copies)


def split_two(value):
    high = value.astype(BF16)
    return high, (value - high.astype(F32)).astype(BF16)


def matmul_nt(left, right, precision=None):
    return lax.dot_general(
        left, right, (((1,), (1,)), ((), ())), precision=precision, preferred_element_type=F32
    )


def small_matmul(left, right):
    total = left[:, 0:1] * right[0:1, :]
    for k in range(1, left.shape[1]):
        total = total + left[:, k : k + 1] * right[k : k + 1, :]
    return total


def unpack(blocks, wide):
    count, vecs, lanes = blocks.shape
    width = lanes // 4
    for at in range(0, count, 4):
        four = [blocks[at + index] for index in range(4)]
        for part in range(4):
            wide[part * vecs : (part + 1) * vecs, pl.ds(at * width, 4 * width)] = jnp.concatenate(
                [block[:, part * width : (part + 1) * width] for block in four], axis=1
            )


def target_columns(own):
    beads = own.shape[1] // 4
    targets = own[:, 3 * beads :].T
    return [jnp.broadcast_to(targets[:, axis : axis + 1], (beads, 128)) for axis in range(3)]


def tensor(columns, wide, start):
    moved = [columns[axis] - wide[24 + axis : 25 + axis, pl.ds(start, 128)] for axis in range(3)]
    square = moved[0] * moved[0] + moved[1] * moved[1] + moved[2] * moved[2]
    square = jnp.maximum(square, 1e-12)
    inverse = lax.rsqrt(square)
    inverse_sq = inverse * inverse
    near = square < 4.0
    iso = inverse * jnp.where(near, square * (inverse - 9.0 / 32.0), 0.75 + 0.5 * inverse_sq)
    along = inverse * jnp.where(near, 3.0 / 32.0, inverse_sq * (0.75 - 1.5 * inverse_sq))
    scaled = [along * item for item in moved]
    parts = [
        iso + scaled[0] * moved[0],
        scaled[0] * moved[1],
        scaled[0] * moved[2],
        iso + scaled[1] * moved[1],
        scaled[1] * moved[2],
        iso + scaled[2] * moved[2],
    ]
    highs, lows = zip(*[split_two(value) for value in parts])
    return jnp.concatenate(highs, axis=0), jnp.concatenate(lows, axis=0)


def apply_tensor(both, high, low):
    half = both.shape[0] // 2
    first = matmul_nt(both, high)
    return first[:half] + first[half:] + matmul_nt(both[:half], low)


def split_rows(*values):
    highs, lows = zip(*[split_two(value) for value in values])
    return jnp.concatenate(highs + lows, axis=0)


def inner(left, right):
    return [jnp.sum(left * right[row : row + 1], axis=1, keepdims=True) for row in range(right.shape[0])]


def assemble(products):
    beads = products.shape[1] // 6

    def part(row, component):
        return products[8 * row : 8 * row + 8, component * beads : (component + 1) * beads]

    x = part(0, 0) + part(1, 1) + part(2, 2)
    y = part(0, 1) + part(1, 3) + part(2, 4)
    z = part(0, 2) + part(1, 4) + part(2, 5)
    return jnp.concatenate([x, y, z, jnp.zeros(x.shape, F32)], axis=1)


def filled_product(columns, source, wide, start, high, low):
    width = high.shape[1]
    products = jnp.zeros((32, high.shape[0]), F32)
    for at in range(0, width, 512):
        step = min(512, width - at)
        lanes = pl.ds(at, step)
        both = split_rows(wide[:, pl.ds(pl.multiple_of(start + at, 128), step)])
        pieces = [
            tensor(columns, source, pl.multiple_of(start + part, 128)) for part in range(at, at + step, 128)
        ]
        upper, lower = [jnp.concatenate(piece, axis=1) for piece in zip(*pieces)]
        high[:, lanes] = upper
        low[:, lanes] = lower
        products = products + apply_tensor(both, upper, lower)
    return products


def all_filled(own, source, wide, high, low):
    columns = target_columns(own)
    width = high.shape[1]
    chunk = lambda start: filled_product(columns, source, wide, start, high, low)
    if wide.shape[1] == width:
        return chunk(0)
    body = lambda index, total: total + chunk(index * width)
    return lax.fori_loop(1, wide.shape[1] // width, body, chunk(0))


def without_positions(block):
    lanes = lax.broadcasted_iota(jnp.int32, block.shape, 1)
    return jnp.where(lanes < block.shape[1] // 4 * 3, block, 0.0)


def row_sums(wide):
    total = jnp.zeros((wide.shape[0], wide.shape[0]), F32)
    for at in range(0, wide.shape[1], CHUNK):
        both = split_rows(wide[:, at : min(at + CHUNK, wide.shape[1])])
        half = both.shape[0] // 2
        first, second = matmul_nt(both, both[:half]), matmul_nt(both, both[half:])
        total = total + ((first[:half] + first[half:]) + (second[:half] + second[half:]))
    return total


def first_stage(size, last, own, blocks, *refs):
    refs = list(refs)
    if last:
        before, before_sums, first_out, image, copies, wide, high, low = refs
    else:
        out, sums_out, wide, high, low = refs
    unpack(blocks, wide)
    sums = row_sums(wide)
    products = all_filled(own[...], wide, wide, high, low)
    if not last:
        out[...], sums_out[...] = products, sums
        return
    sums = (sums + before_sums[...]) / size
    _, inverse = cholesky(sums[:8, :8] + sums[8:16, 8:16] + sums[16:24, 16:24])
    first = small_matmul(inverse, without_positions(own[...]))
    block = small_matmul(inverse, assemble(products + before[...]))
    first_out[...] = first
    image[...] = block
    columns = inner(first, block) + inner(block, block)
    lanes = lax.broadcasted_iota(jnp.int32, (block.shape[0], block.shape[1] // 2), 1)
    shares = jnp.zeros(lanes.shape, F32)
    for index, column in enumerate(columns):
        shares = jnp.where(lanes == block.shape[1] // 8 * 3 + index, column, shares)
    copy_halves(block, copies, shares)


def cholesky(matrix):
    size = matrix.shape[0]
    shape = (size, size)
    rows = lax.broadcasted_iota(jnp.int32, shape, 0)
    cols = lax.broadcasted_iota(jnp.int32, shape, 1)
    entry = {}
    for j in range(size):
        column = jnp.broadcast_to(matrix[:, j : j + 1], shape)
        for i in range(j, size):
            entry[i, j] = jnp.broadcast_to(column[i : i + 1, :], shape)
    factor_t = jnp.zeros(shape, F32)
    inverse = jnp.zeros(shape, F32)
    inverse_rows = []
    for j in range(size):
        scale = lax.rsqrt(entry[j, j])
        lower_row = entry[j, j] * scale
        entry[j, j] = scale
        for i in range(j + 1, size):
            entry[i, j] = entry[i, j] * scale
        for i in range(j + 1, size):
            for k in range(j + 1, i + 1):
                entry[i, k] = entry[i, k] - entry[i, j] * entry[k, j]
        lower_row = jnp.where(cols == j, lower_row, 0.0)
        for i in range(j + 1, size):
            lower_row = jnp.where(cols == i, entry[i, j], lower_row)
        factor_t = jnp.where(rows == j, lower_row, factor_t)
        row = jnp.where(cols == j, 1.0, 0.0)
        for k in range(j):
            row = row - entry[j, k] * inverse_rows[k]
        row = row * scale
        inverse_rows.append(row)
        inverse = jnp.where(rows == j, row, inverse)
    return factor_t, inverse


def second_product(fill, own, wide, wide_image, high, low):
    if fill:
        return all_filled(own, wide, wide_image, high, low)
    return apply_tensor(split_rows(wide_image[...]), high[...], low[...])


def third_stage(size, fill, own, wide, *refs):
    refs = list(refs)
    if not fill:
        (high, low), refs = refs[:2], refs[2:]
    images, own_first, own_image, products, vectors, known, small, coefficients = refs[:8]
    if fill:
        high, low = refs[8:10]
    wide_image = refs[-1]
    unpack(images, wide_image)
    products[...] = second_product(fill, own[...], wide, wide_image, high, low)
    sums = wide_image[24:, :128]
    for at in range(128, wide_image.shape[1], 128):
        sums = sums + wide_image[24:, at : at + 128]
    width = own.shape[1] // 8
    sums = sum(sums[:, at : at + width] for at in range(width, 128, width)) + sums[:, :width]
    sums = sums / size
    alpha = sums[:, :8]
    alpha_t = alpha.T
    factor_t, inverse = cholesky(sums[:, 8:16] - small_matmul(alpha_t, alpha))
    first, image = own_first[...], own_image[...]
    vectors[...] = small_matmul(inverse, image - small_matmul(alpha_t, first))
    known[...] = small_matmul(inverse, small_matmul(alpha_t, image)) + small_matmul(factor_t, first)
    small[...] = inverse
    coefficients[0] = alpha
    coefficients[1] = factor_t.T


def fourth_stage(fill, own, wide, *refs):
    refs = list(refs)
    if not fill:
        (high, low), refs = refs[:2], refs[2:]
    images, before, vectors_in, known, small, shifted, partials = refs[:7]
    if fill:
        high, low = refs[7:9]
    wide_image = refs[-1]
    unpack(images, wide_image)
    products = second_product(fill, own[...], wide, wide_image, high, low) + before[...]
    vectors = vectors_in[...]
    shift = small_matmul(small[...], assemble(products)) - known[...]
    shifted[...] = shift
    lanes = lax.broadcasted_iota(jnp.int32, (8, partials.shape[2]), 1)
    rows = lax.broadcasted_iota(jnp.int32, lanes.shape, 0)
    line = jnp.zeros(lanes.shape, F32)
    for row, column in enumerate(inner(shift, vectors)):
        line = jnp.where(lanes == 8 * row + rows, column, line)
    line = jnp.sum(line, axis=0, keepdims=True)
    partials[...] = jnp.broadcast_to(line[None], partials.shape)


def last_kernel(size, vectors, shifted, both, partials, basis, residual, coefficients):
    beads = basis.shape[2]
    width = partials.shape[2]
    total = jnp.sum(partials[...], axis=0) / size
    spread = jnp.broadcast_to(total, (8, width))
    rows = lax.broadcasted_iota(jnp.int32, spread.shape, 0)
    cols = lax.broadcasted_iota(jnp.int32, spread.shape, 1)
    block = vectors[...]
    left = shifted[...]
    transposed = jnp.where(cols % 8 == rows, spread, 0.0)
    for k in range(8):
        column = jnp.sum(jnp.where(cols // 8 == k, transposed, 0.0), axis=1, keepdims=True)
        left = left - column * block[k : k + 1, :]
    coefficients[0:2] = both[...]
    for k in range(8):
        coefficients[2, k : k + 1, :] = total[:, 8 * k : 8 * k + 8]
    for part in range(3):
        basis[part] = block[:, part * beads : (part + 1) * beads]
        residual[part] = left[:, part * beads : (part + 1) * beads]


def array(*shape, dtype=F32):
    return jax.ShapeDtypeStruct(shape, dtype)


def call(kernel, outs, scratch=(), **options):
    return pl.pallas_call(
        kernel,
        out_shape=outs,
        scratch_shapes=list(scratch),
        compiler_params=pltpu.CompilerParams(vmem_limit_bytes=48 * 1024 * 1024),
        **options,
    )


def to_all(copies):
    return lax.all_to_all(copies, ("row", "col"), 0, 0, tiled=True)


def gather(copies):
    mine = to_all(copies.reshape((-1,) + copies.shape[2:]))
    cols = lax.axis_size("col")
    return mine, lax.ppermute(mine, "col", [(col, col ^ 1) for col in range(cols)])


def local(positions, noise):
    vecs, _, beads = noise.shape
    devices = lax.axis_size("row") * lax.axis_size("col")
    total = beads * devices // 2
    size = 3.0 * beads * devices
    keep = 2 * 2 * 2 * 6 * beads * total <= KEPT
    width = total if keep else min(total, CHUNK)
    block = array(vecs, 4 * beads)
    copies = array(devices // 2, 2, vecs, 2 * beads)
    products = array(4 * vecs, 6 * beads)
    wide, held_wide = array(4 * vecs, total), pltpu.VMEM((4 * vecs, total), F32)
    kept = [array(6 * beads, width, dtype=BF16)] * 2 if keep else []
    held = [] if keep else [pltpu.VMEM((6 * beads, width), BF16)] * 2

    arguments = [
        pltpu.with_memory_space_constraint(item, pltpu.HBM) for item in (positions, noise.transpose(1, 0, 2))
    ]
    own, own_copies = call(
        pack_kernel,
        [block, copies],
        [pltpu.VMEM(item.shape, F32) for item in arguments] + [pltpu.SemaphoreType.DMA((2,))],
        in_specs=[pl.BlockSpec(memory_space=pltpu.HBM)] * 2,
    )(*arguments)
    one, two = gather(own_copies)
    partial, sums, one_wide, *one_tensor = call(
        functools.partial(first_stage, size, False), [products, array(4 * vecs, 4 * vecs), wide] + kept, held
    )(own, one)
    first, image, images, two_wide, *two_tensor = call(
        functools.partial(first_stage, size, True), [block, block, copies, wide] + kept, held
    )(own, two, partial, sums)
    one, two = gather(images)
    partial, vectors, known, small, both = call(
        functools.partial(third_stage, size, not keep),
        [products, block, block, array(vecs, vecs), array(2, vecs, vecs)],
        held + [held_wide],
    )(own, one_wide, *one_tensor, one, first, image)
    shifted, partials = call(
        functools.partial(fourth_stage, not keep), [block, array(devices, 1, vecs * vecs)], held + [held_wide]
    )(own, two_wide, *two_tensor, two, partial, vectors, known, small)
    partials = to_all(partials)
    basis, residual, coefficients = call(
        functools.partial(last_kernel, size),
        [array(3, vecs, beads), array(3, vecs, beads), array(3, vecs, vecs)],
    )(vectors, shifted, both, partials)
    return (basis.transpose(1, 0, 2), residual.transpose(1, 0, 2), coefficients)


def solution(mesh):
    return jax.shard_map(
        local,
        mesh=mesh,
        in_specs=(P(None, ("row", "col")), P(None, None, ("row", "col"))),
        out_specs=(P(None, None, ("row", "col")), P(None, None, ("row", "col")), P()),
        check_vma=False,
    )
```

```python
import functools

import jax
import jax.numpy as jnp
from jax import lax
from jax.experimental import pallas as pl
from jax.experimental.pallas import tpu as pltpu
from jax.sharding import PartitionSpec as P

CHUNK = 1024
KEPT = 8 * 1024 * 1024
F32 = jnp.float32
BF16 = jnp.bfloat16


def copy_halves(block, copies, extra=None):
    beads = block.shape[1] // 4
    middle = beads // 2
    for core in range(2):
        parts = [block[:, part * beads + core * middle : part * beads + (core + 1) * middle] for part in range(4)]
        half = jnp.concatenate(parts, axis=1)
        if extra is not None:
            half = half + extra
        copies[:, core] = jnp.broadcast_to(half[None], (copies.shape[0],) + half.shape)


def pack_kernel(positions, noise, block, copies, held_positions, held_noise, sems):
    reads = [
        pltpu.make_async_copy(positions, held_positions, sems.at[0]),
        pltpu.make_async_copy(noise, held_noise, sems.at[1]),
    ]
    for read in reads:
        read.start()
    beads = block.shape[1] // 4
    block[...] = jnp.zeros(block.shape, F32)
    for read in reads:
        read.wait()
    for part in range(3):
        block[:, part * beads : (part + 1) * beads] = held_noise[part]
    block[:3, 3 * beads :] = held_positions[...]
    copy_halves(block[...], copies)


def split_two(value):
    high = value.astype(BF16)
    return high, (value - high.astype(F32)).astype(BF16)


def matmul_nt(left, right, precision=None):
    return lax.dot_general(
        left, right, (((1,), (1,)), ((), ())), precision=precision, preferred_element_type=F32
    )


def small_matmul(left, right):
    total = left[:, 0:1] * right[0:1, :]
    for k in range(1, left.shape[1]):
        total = total + left[:, k : k + 1] * right[k : k + 1, :]
    return total


def unpack(blocks, wide):
    count, vecs, lanes = blocks.shape
    width = lanes // 4
    for at in range(0, count, 4):
        four = [blocks[at + index] for index in range(4)]
        for part in range(4):
            wide[part * vecs : (part + 1) * vecs, pl.ds(at * width, 4 * width)] = jnp.concatenate(
                [block[:, part * width : (part + 1) * width] for block in four], axis=1
            )


def target_columns(own):
    beads = own.shape[1] // 4
    targets = own[:, 3 * beads :].T
    return [jnp.broadcast_to(targets[:, axis : axis + 1], (beads, 128)) for axis in range(3)]


def tensor(columns, wide, start):
    moved = [columns[axis] - wide[24 + axis : 25 + axis, pl.ds(start, 128)] for axis in range(3)]
    square = moved[0] * moved[0] + moved[1] * moved[1] + moved[2] * moved[2]
    square = jnp.maximum(square, 1e-12)
    inverse = lax.rsqrt(square)
    inverse_sq = inverse * inverse
    near = square < 4.0
    iso = inverse * jnp.where(near, square * (inverse - 9.0 / 32.0), 0.75 + 0.5 * inverse_sq)
    along = inverse * jnp.where(near, 3.0 / 32.0, inverse_sq * (0.75 - 1.5 * inverse_sq))
    scaled = [along * item for item in moved]
    parts = [
        iso + scaled[0] * moved[0],
        scaled[0] * moved[1],
        scaled[0] * moved[2],
        iso + scaled[1] * moved[1],
        scaled[1] * moved[2],
        iso + scaled[2] * moved[2],
    ]
    highs, lows = zip(*[split_two(value) for value in parts])
    return jnp.concatenate(highs, axis=0), jnp.concatenate(lows, axis=0)


def apply_tensor(both, high, low):
    half = both.shape[0] // 2
    first = matmul_nt(both, high)
    return first[:half] + first[half:] + matmul_nt(both[:half], low)


def split_rows(*values):
    highs, lows = zip(*[split_two(value) for value in values])
    return jnp.concatenate(highs + lows, axis=0)


def inner(left, right):
    return [jnp.sum(left * right[row : row + 1], axis=1, keepdims=True) for row in range(right.shape[0])]


def assemble(products):
    beads = products.shape[1] // 6

    def part(row, component):
        return products[8 * row : 8 * row + 8, component * beads : (component + 1) * beads]

    x = part(0, 0) + part(1, 1) + part(2, 2)
    y = part(0, 1) + part(1, 3) + part(2, 4)
    z = part(0, 2) + part(1, 4) + part(2, 5)
    return jnp.concatenate([x, y, z, jnp.zeros(x.shape, F32)], axis=1)


def filled_product(columns, source, wide, start, high, low):
    width = high.shape[1]
    products = jnp.zeros((32, high.shape[0]), F32)
    for at in range(0, width, 1024):
        step = min(1024, width - at)
        lanes = pl.ds(at, step)
        both = split_rows(wide[:, pl.ds(pl.multiple_of(start + at, 128), step)])
        pieces = [
            tensor(columns, source, pl.multiple_of(start + part, 128)) for part in range(at, at + step, 128)
        ]
        upper, lower = [jnp.concatenate(piece, axis=1) for piece in zip(*pieces)]
        high[:, lanes] = upper
        low[:, lanes] = lower
        products = products + apply_tensor(both, upper, lower)
    return products


def all_filled(own, source, wide, high, low):
    columns = target_columns(own)
    width = high.shape[1]
    chunk = lambda start: filled_product(columns, source, wide, start, high, low)
    if wide.shape[1] == width:
        return chunk(0)
    body = lambda index, total: total + chunk(index * width)
    return lax.fori_loop(1, wide.shape[1] // width, body, chunk(0))


def without_positions(block):
    lanes = lax.broadcasted_iota(jnp.int32, block.shape, 1)
    return jnp.where(lanes < block.shape[1] // 4 * 3, block, 0.0)


def row_sums(wide):
    total = jnp.zeros((wide.shape[0], wide.shape[0]), F32)
    for at in range(0, wide.shape[1], CHUNK):
        both = split_rows(wide[:, at : min(at + CHUNK, wide.shape[1])])
        half = both.shape[0] // 2
        first, second = matmul_nt(both, both[:half]), matmul_nt(both, both[half:])
        total = total + ((first[:half] + first[half:]) + (second[:half] + second[half:]))
    return total


def first_stage(size, last, own, blocks, *refs):
    refs = list(refs)
    if last:
        before, before_sums, first_out, image, copies, wide, high, low = refs
    else:
        out, sums_out, wide, high, low = refs
    unpack(blocks, wide)
    sums = row_sums(wide)
    products = all_filled(own[...], wide, wide, high, low)
    if not last:
        out[...], sums_out[...] = products, sums
        return
    sums = (sums + before_sums[...]) / size
    _, inverse = cholesky(sums[:8, :8] + sums[8:16, 8:16] + sums[16:24, 16:24])
    first = small_matmul(inverse, without_positions(own[...]))
    block = small_matmul(inverse, assemble(products + before[...]))
    first_out[...] = first
    image[...] = block
    columns = inner(first, block) + inner(block, block)
    lanes = lax.broadcasted_iota(jnp.int32, (block.shape[0], block.shape[1] // 2), 1)
    shares = jnp.zeros(lanes.shape, F32)
    for index, column in enumerate(columns):
        shares = jnp.where(lanes == block.shape[1] // 8 * 3 + index, column, shares)
    copy_halves(block, copies, shares)


def cholesky(matrix):
    size = matrix.shape[0]
    shape = (size, size)
    rows = lax.broadcasted_iota(jnp.int32, shape, 0)
    cols = lax.broadcasted_iota(jnp.int32, shape, 1)
    entry = {}
    for j in range(size):
        column = jnp.broadcast_to(matrix[:, j : j + 1], shape)
        for i in range(j, size):
            entry[i, j] = jnp.broadcast_to(column[i : i + 1, :], shape)
    factor_t = jnp.zeros(shape, F32)
    inverse = jnp.zeros(shape, F32)
    inverse_rows = []
    for j in range(size):
        scale = lax.rsqrt(entry[j, j])
        lower_row = entry[j, j] * scale
        entry[j, j] = scale
        for i in range(j + 1, size):
            entry[i, j] = entry[i, j] * scale
        for i in range(j + 1, size):
            for k in range(j + 1, i + 1):
                entry[i, k] = entry[i, k] - entry[i, j] * entry[k, j]
        lower_row = jnp.where(cols == j, lower_row, 0.0)
        for i in range(j + 1, size):
            lower_row = jnp.where(cols == i, entry[i, j], lower_row)
        factor_t = jnp.where(rows == j, lower_row, factor_t)
        row = jnp.where(cols == j, 1.0, 0.0)
        for k in range(j):
            row = row - entry[j, k] * inverse_rows[k]
        row = row * scale
        inverse_rows.append(row)
        inverse = jnp.where(rows == j, row, inverse)
    return factor_t, inverse


def second_product(fill, own, wide, wide_image, high, low):
    if fill:
        return all_filled(own, wide, wide_image, high, low)
    return apply_tensor(split_rows(wide_image[...]), high[...], low[...])


def third_stage(size, fill, own, wide, *refs):
    refs = list(refs)
    if not fill:
        (high, low), refs = refs[:2], refs[2:]
    images, own_first, own_image, products, vectors, known, small, coefficients = refs[:8]
    if fill:
        high, low = refs[8:10]
    wide_image = refs[-1]
    unpack(images, wide_image)
    products[...] = second_product(fill, own[...], wide, wide_image, high, low)
    sums = wide_image[24:, :128]
    for at in range(128, wide_image.shape[1], 128):
        sums = sums + wide_image[24:, at : at + 128]
    width = own.shape[1] // 8
    sums = sum(sums[:, at : at + width] for at in range(width, 128, width)) + sums[:, :width]
    sums = sums / size
    alpha = sums[:, :8]
    alpha_t = alpha.T
    factor_t, inverse = cholesky(sums[:, 8:16] - small_matmul(alpha_t, alpha))
    first, image = own_first[...], own_image[...]
    vectors[...] = small_matmul(inverse, image - small_matmul(alpha_t, first))
    known[...] = small_matmul(inverse, small_matmul(alpha_t, image)) + small_matmul(factor_t, first)
    small[...] = inverse
    coefficients[0] = alpha
    coefficients[1] = factor_t.T


def fourth_stage(fill, own, wide, *refs):
    refs = list(refs)
    if not fill:
        (high, low), refs = refs[:2], refs[2:]
    images, before, vectors_in, known, small, shifted, partials = refs[:7]
    if fill:
        high, low = refs[7:9]
    wide_image = refs[-1]
    unpack(images, wide_image)
    products = second_product(fill, own[...], wide, wide_image, high, low) + before[...]
    vectors = vectors_in[...]
    shift = small_matmul(small[...], assemble(products)) - known[...]
    shifted[...] = shift
    lanes = lax.broadcasted_iota(jnp.int32, (8, partials.shape[2]), 1)
    rows = lax.broadcasted_iota(jnp.int32, lanes.shape, 0)
    line = jnp.zeros(lanes.shape, F32)
    for row, column in enumerate(inner(shift, vectors)):
        line = jnp.where(lanes == 8 * row + rows, column, line)
    line = jnp.sum(line, axis=0, keepdims=True)
    partials[...] = jnp.broadcast_to(line[None], partials.shape)


def last_kernel(size, vectors, shifted, both, partials, basis, residual, coefficients):
    beads = basis.shape[2]
    width = partials.shape[2]
    parts = [partials[index] for index in range(partials.shape[0])]
    while len(parts) > 1:
        parts = [sum(parts[at : at + 2]) for at in range(0, len(parts), 2)]
    total = parts[0] / size
    spread = jnp.broadcast_to(total, (8, width))
    rows = lax.broadcasted_iota(jnp.int32, spread.shape, 0)
    cols = lax.broadcasted_iota(jnp.int32, spread.shape, 1)
    block = vectors[...]
    left = shifted[...]
    transposed = jnp.where(cols % 8 == rows, spread, 0.0)
    for k in range(8):
        column = jnp.sum(jnp.where(cols // 8 == k, transposed, 0.0), axis=1, keepdims=True)
        left = left - column * block[k : k + 1, :]
    coefficients[0:2] = both[...]
    for k in range(8):
        coefficients[2, k : k + 1, :] = total[:, 8 * k : 8 * k + 8]
    for part in range(3):
        basis[part] = block[:, part * beads : (part + 1) * beads]
        residual[part] = left[:, part * beads : (part + 1) * beads]


def array(*shape, dtype=F32):
    return jax.ShapeDtypeStruct(shape, dtype)


def call(kernel, outs, scratch=(), **options):
    return pl.pallas_call(
        kernel,
        out_shape=outs,
        scratch_shapes=list(scratch),
        compiler_params=pltpu.CompilerParams(vmem_limit_bytes=48 * 1024 * 1024),
        **options,
    )


def to_all(copies):
    return lax.all_to_all(copies, ("row", "col"), 0, 0, tiled=True)


def gather(copies):
    mine = to_all(copies.reshape((-1,) + copies.shape[2:]))
    cols = lax.axis_size("col")
    return mine, lax.ppermute(mine, "col", [(col, col ^ 1) for col in range(cols)])


def local(positions, noise):
    vecs, _, beads = noise.shape
    devices = lax.axis_size("row") * lax.axis_size("col")
    total = beads * devices // 2
    size = 3.0 * beads * devices
    keep = 2 * 2 * 2 * 6 * beads * total <= KEPT
    width = total if keep else min(total, CHUNK)
    block = array(vecs, 4 * beads)
    copies = array(devices // 2, 2, vecs, 2 * beads)
    products = array(4 * vecs, 6 * beads)
    wide, held_wide = array(4 * vecs, total), pltpu.VMEM((4 * vecs, total), F32)
    kept = [array(6 * beads, width, dtype=BF16)] * 2 if keep else []
    held = [] if keep else [pltpu.VMEM((6 * beads, width), BF16)] * 2

    arguments = [
        pltpu.with_memory_space_constraint(item, pltpu.HBM) for item in (positions, noise.transpose(1, 0, 2))
    ]
    own, own_copies = call(
        pack_kernel,
        [block, copies],
        [pltpu.VMEM(item.shape, F32) for item in arguments] + [pltpu.SemaphoreType.DMA((2,))],
        in_specs=[pl.BlockSpec(memory_space=pltpu.HBM)] * 2,
    )(*arguments)
    one, two = gather(own_copies)
    partial, sums, one_wide, *one_tensor = call(
        functools.partial(first_stage, size, False), [products, array(4 * vecs, 4 * vecs), wide] + kept, held
    )(own, one)
    first, image, images, two_wide, *two_tensor = call(
        functools.partial(first_stage, size, True), [block, block, copies, wide] + kept, held
    )(own, two, partial, sums)
    one, two = gather(images)
    partial, vectors, known, small, both = call(
        functools.partial(third_stage, size, not keep),
        [products, block, block, array(vecs, vecs), array(2, vecs, vecs)],
        held + [held_wide],
    )(own, one_wide, *one_tensor, one, first, image)
    shifted, partials = call(
        functools.partial(fourth_stage, not keep), [block, array(devices, 1, vecs * vecs)], held + [held_wide]
    )(own, two_wide, *two_tensor, two, partial, vectors, known, small)
    partials = to_all(partials)
    basis, residual, coefficients = call(
        functools.partial(last_kernel, size),
        [array(3, vecs, beads), array(3, vecs, beads), array(3, vecs, vecs)],
    )(vectors, shifted, both, partials)
    return (basis.transpose(1, 0, 2), residual.transpose(1, 0, 2), coefficients)


def solution(mesh):
    return jax.shard_map(
        local,
        mesh=mesh,
        in_specs=(P(None, ("row", "col")), P(None, None, ("row", "col"))),
        out_specs=(P(None, None, ("row", "col")), P(None, None, ("row", "col")), P()),
        check_vma=False,
    )
```

```python
import functools

import jax
import jax.numpy as jnp
from jax import lax
from jax.experimental import pallas as pl
from jax.experimental.pallas import tpu as pltpu
from jax.sharding import PartitionSpec as P

CHUNK = 1024
KEPT = 8 * 1024 * 1024
F32 = jnp.float32
BF16 = jnp.bfloat16


def copy_halves(block, copies, extra=None):
    beads = block.shape[1] // 4
    middle = beads // 2
    for core in range(2):
        parts = [block[:, part * beads + core * middle : part * beads + (core + 1) * middle] for part in range(4)]
        half = jnp.concatenate(parts, axis=1)
        if extra is not None:
            half = half + extra
        copies[:, core] = jnp.broadcast_to(half[None], (copies.shape[0],) + half.shape)


def pack_kernel(positions, noise, block, copies, held_positions, held_noise, sems):
    reads = [
        pltpu.make_async_copy(positions, held_positions, sems.at[0]),
        pltpu.make_async_copy(noise, held_noise, sems.at[1]),
    ]
    for read in reads:
        read.start()
    beads = block.shape[1] // 4
    block[...] = jnp.zeros(block.shape, F32)
    for read in reads:
        read.wait()
    for part in range(3):
        block[:, part * beads : (part + 1) * beads] = held_noise[part]
    block[:3, 3 * beads :] = held_positions[...]
    copy_halves(block[...], copies)


def split_two(value):
    high = value.astype(BF16)
    return high, (value - high.astype(F32)).astype(BF16)


def matmul_nt(left, right, precision=None):
    return lax.dot_general(
        left, right, (((1,), (1,)), ((), ())), precision=precision, preferred_element_type=F32
    )


def small_matmul(left, right):
    total = left[:, 0:1] * right[0:1, :]
    for k in range(1, left.shape[1]):
        total = total + left[:, k : k + 1] * right[k : k + 1, :]
    return total


def unpack(blocks, wide):
    count, vecs, lanes = blocks.shape
    width = lanes // 4
    for at in range(0, count, 4):
        four = [blocks[at + index] for index in range(4)]
        for part in range(4):
            wide[part * vecs : (part + 1) * vecs, pl.ds(at * width, 4 * width)] = jnp.concatenate(
                [block[:, part * width : (part + 1) * width] for block in four], axis=1
            )


def target_columns(own):
    beads = own.shape[1] // 4
    targets = own[:, 3 * beads :].T
    return [jnp.broadcast_to(targets[:, axis : axis + 1], (beads, 128)) for axis in range(3)]


def tensor(columns, wide, start):
    moved = [columns[axis] - wide[24 + axis : 25 + axis, pl.ds(start, 128)] for axis in range(3)]
    square = moved[0] * moved[0] + moved[1] * moved[1] + moved[2] * moved[2]
    square = jnp.maximum(square, 1e-12)
    inverse = lax.rsqrt(square)
    inverse_sq = inverse * inverse
    near = square < 4.0
    iso = inverse * jnp.where(near, square * (inverse - 9.0 / 32.0), 0.75 + 0.5 * inverse_sq)
    along = inverse * jnp.where(near, 3.0 / 32.0, inverse_sq * (0.75 - 1.5 * inverse_sq))
    scaled = [along * item for item in moved]
    parts = [
        iso + scaled[0] * moved[0],
        scaled[0] * moved[1],
        scaled[0] * moved[2],
        iso + scaled[1] * moved[1],
        scaled[1] * moved[2],
        iso + scaled[2] * moved[2],
    ]
    highs, lows = zip(*[split_two(value) for value in parts])
    return jnp.concatenate(highs, axis=0), jnp.concatenate(lows, axis=0)


def apply_tensor(both, high, low):
    half = both.shape[0] // 2
    first = matmul_nt(both, high)
    return first[:half] + first[half:] + matmul_nt(both[:half], low)


def split_rows(*values):
    highs, lows = zip(*[split_two(value) for value in values])
    return jnp.concatenate(highs + lows, axis=0)


def inner(left, right):
    return [jnp.sum(left * right[row : row + 1], axis=1, keepdims=True) for row in range(right.shape[0])]


def assemble(products):
    beads = products.shape[1] // 6

    def part(row, component):
        return products[8 * row : 8 * row + 8, component * beads : (component + 1) * beads]

    x = part(0, 0) + part(1, 1) + part(2, 2)
    y = part(0, 1) + part(1, 3) + part(2, 4)
    z = part(0, 2) + part(1, 4) + part(2, 5)
    return jnp.concatenate([x, y, z, jnp.zeros(x.shape, F32)], axis=1)


def filled_product(columns, source, wide, start, high, low):
    width = high.shape[1]
    products = jnp.zeros((32, high.shape[0]), F32)
    for at in range(0, width, 512):
        step = min(512, width - at)
        lanes = pl.ds(at, step)
        both = split_rows(wide[:, pl.ds(pl.multiple_of(start + at, 128), step)])
        pieces = [
            tensor(columns, source, pl.multiple_of(start + part, 128)) for part in range(at, at + step, 128)
        ]
        upper, lower = [jnp.concatenate(piece, axis=1) for piece in zip(*pieces)]
        high[:, lanes] = upper
        low[:, lanes] = lower
        products = products + apply_tensor(both, upper, lower)
    return products


def all_filled(own, source, wide, high, low):
    columns = target_columns(own)
    width = high.shape[1]
    chunk = lambda start: filled_product(columns, source, wide, start, high, low)
    if wide.shape[1] == width:
        return chunk(0)
    body = lambda index, total: total + chunk(index * width)
    return lax.fori_loop(1, wide.shape[1] // width, body, chunk(0))


def without_positions(block):
    lanes = lax.broadcasted_iota(jnp.int32, block.shape, 1)
    return jnp.where(lanes < block.shape[1] // 4 * 3, block, 0.0)


def row_sums(wide):
    total = jnp.zeros((wide.shape[0], wide.shape[0]), F32)
    for at in range(0, wide.shape[1], CHUNK):
        both = split_rows(wide[:, at : min(at + CHUNK, wide.shape[1])])
        half = both.shape[0] // 2
        first, second = matmul_nt(both, both[:half]), matmul_nt(both, both[half:])
        total = total + ((first[:half] + first[half:]) + (second[:half] + second[half:]))
    return total


def first_stage(size, last, own, blocks, *refs):
    refs = list(refs)
    if last:
        before, before_sums, first_out, image, copies, wide, high, low = refs
    else:
        out, sums_out, wide, high, low = refs
    unpack(blocks, wide)
    sums = row_sums(wide)
    products = all_filled(own[...], wide, wide, high, low)
    if not last:
        out[...], sums_out[...] = products, sums
        return
    sums = (sums + before_sums[...]) / size
    _, inverse = cholesky(sums[:8, :8] + sums[8:16, 8:16] + sums[16:24, 16:24])
    first = small_matmul(inverse, without_positions(own[...]))
    block = small_matmul(inverse, assemble(products + before[...]))
    first_out[...] = first
    image[...] = block
    columns = inner(first, block) + inner(block, block)
    lanes = lax.broadcasted_iota(jnp.int32, (block.shape[0], block.shape[1] // 2), 1)
    shares = jnp.zeros(lanes.shape, F32)
    for index, column in enumerate(columns):
        shares = jnp.where(lanes == block.shape[1] // 8 * 3 + index, column, shares)
    copy_halves(block, copies, shares)


def cholesky(matrix):
    size = matrix.shape[0]
    shape = (size, size)
    rows = lax.broadcasted_iota(jnp.int32, shape, 0)
    cols = lax.broadcasted_iota(jnp.int32, shape, 1)
    entry = {}
    for j in range(size):
        column = jnp.broadcast_to(matrix[:, j : j + 1], shape)
        for i in range(j, size):
            entry[i, j] = jnp.broadcast_to(column[i : i + 1, :], shape)
    factor_t = jnp.zeros(shape, F32)
    inverse = jnp.zeros(shape, F32)
    inverse_rows = []
    for j in range(size):
        scale = lax.rsqrt(entry[j, j])
        lower_row = entry[j, j] * scale
        entry[j, j] = scale
        for i in range(j + 1, size):
            entry[i, j] = entry[i, j] * scale
        for i in range(j + 1, size):
            for k in range(j + 1, i + 1):
                entry[i, k] = entry[i, k] - entry[i, j] * entry[k, j]
        lower_row = jnp.where(cols == j, lower_row, 0.0)
        for i in range(j + 1, size):
            lower_row = jnp.where(cols == i, entry[i, j], lower_row)
        factor_t = jnp.where(rows == j, lower_row, factor_t)
        row = jnp.where(cols == j, 1.0, 0.0)
        for k in range(j):
            row = row - entry[j, k] * inverse_rows[k]
        row = row * scale
        inverse_rows.append(row)
        inverse = jnp.where(rows == j, row, inverse)
    return factor_t, inverse


def second_product(fill, own, wide, wide_image, high, low):
    if fill:
        return all_filled(own, wide, wide_image, high, low)
    products = jnp.zeros((32, high.shape[0]), F32)
    for at in range(0, high.shape[1], 512):
        lanes = slice(at, min(at + 512, high.shape[1]))
        products = products + apply_tensor(split_rows(wide_image[:, lanes]), high[:, lanes], low[:, lanes])
    return products


def third_stage(size, fill, own, wide, *refs):
    refs = list(refs)
    if not fill:
        (high, low), refs = refs[:2], refs[2:]
    images, own_first, own_image, products, vectors, known, small, coefficients = refs[:8]
    if fill:
        high, low = refs[8:10]
    wide_image = refs[-1]
    unpack(images, wide_image)
    products[...] = second_product(fill, own[...], wide, wide_image, high, low)
    sums = wide_image[24:, :128]
    for at in range(128, wide_image.shape[1], 128):
        sums = sums + wide_image[24:, at : at + 128]
    width = own.shape[1] // 8
    sums = sum(sums[:, at : at + width] for at in range(width, 128, width)) + sums[:, :width]
    sums = sums / size
    alpha = sums[:, :8]
    alpha_t = alpha.T
    factor_t, inverse = cholesky(sums[:, 8:16] - small_matmul(alpha_t, alpha))
    first, image = own_first[...], own_image[...]
    vectors[...] = small_matmul(inverse, image - small_matmul(alpha_t, first))
    known[...] = small_matmul(inverse, small_matmul(alpha_t, image)) + small_matmul(factor_t, first)
    small[...] = inverse
    coefficients[0] = alpha
    coefficients[1] = factor_t.T


def fourth_stage(fill, own, wide, *refs):
    refs = list(refs)
    if not fill:
        (high, low), refs = refs[:2], refs[2:]
    images, before, vectors_in, known, small, shifted, partials = refs[:7]
    if fill:
        high, low = refs[7:9]
    wide_image = refs[-1]
    unpack(images, wide_image)
    products = second_product(fill, own[...], wide, wide_image, high, low) + before[...]
    vectors = vectors_in[...]
    shift = small_matmul(small[...], assemble(products)) - known[...]
    shifted[...] = shift
    lanes = lax.broadcasted_iota(jnp.int32, (8, partials.shape[2]), 1)
    rows = lax.broadcasted_iota(jnp.int32, lanes.shape, 0)
    line = jnp.zeros(lanes.shape, F32)
    for row, column in enumerate(inner(shift, vectors)):
        line = jnp.where(lanes == 8 * row + rows, column, line)
    line = jnp.sum(line, axis=0, keepdims=True)
    partials[...] = jnp.broadcast_to(line[None], partials.shape)


def last_kernel(size, vectors, shifted, both, partials, basis, residual, coefficients):
    beads = basis.shape[2]
    width = partials.shape[2]
    total = jnp.sum(partials[...], axis=0) / size
    spread = jnp.broadcast_to(total, (8, width))
    rows = lax.broadcasted_iota(jnp.int32, spread.shape, 0)
    cols = lax.broadcasted_iota(jnp.int32, spread.shape, 1)
    block = vectors[...]
    left = shifted[...]
    transposed = jnp.where(cols % 8 == rows, spread, 0.0)
    for k in range(8):
        column = jnp.sum(jnp.where(cols // 8 == k, transposed, 0.0), axis=1, keepdims=True)
        left = left - column * block[k : k + 1, :]
    coefficients[0:2] = both[...]
    for k in range(8):
        coefficients[2, k : k + 1, :] = total[:, 8 * k : 8 * k + 8]
    for part in range(3):
        basis[part] = block[:, part * beads : (part + 1) * beads]
        residual[part] = left[:, part * beads : (part + 1) * beads]


def array(*shape, dtype=F32):
    return jax.ShapeDtypeStruct(shape, dtype)


def call(kernel, outs, scratch=(), **options):
    return pl.pallas_call(
        kernel,
        out_shape=outs,
        scratch_shapes=list(scratch),
        compiler_params=pltpu.CompilerParams(vmem_limit_bytes=48 * 1024 * 1024),
        **options,
    )


def to_all(copies):
    return lax.all_to_all(copies, ("row", "col"), 0, 0, tiled=True)


def gather(copies):
    mine = to_all(copies.reshape((-1,) + copies.shape[2:]))
    cols = lax.axis_size("col")
    return mine, lax.ppermute(mine, "col", [(col, col ^ 1) for col in range(cols)])


def local(positions, noise):
    vecs, _, beads = noise.shape
    devices = lax.axis_size("row") * lax.axis_size("col")
    total = beads * devices // 2
    size = 3.0 * beads * devices
    keep = 2 * 2 * 2 * 6 * beads * total <= KEPT
    width = total if keep else min(total, CHUNK)
    block = array(vecs, 4 * beads)
    copies = array(devices // 2, 2, vecs, 2 * beads)
    products = array(4 * vecs, 6 * beads)
    wide, held_wide = array(4 * vecs, total), pltpu.VMEM((4 * vecs, total), F32)
    kept = [array(6 * beads, width, dtype=BF16)] * 2 if keep else []
    held = [] if keep else [pltpu.VMEM((6 * beads, width), BF16)] * 2

    arguments = [
        pltpu.with_memory_space_constraint(item, pltpu.HBM) for item in (positions, noise.transpose(1, 0, 2))
    ]
    own, own_copies = call(
        pack_kernel,
        [block, copies],
        [pltpu.VMEM(item.shape, F32) for item in arguments] + [pltpu.SemaphoreType.DMA((2,))],
        in_specs=[pl.BlockSpec(memory_space=pltpu.HBM)] * 2,
    )(*arguments)
    one, two = gather(own_copies)
    partial, sums, one_wide, *one_tensor = call(
        functools.partial(first_stage, size, False), [products, array(4 * vecs, 4 * vecs), wide] + kept, held
    )(own, one)
    first, image, images, two_wide, *two_tensor = call(
        functools.partial(first_stage, size, True), [block, block, copies, wide] + kept, held
    )(own, two, partial, sums)
    one, two = gather(images)
    partial, vectors, known, small, both = call(
        functools.partial(third_stage, size, not keep),
        [products, block, block, array(vecs, vecs), array(2, vecs, vecs)],
        held + [held_wide],
    )(own, one_wide, *one_tensor, one, first, image)
    shifted, partials = call(
        functools.partial(fourth_stage, not keep), [block, array(devices, 1, vecs * vecs)], held + [held_wide]
    )(own, two_wide, *two_tensor, two, partial, vectors, known, small)
    partials = to_all(partials)
    basis, residual, coefficients = call(
        functools.partial(last_kernel, size),
        [array(3, vecs, beads), array(3, vecs, beads), array(3, vecs, vecs)],
    )(vectors, shifted, both, partials)
    return (basis.transpose(1, 0, 2), residual.transpose(1, 0, 2), coefficients)


def solution(mesh):
    return jax.shard_map(
        local,
        mesh=mesh,
        in_specs=(P(None, ("row", "col")), P(None, None, ("row", "col"))),
        out_specs=(P(None, None, ("row", "col")), P(None, None, ("row", "col")), P()),
        check_vma=False,
    )
```

```python
import functools

import jax
import jax.numpy as jnp
from jax import lax
from jax.experimental import pallas as pl
from jax.experimental.pallas import tpu as pltpu
from jax.sharding import PartitionSpec as P

CHUNK = 1024
KEPT = 8 * 1024 * 1024
F32 = jnp.float32
BF16 = jnp.bfloat16


def copy_halves(block, copies, extra=None):
    beads = block.shape[1] // 4
    middle = beads // 2
    for core in range(2):
        parts = [block[:, part * beads + core * middle : part * beads + (core + 1) * middle] for part in range(4)]
        half = jnp.concatenate(parts, axis=1)
        if extra is not None:
            half = half + extra
        copies[:, core] = jnp.broadcast_to(half[None], (copies.shape[0],) + half.shape)


def pack_kernel(positions, noise, block, copies, held_positions, held_noise, sems):
    reads = [
        pltpu.make_async_copy(positions, held_positions, sems.at[0]),
        pltpu.make_async_copy(noise, held_noise, sems.at[1]),
    ]
    for read in reads:
        read.start()
    beads = block.shape[1] // 4
    block[...] = jnp.zeros(block.shape, F32)
    for read in reads:
        read.wait()
    for part in range(3):
        block[:, part * beads : (part + 1) * beads] = held_noise[part]
    block[:3, 3 * beads :] = held_positions[...]
    copy_halves(block[...], copies)


def split_two(value):
    high = value.astype(BF16)
    return high, (value - high.astype(F32)).astype(BF16)


def matmul_nt(left, right, precision=None):
    return lax.dot_general(
        left, right, (((1,), (1,)), ((), ())), precision=precision, preferred_element_type=F32
    )


def small_matmul(left, right):
    total = left[:, 0:1] * right[0:1, :]
    for k in range(1, left.shape[1]):
        total = total + left[:, k : k + 1] * right[k : k + 1, :]
    return total


def unpack(blocks, wide):
    count, vecs, lanes = blocks.shape
    width = lanes // 4
    for at in range(0, count, 4):
        four = [blocks[at + index] for index in range(4)]
        for part in range(4):
            wide[part * vecs : (part + 1) * vecs, pl.ds(at * width, 4 * width)] = jnp.concatenate(
                [block[:, part * width : (part + 1) * width] for block in four], axis=1
            )


def target_columns(own):
    beads = own.shape[1] // 4
    targets = own[:, 3 * beads :].T
    return [jnp.broadcast_to(targets[:, axis : axis + 1], (beads, 128)) for axis in range(3)]


def tensor(columns, wide, start):
    moved = [columns[axis] - wide[24 + axis : 25 + axis, pl.ds(start, 128)] for axis in range(3)]
    square = moved[0] * moved[0] + moved[1] * moved[1] + moved[2] * moved[2]
    square = jnp.maximum(square, 1e-12)
    inverse = lax.rsqrt(square)
    inverse_sq = inverse * inverse
    near = square < 4.0
    iso = inverse * jnp.where(near, square * (inverse - 9.0 / 32.0), 0.75 + 0.5 * inverse_sq)
    along = inverse * jnp.where(near, 3.0 / 32.0, inverse_sq * (0.75 - 1.5 * inverse_sq))
    scaled = [along * item for item in moved]
    parts = [
        iso + scaled[0] * moved[0],
        scaled[0] * moved[1],
        scaled[0] * moved[2],
        iso + scaled[1] * moved[1],
        scaled[1] * moved[2],
        iso + scaled[2] * moved[2],
    ]
    highs, lows = zip(*[split_two(value) for value in parts])
    return jnp.concatenate(highs, axis=0), jnp.concatenate(lows, axis=0)


def apply_tensor(both, high, low):
    half = both.shape[0] // 2
    first = matmul_nt(both, high)
    return first[:half] + first[half:] + matmul_nt(both[:half], low)


def split_rows(*values):
    highs, lows = zip(*[split_two(value) for value in values])
    return jnp.concatenate(highs + lows, axis=0)


def inner(left, right):
    return [jnp.sum(left * right[row : row + 1], axis=1, keepdims=True) for row in range(right.shape[0])]


def assemble(products):
    beads = products.shape[1] // 6

    def part(row, component):
        return products[8 * row : 8 * row + 8, component * beads : (component + 1) * beads]

    x = part(0, 0) + part(1, 1) + part(2, 2)
    y = part(0, 1) + part(1, 3) + part(2, 4)
    z = part(0, 2) + part(1, 4) + part(2, 5)
    return jnp.concatenate([x, y, z, jnp.zeros(x.shape, F32)], axis=1)


def filled_product(columns, source, wide, start, high, low):
    width = high.shape[1]
    steps = [(at, min(512, width - at)) for at in range(0, width, 512)]
    vectors = [split_rows(wide[:, pl.ds(pl.multiple_of(start + at, 128), step)]) for at, step in steps]
    sums = row_sums(vectors)
    products = jnp.zeros((32, high.shape[0]), F32)
    for (at, step), both in zip(steps, vectors):
        lanes = pl.ds(at, step)
        pieces = [
            tensor(columns, source, pl.multiple_of(start + part, 128)) for part in range(at, at + step, 128)
        ]
        upper, lower = [jnp.concatenate(piece, axis=1) for piece in zip(*pieces)]
        high[:, lanes] = upper
        low[:, lanes] = lower
        products = products + apply_tensor(both, upper, lower)
    return products, sums


def all_filled(own, source, wide, high, low):
    columns = target_columns(own)
    width = high.shape[1]
    chunk = lambda start: filled_product(columns, source, wide, start, high, low)
    if wide.shape[1] == width:
        return chunk(0)
    body = lambda index, totals: tuple(a + b for a, b in zip(totals, chunk(index * width)))
    return lax.fori_loop(1, wide.shape[1] // width, body, chunk(0))


def without_positions(block):
    lanes = lax.broadcasted_iota(jnp.int32, block.shape, 1)
    return jnp.where(lanes < block.shape[1] // 4 * 3, block, 0.0)


def row_sums(vectors):
    total = 0.0
    for both in vectors:
        half = both.shape[0] // 2
        first, second = matmul_nt(both, both[:half]), matmul_nt(both, both[half:])
        total = total + ((first[:half] + first[half:]) + (second[:half] + second[half:]))
    return total


def first_stage(size, last, own, blocks, *refs):
    refs = list(refs)
    if last:
        before, before_sums, first_out, image, copies, wide, high, low = refs
    else:
        out, sums_out, wide, high, low = refs
    unpack(blocks, wide)
    products, sums = all_filled(own[...], wide, wide, high, low)
    if not last:
        out[...], sums_out[...] = products, sums
        return
    sums = (sums + before_sums[...]) / size
    _, inverse = cholesky(sums[:8, :8] + sums[8:16, 8:16] + sums[16:24, 16:24])
    first = small_matmul(inverse, without_positions(own[...]))
    block = small_matmul(inverse, assemble(products + before[...]))
    first_out[...] = first
    image[...] = block
    columns = inner(first, block) + inner(block, block)
    lanes = lax.broadcasted_iota(jnp.int32, (block.shape[0], block.shape[1] // 2), 1)
    shares = jnp.zeros(lanes.shape, F32)
    for index, column in enumerate(columns):
        shares = jnp.where(lanes == block.shape[1] // 8 * 3 + index, column, shares)
    copy_halves(block, copies, shares)


def cholesky(matrix):
    size = matrix.shape[0]
    shape = (size, size)
    rows = lax.broadcasted_iota(jnp.int32, shape, 0)
    cols = lax.broadcasted_iota(jnp.int32, shape, 1)
    entry = {}
    for j in range(size):
        column = jnp.broadcast_to(matrix[:, j : j + 1], shape)
        for i in range(j, size):
            entry[i, j] = jnp.broadcast_to(column[i : i + 1, :], shape)
    factor_t = jnp.zeros(shape, F32)
    inverse = jnp.zeros(shape, F32)
    inverse_rows = []
    for j in range(size):
        scale = lax.rsqrt(entry[j, j])
        lower_row = entry[j, j] * scale
        entry[j, j] = scale
        for i in range(j + 1, size):
            entry[i, j] = entry[i, j] * scale
        for i in range(j + 1, size):
            for k in range(j + 1, i + 1):
                entry[i, k] = entry[i, k] - entry[i, j] * entry[k, j]
        lower_row = jnp.where(cols == j, lower_row, 0.0)
        for i in range(j + 1, size):
            lower_row = jnp.where(cols == i, entry[i, j], lower_row)
        factor_t = jnp.where(rows == j, lower_row, factor_t)
        row = jnp.where(cols == j, 1.0, 0.0)
        for k in range(j):
            row = row - entry[j, k] * inverse_rows[k]
        row = row * scale
        inverse_rows.append(row)
        inverse = jnp.where(rows == j, row, inverse)
    return factor_t, inverse


def second_product(fill, own, wide, wide_image, high, low):
    if fill:
        return all_filled(own, wide, wide_image, high, low)[0]
    return apply_tensor(split_rows(wide_image[...]), high[...], low[...])


def third_stage(size, fill, own, wide, *refs):
    refs = list(refs)
    if not fill:
        (high, low), refs = refs[:2], refs[2:]
    images, own_first, own_image, products, vectors, known, small, coefficients = refs[:8]
    if fill:
        high, low = refs[8:10]
    wide_image = refs[-1]
    unpack(images, wide_image)
    products[...] = second_product(fill, own[...], wide, wide_image, high, low)
    sums = wide_image[24:, :128]
    for at in range(128, wide_image.shape[1], 128):
        sums = sums + wide_image[24:, at : at + 128]
    width = own.shape[1] // 8
    sums = sum(sums[:, at : at + width] for at in range(width, 128, width)) + sums[:, :width]
    sums = sums / size
    alpha = sums[:, :8]
    alpha_t = alpha.T
    factor_t, inverse = cholesky(sums[:, 8:16] - small_matmul(alpha_t, alpha))
    first, image = own_first[...], own_image[...]
    vectors[...] = small_matmul(inverse, image - small_matmul(alpha_t, first))
    known[...] = small_matmul(inverse, small_matmul(alpha_t, image)) + small_matmul(factor_t, first)
    small[...] = inverse
    coefficients[0] = alpha
    coefficients[1] = factor_t.T


def fourth_stage(fill, own, wide, *refs):
    refs = list(refs)
    if not fill:
        (high, low), refs = refs[:2], refs[2:]
    images, before, vectors_in, known, small, shifted, partials = refs[:7]
    if fill:
        high, low = refs[7:9]
    wide_image = refs[-1]
    unpack(images, wide_image)
    products = second_product(fill, own[...], wide, wide_image, high, low) + before[...]
    vectors = vectors_in[...]
    shift = small_matmul(small[...], assemble(products)) - known[...]
    shifted[...] = shift
    lanes = lax.broadcasted_iota(jnp.int32, (8, partials.shape[2]), 1)
    rows = lax.broadcasted_iota(jnp.int32, lanes.shape, 0)
    line = jnp.zeros(lanes.shape, F32)
    for row, column in enumerate(inner(shift, vectors)):
        line = jnp.where(lanes == 8 * row + rows, column, line)
    line = jnp.sum(line, axis=0, keepdims=True)
    partials[...] = jnp.broadcast_to(line[None], partials.shape)


def last_kernel(size, vectors, shifted, both, partials, basis, residual, coefficients):
    beads = basis.shape[2]
    width = partials.shape[2]
    total = jnp.sum(partials[...], axis=0) / size
    spread = jnp.broadcast_to(total, (8, width))
    rows = lax.broadcasted_iota(jnp.int32, spread.shape, 0)
    cols = lax.broadcasted_iota(jnp.int32, spread.shape, 1)
    block = vectors[...]
    left = shifted[...]
    transposed = jnp.where(cols % 8 == rows, spread, 0.0)
    for k in range(8):
        column = jnp.sum(jnp.where(cols // 8 == k, transposed, 0.0), axis=1, keepdims=True)
        left = left - column * block[k : k + 1, :]
    coefficients[0:2] = both[...]
    for k in range(8):
        coefficients[2, k : k + 1, :] = total[:, 8 * k : 8 * k + 8]
    for part in range(3):
        basis[part] = block[:, part * beads : (part + 1) * beads]
        residual[part] = left[:, part * beads : (part + 1) * beads]


def array(*shape, dtype=F32):
    return jax.ShapeDtypeStruct(shape, dtype)


def call(kernel, outs, scratch=(), **options):
    return pl.pallas_call(
        kernel,
        out_shape=outs,
        scratch_shapes=list(scratch),
        compiler_params=pltpu.CompilerParams(vmem_limit_bytes=48 * 1024 * 1024),
        **options,
    )


def to_all(copies):
    return lax.all_to_all(copies, ("row", "col"), 0, 0, tiled=True)


def gather(copies):
    mine = to_all(copies.reshape((-1,) + copies.shape[2:]))
    cols = lax.axis_size("col")
    return mine, lax.ppermute(mine, "col", [(col, col ^ 1) for col in range(cols)])


def local(positions, noise):
    vecs, _, beads = noise.shape
    devices = lax.axis_size("row") * lax.axis_size("col")
    total = beads * devices // 2
    size = 3.0 * beads * devices
    keep = 2 * 2 * 2 * 6 * beads * total <= KEPT
    width = total if keep else min(total, CHUNK)
    block = array(vecs, 4 * beads)
    copies = array(devices // 2, 2, vecs, 2 * beads)
    products = array(4 * vecs, 6 * beads)
    wide, held_wide = array(4 * vecs, total), pltpu.VMEM((4 * vecs, total), F32)
    kept = [array(6 * beads, width, dtype=BF16)] * 2 if keep else []
    held = [] if keep else [pltpu.VMEM((6 * beads, width), BF16)] * 2

    arguments = [
        pltpu.with_memory_space_constraint(item, pltpu.HBM) for item in (positions, noise.transpose(1, 0, 2))
    ]
    own, own_copies = call(
        pack_kernel,
        [block, copies],
        [pltpu.VMEM(item.shape, F32) for item in arguments] + [pltpu.SemaphoreType.DMA((2,))],
        in_specs=[pl.BlockSpec(memory_space=pltpu.HBM)] * 2,
    )(*arguments)
    one, two = gather(own_copies)
    partial, sums, one_wide, *one_tensor = call(
        functools.partial(first_stage, size, False), [products, array(4 * vecs, 4 * vecs), wide] + kept, held
    )(own, one)
    first, image, images, two_wide, *two_tensor = call(
        functools.partial(first_stage, size, True), [block, block, copies, wide] + kept, held
    )(own, two, partial, sums)
    one, two = gather(images)
    partial, vectors, known, small, both = call(
        functools.partial(third_stage, size, not keep),
        [products, block, block, array(vecs, vecs), array(2, vecs, vecs)],
        held + [held_wide],
    )(own, one_wide, *one_tensor, one, first, image)
    shifted, partials = call(
        functools.partial(fourth_stage, not keep), [block, array(devices, 1, vecs * vecs)], held + [held_wide]
    )(own, two_wide, *two_tensor, two, partial, vectors, known, small)
    partials = to_all(partials)
    basis, residual, coefficients = call(
        functools.partial(last_kernel, size),
        [array(3, vecs, beads), array(3, vecs, beads), array(3, vecs, vecs)],
    )(vectors, shifted, both, partials)
    return (basis.transpose(1, 0, 2), residual.transpose(1, 0, 2), coefficients)


def solution(mesh):
    return jax.shard_map(
        local,
        mesh=mesh,
        in_specs=(P(None, ("row", "col")), P(None, None, ("row", "col"))),
        out_specs=(P(None, None, ("row", "col")), P(None, None, ("row", "col")), P()),
        check_vma=False,
    )
```

```python
import functools

import jax
import jax.numpy as jnp
from jax import lax
from jax.experimental import pallas as pl
from jax.experimental.pallas import tpu as pltpu
from jax.sharding import PartitionSpec as P

CHUNK = 1024
KEPT = 8 * 1024 * 1024
F32 = jnp.float32
BF16 = jnp.bfloat16


def copy_halves(block, copies, extra=None):
    beads = block.shape[1] // 4
    middle = beads // 2
    for core in range(2):
        parts = [block[:, part * beads + core * middle : part * beads + (core + 1) * middle] for part in range(4)]
        half = jnp.concatenate(parts, axis=1)
        if extra is not None:
            half = half + extra
        copies[:, core] = jnp.broadcast_to(half[None], (copies.shape[0],) + half.shape)


def pack_kernel(positions, noise, block, copies, held_positions, held_noise, sems):
    reads = [
        pltpu.make_async_copy(positions, held_positions, sems.at[0]),
        pltpu.make_async_copy(noise, held_noise, sems.at[1]),
    ]
    for read in reads:
        read.start()
    beads = block.shape[1] // 4
    block[...] = jnp.zeros(block.shape, F32)
    for read in reads:
        read.wait()
    for part in range(3):
        block[:, part * beads : (part + 1) * beads] = held_noise[part]
    block[:3, 3 * beads :] = held_positions[...]
    copy_halves(block[...], copies)


def split_two(value):
    high = value.astype(BF16)
    return high, (value - high.astype(F32)).astype(BF16)


def matmul_nt(left, right, precision=None):
    return lax.dot_general(
        left, right, (((1,), (1,)), ((), ())), precision=precision, preferred_element_type=F32
    )


def small_matmul(left, right):
    total = left[:, 0:1] * right[0:1, :]
    for k in range(1, left.shape[1]):
        total = total + left[:, k : k + 1] * right[k : k + 1, :]
    return total


def unpack(blocks, wide, parts=4):
    count, vecs, lanes = blocks.shape
    width = lanes // 4
    for at in range(0, count, 4):
        four = [blocks[at + index] for index in range(4)]
        for part in range(parts):
            wide[part * vecs : (part + 1) * vecs, pl.ds(at * width, 4 * width)] = jnp.concatenate(
                [block[:, part * width : (part + 1) * width] for block in four], axis=1
            )


def target_columns(own):
    beads = own.shape[1] // 4
    targets = own[:, 3 * beads :].T
    return [jnp.broadcast_to(targets[:, axis : axis + 1], (beads, 128)) for axis in range(3)]


def tensor(columns, wide, start):
    moved = [columns[axis] - wide[24 + axis : 25 + axis, pl.ds(start, 128)] for axis in range(3)]
    square = moved[0] * moved[0] + moved[1] * moved[1] + moved[2] * moved[2]
    square = jnp.maximum(square, 1e-12)
    inverse = lax.rsqrt(square)
    inverse_sq = inverse * inverse
    near = square < 4.0
    iso = inverse * jnp.where(near, square * (inverse - 9.0 / 32.0), 0.75 + 0.5 * inverse_sq)
    along = inverse * jnp.where(near, 3.0 / 32.0, inverse_sq * (0.75 - 1.5 * inverse_sq))
    scaled = [along * item for item in moved]
    parts = [
        iso + scaled[0] * moved[0],
        scaled[0] * moved[1],
        scaled[0] * moved[2],
        iso + scaled[1] * moved[1],
        scaled[1] * moved[2],
        iso + scaled[2] * moved[2],
    ]
    highs, lows = zip(*[split_two(value) for value in parts])
    return jnp.concatenate(highs, axis=0), jnp.concatenate(lows, axis=0)


def apply_tensor(both, high, low):
    half = both.shape[0] // 2
    first = matmul_nt(both, high)
    return first[:half] + first[half:] + matmul_nt(both[:half], low)


def split_rows(*values):
    highs, lows = zip(*[split_two(value) for value in values])
    return jnp.concatenate(highs + lows, axis=0)


def inner(left, right):
    return [jnp.sum(left * right[row : row + 1], axis=1, keepdims=True) for row in range(right.shape[0])]


def assemble(products):
    beads = products.shape[1] // 6

    def part(row, component):
        return products[8 * row : 8 * row + 8, component * beads : (component + 1) * beads]

    x = part(0, 0) + part(1, 1) + part(2, 2)
    y = part(0, 1) + part(1, 3) + part(2, 4)
    z = part(0, 2) + part(1, 4) + part(2, 5)
    return jnp.concatenate([x, y, z, jnp.zeros(x.shape, F32)], axis=1)


def filled_product(columns, source, wide, start, high, low):
    width = high.shape[1]
    products = jnp.zeros((32, high.shape[0]), F32)
    for at in range(0, width, 512):
        step = min(512, width - at)
        lanes = pl.ds(at, step)
        both = split_rows(wide[:, pl.ds(pl.multiple_of(start + at, 128), step)])
        pieces = [
            tensor(columns, source, pl.multiple_of(start + part, 128)) for part in range(at, at + step, 128)
        ]
        upper, lower = [jnp.concatenate(piece, axis=1) for piece in zip(*pieces)]
        high[:, lanes] = upper
        low[:, lanes] = lower
        products = products + apply_tensor(both, upper, lower)
    return products


def all_filled(own, source, wide, high, low):
    columns = target_columns(own)
    width = high.shape[1]
    chunk = lambda start: filled_product(columns, source, wide, start, high, low)
    if wide.shape[1] == width:
        return chunk(0)
    body = lambda index, total: total + chunk(index * width)
    return lax.fori_loop(1, wide.shape[1] // width, body, chunk(0))


def without_positions(block):
    lanes = lax.broadcasted_iota(jnp.int32, block.shape, 1)
    return jnp.where(lanes < block.shape[1] // 4 * 3, block, 0.0)


def row_sums(wide):
    total = jnp.zeros((wide.shape[0], wide.shape[0]), F32)
    for at in range(0, wide.shape[1], CHUNK):
        both = split_rows(wide[:, at : min(at + CHUNK, wide.shape[1])])
        half = both.shape[0] // 2
        first, second = matmul_nt(both, both[:half]), matmul_nt(both, both[half:])
        total = total + ((first[:half] + first[half:]) + (second[:half] + second[half:]))
    return total


def first_stage(size, last, own, blocks, *refs):
    refs = list(refs)
    if last:
        before, before_sums, first_out, image, copies, wide, high, low = refs
    else:
        out, sums_out, wide, high, low = refs
    unpack(blocks, wide)
    sums = row_sums(wide)
    products = all_filled(own[...], wide, wide, high, low)
    if not last:
        out[...], sums_out[...] = products, sums
        return
    sums = (sums + before_sums[...]) / size
    _, inverse = cholesky(sums[:8, :8] + sums[8:16, 8:16] + sums[16:24, 16:24])
    first = small_matmul(inverse, without_positions(own[...]))
    block = small_matmul(inverse, assemble(products + before[...]))
    first_out[...] = first
    image[...] = block
    columns = inner(first, block) + inner(block, block)
    lanes = lax.broadcasted_iota(jnp.int32, (block.shape[0], block.shape[1] // 2), 1)
    shares = jnp.zeros(lanes.shape, F32)
    for index, column in enumerate(columns):
        shares = jnp.where(lanes == block.shape[1] // 8 * 3 + index, column, shares)
    copy_halves(block, copies, shares)


def cholesky(matrix):
    size = matrix.shape[0]
    shape = (size, size)
    rows = lax.broadcasted_iota(jnp.int32, shape, 0)
    cols = lax.broadcasted_iota(jnp.int32, shape, 1)
    entry = {}
    for j in range(size):
        column = jnp.broadcast_to(matrix[:, j : j + 1], shape)
        for i in range(j, size):
            entry[i, j] = jnp.broadcast_to(column[i : i + 1, :], shape)
    factor_t = jnp.zeros(shape, F32)
    inverse = jnp.zeros(shape, F32)
    inverse_rows = []
    for j in range(size):
        scale = lax.rsqrt(entry[j, j])
        lower_row = entry[j, j] * scale
        entry[j, j] = scale
        for i in range(j + 1, size):
            entry[i, j] = entry[i, j] * scale
        for i in range(j + 1, size):
            for k in range(j + 1, i + 1):
                entry[i, k] = entry[i, k] - entry[i, j] * entry[k, j]
        lower_row = jnp.where(cols == j, lower_row, 0.0)
        for i in range(j + 1, size):
            lower_row = jnp.where(cols == i, entry[i, j], lower_row)
        factor_t = jnp.where(rows == j, lower_row, factor_t)
        row = jnp.where(cols == j, 1.0, 0.0)
        for k in range(j):
            row = row - entry[j, k] * inverse_rows[k]
        row = row * scale
        inverse_rows.append(row)
        inverse = jnp.where(rows == j, row, inverse)
    return factor_t, inverse


def second_product(fill, own, wide, wide_image, high, low):
    if fill:
        return all_filled(own, wide, wide_image, high, low)
    return apply_tensor(split_rows(wide_image[...]), high[...], low[...])


def third_stage(size, fill, own, wide, *refs):
    refs = list(refs)
    if not fill:
        (high, low), refs = refs[:2], refs[2:]
    images, own_first, own_image, products, vectors, known, small, coefficients = refs[:8]
    if fill:
        high, low = refs[8:10]
    wide_image = refs[-1]
    unpack(images, wide_image)
    products[...] = second_product(fill, own[...], wide, wide_image, high, low)
    sums = wide_image[24:, :128]
    for at in range(128, wide_image.shape[1], 128):
        sums = sums + wide_image[24:, at : at + 128]
    width = own.shape[1] // 8
    sums = sum(sums[:, at : at + width] for at in range(width, 128, width)) + sums[:, :width]
    sums = sums / size
    alpha = sums[:, :8]
    alpha_t = alpha.T
    factor_t, inverse = cholesky(sums[:, 8:16] - small_matmul(alpha_t, alpha))
    first, image = own_first[...], own_image[...]
    vectors[...] = small_matmul(inverse, image - small_matmul(alpha_t, first))
    known[...] = small_matmul(inverse, small_matmul(alpha_t, image)) + small_matmul(factor_t, first)
    small[...] = inverse
    coefficients[0] = alpha
    coefficients[1] = factor_t.T


def fourth_stage(fill, own, wide, *refs):
    refs = list(refs)
    if not fill:
        (high, low), refs = refs[:2], refs[2:]
    images, before, vectors_in, known, small, shifted, partials = refs[:7]
    if fill:
        high, low = refs[7:9]
    wide_image = refs[-1]
    unpack(images, wide_image, 3)
    wide_image[24:] = jnp.zeros((8, wide_image.shape[1]), F32)
    products = second_product(fill, own[...], wide, wide_image, high, low) + before[...]
    vectors = vectors_in[...]
    shift = small_matmul(small[...], assemble(products)) - known[...]
    shifted[...] = shift
    lanes = lax.broadcasted_iota(jnp.int32, (8, partials.shape[2]), 1)
    rows = lax.broadcasted_iota(jnp.int32, lanes.shape, 0)
    line = jnp.zeros(lanes.shape, F32)
    for row, column in enumerate(inner(shift, vectors)):
        line = jnp.where(lanes == 8 * row + rows, column, line)
    line = jnp.sum(line, axis=0, keepdims=True)
    partials[...] = jnp.broadcast_to(line[None], partials.shape)


def last_kernel(size, vectors, shifted, both, partials, basis, residual, coefficients):
    beads = basis.shape[2]
    width = partials.shape[2]
    total = jnp.sum(partials[...], axis=0) / size
    spread = jnp.broadcast_to(total, (8, width))
    rows = lax.broadcasted_iota(jnp.int32, spread.shape, 0)
    cols = lax.broadcasted_iota(jnp.int32, spread.shape, 1)
    block = vectors[...]
    left = shifted[...]
    transposed = jnp.where(cols % 8 == rows, spread, 0.0)
    for k in range(8):
        column = jnp.sum(jnp.where(cols // 8 == k, transposed, 0.0), axis=1, keepdims=True)
        left = left - column * block[k : k + 1, :]
    coefficients[0:2] = both[...]
    for k in range(8):
        coefficients[2, k : k + 1, :] = total[:, 8 * k : 8 * k + 8]
    for part in range(3):
        basis[part] = block[:, part * beads : (part + 1) * beads]
        residual[part] = left[:, part * beads : (part + 1) * beads]


def array(*shape, dtype=F32):
    return jax.ShapeDtypeStruct(shape, dtype)


def call(kernel, outs, scratch=(), **options):
    return pl.pallas_call(
        kernel,
        out_shape=outs,
        scratch_shapes=list(scratch),
        compiler_params=pltpu.CompilerParams(vmem_limit_bytes=48 * 1024 * 1024),
        **options,
    )


def to_all(copies):
    return lax.all_to_all(copies, ("row", "col"), 0, 0, tiled=True)


def gather(copies):
    mine = to_all(copies.reshape((-1,) + copies.shape[2:]))
    cols = lax.axis_size("col")
    return mine, lax.ppermute(mine, "col", [(col, col ^ 1) for col in range(cols)])


def local(positions, noise):
    vecs, _, beads = noise.shape
    devices = lax.axis_size("row") * lax.axis_size("col")
    total = beads * devices // 2
    size = 3.0 * beads * devices
    keep = 2 * 2 * 2 * 6 * beads * total <= KEPT
    width = total if keep else min(total, CHUNK)
    block = array(vecs, 4 * beads)
    copies = array(devices // 2, 2, vecs, 2 * beads)
    products = array(4 * vecs, 6 * beads)
    wide, held_wide = array(4 * vecs, total), pltpu.VMEM((4 * vecs, total), F32)
    kept = [array(6 * beads, width, dtype=BF16)] * 2 if keep else []
    held = [] if keep else [pltpu.VMEM((6 * beads, width), BF16)] * 2

    arguments = [
        pltpu.with_memory_space_constraint(item, pltpu.HBM) for item in (positions, noise.transpose(1, 0, 2))
    ]
    own, own_copies = call(
        pack_kernel,
        [block, copies],
        [pltpu.VMEM(item.shape, F32) for item in arguments] + [pltpu.SemaphoreType.DMA((2,))],
        in_specs=[pl.BlockSpec(memory_space=pltpu.HBM)] * 2,
    )(*arguments)
    one, two = gather(own_copies)
    partial, sums, one_wide, *one_tensor = call(
        functools.partial(first_stage, size, False), [products, array(4 * vecs, 4 * vecs), wide] + kept, held
    )(own, one)
    first, image, images, two_wide, *two_tensor = call(
        functools.partial(first_stage, size, True), [block, block, copies, wide] + kept, held
    )(own, two, partial, sums)
    one, two = gather(images)
    partial, vectors, known, small, both = call(
        functools.partial(third_stage, size, not keep),
        [products, block, block, array(vecs, vecs), array(2, vecs, vecs)],
        held + [held_wide],
    )(own, one_wide, *one_tensor, one, first, image)
    shifted, partials = call(
        functools.partial(fourth_stage, not keep), [block, array(devices, 1, vecs * vecs)], held + [held_wide]
    )(own, two_wide, *two_tensor, two, partial, vectors, known, small)
    partials = to_all(partials)
    basis, residual, coefficients = call(
        functools.partial(last_kernel, size),
        [array(3, vecs, beads), array(3, vecs, beads), array(3, vecs, vecs)],
    )(vectors, shifted, both, partials)
    return (basis.transpose(1, 0, 2), residual.transpose(1, 0, 2), coefficients)


def solution(mesh):
    return jax.shard_map(
        local,
        mesh=mesh,
        in_specs=(P(None, ("row", "col")), P(None, None, ("row", "col"))),
        out_specs=(P(None, None, ("row", "col")), P(None, None, ("row", "col")), P()),
        check_vma=False,
    )
```
